128 devices in a mesh: scene: 4 (over x_lo, core), frame: 32 (over y, z, x_hi).
Axes of the slice: x: 4 (x_hi: 2, x_lo: 2; x = x_hi * 2 + x_lo), y: 4, z: 4, core: 2. Of those that a mesh axis runs over, the one named last changes fastest.
Arguments:
- features: bfloat16 [32768, 1024], P(('scene', 'frame')), parts along dimension 0, may hold values from -1.5 to 1.5
- norm_gain: float32 [1024], replicated, may hold values from 0.1 to 1.9
- w_qkv: bfloat16 [1024, 3072], replicated, may hold values from -1.3125 to 1.3125
- w_out: bfloat16 [1024, 1024], replicated, may hold values from -0.1875 to 0.1875
- counts: int32 [128], P('scene'), parts along dimension 0, may hold values from 1 to 32, as said below
- query_index: int32 [128, 32], P(('scene', 'frame')), parts along dimension 0, may hold values from 0 to 255
- owner: int32 [128], P('scene'), parts along dimension 0, may hold values from 0 to 31
Outputs:
- mixed: bfloat16 [32768, 1024], P(('scene', 'frame')), parts along dimension 0
- correlation: float32 [128, 32, 32, 256], P(('scene', 'frame')), parts along dimension 0
The draws below stay inside these ranges and needn't reach their ends.
There are 4 independent parts, one for each index of `scene`. The reference program is written for one: setup_inputs(seed, part) draws one part's arguments, and reference() takes and returns one part's arrays. A program takes and returns all parts, laid end to end along the dimension named above; an argument that names none is the same for every part. Nothing has to cross between parts.
Inputs may be any that keep to these rules, and one draw needn't show every extreme that they name: `counts`: every frame has at least one query and some frame has exactly 32.
All inputs are finite; a program needn't handle non-finite values.
Results may differ from the reference program's by a relative error of at most 0.017.
The reference program's roundings to bfloat16 on the way (of `normed`, `pw`, `attended` and `rows`) count: a program that leaves them out, or rounds other values in their place, can miss the bound.
Values may be sent and summed in bfloat16 or wider, within the bound.
No kernel may reach another device: no remote copies, remote signals or barrier semaphores. Data moves between devices by JAX's collectives and lax.ppermute only.
A program may use at most 256 MiB of HBM per device.

```python
import math
import jax
import jax.numpy as jnp
import numpy as np
from jax import lax

D = 1024
HEADS = 16
HDIM = 64
TOK_DEV = 256
QMAX = 32
FRAMES = 32
TOKENS = 8192


def draw_counts(key, part):
    first = jax.random.fold_in(key, 11)
    second = jax.random.fold_in(key, 12)
    values = jax.random.randint(first, (FRAMES,), 1, QMAX + 1)
    chosen = jax.random.randint(second, (), 0, FRAMES)
    return jnp.where(jnp.arange(FRAMES) == chosen, QMAX, values).astype(jnp.int32)


def draw_w_qkv(key, part):
    base_key = jax.random.fold_in(key, 21)
    head_key = jax.random.fold_in(key, 22)
    other_key = jax.random.fold_in(key, 23)
    base = jax.random.truncated_normal(base_key, -5.25, 5.25, (D, 3 * D), jnp.float32)
    first_head = jax.random.randint(head_key, (), 0, HEADS)
    second_head = (first_head + 1 + jax.random.randint(other_key, (), 0, HEADS - 1)) % HEADS
    first_factor = 4.5
    second_factor = 6.0
    drawn_factor = 1.6
    head_of = jnp.arange(D) // (D // HEADS)
    factor = jnp.where(head_of == first_head, first_factor, jnp.where(head_of == second_head, second_factor, drawn_factor)).astype(jnp.float32)
    query_cols = base[:, :D] * factor[None, :]
    key_cols = base[:, D:2 * D] * factor[None, :]
    whole = jnp.concatenate([query_cols, key_cols, base[:, 2 * D:]], axis=1) * D ** (-0.5)
    return whole.astype(jnp.bfloat16)


def set_ends(entries, key, low, top_value):
    place = [jax.random.randint(jax.random.fold_in(key, axis), (), 0, length) for axis, length in enumerate(entries.shape)]
    widest = entries.shape.index(max(entries.shape))
    next_to = place[:widest] + [(place[widest] + 1) % entries.shape[widest]] + place[widest + 1:]
    return entries.at[tuple(place)].set(low).at[tuple(next_to)].set(top_value)


def steps_of(stream_key, dims, cuts, low, high):
    factor_of, own = 1.0, jax.random.fold_in(stream_key, 6)
    for dim, blocks in cuts:
        draws = jnp.exp(jax.random.uniform(jax.random.fold_in(own, dim), (blocks,), jnp.float32, low / len(cuts), high / len(cuts)))
        factor_of = factor_of * jnp.repeat(draws, dims[dim] // blocks).reshape([-1 if axis == dim else 1 for axis in range(len(dims))])
    return factor_of


def rank_table(number_of, skew):
    loads = [(1 << 20) // math.isqrt(standing ** skew) + 1 for standing in range(1, number_of + 1)]
    deviation = 1 + sum(loads) // (1 << 30)
    return np.cumsum(np.array([max(1, weight // deviation) for weight in loads]))


def skewed_ids(key, shape, amount, lean):
    table = rank_table(amount, lean)
    pick = jax.random.randint(jax.random.fold_in(key, 1), shape, 0, int(table[amount - 1]))
    rank = jnp.searchsorted(jnp.asarray(table, jnp.int32), pick, side="right")
    return jax.random.permutation(jax.random.fold_in(key, 2), amount)[rank].astype(jnp.int32)


def centred(rng, shape, deviation, bound, pieces=(), dtype=jnp.bfloat16):
    drawn = deviation * jax.random.normal(rng, shape, jnp.float32)
    if pieces:
        drawn = drawn * steps_of(rng, shape, pieces, -0.22, 0.18)
    return jnp.clip(drawn, -bound, bound).astype(dtype)


def setup_inputs(seed: int = 0, part: int = 0) -> dict:
    streams_of = jax.random.split(jax.random.key(seed), 8)
    part_splits = jax.random.split(jax.random.fold_in(streams_of[7], part), 8)
    features = centred(part_splits[0], (TOKENS, D), 0.25, 1.5, ((0, 32),))
    norm_gain = jnp.clip(1.0 + 0.18 * jax.random.normal(streams_of[1], (D,), jnp.float32), 0.1, 1.9)
    w_qkv = draw_w_qkv(jax.random.fold_in(streams_of[7], 71), part)
    w_out = centred(streams_of[3], (D, D), D ** -0.5, 0.1875)
    counts = draw_counts(jax.random.fold_in(jax.random.fold_in(streams_of[7], part), 71), part)
    query_index = set_ends(jax.random.randint(part_splits[5], (FRAMES, QMAX), 0, TOK_DEV), jax.random.fold_in(part_splits[5], 1), 0, TOK_DEV - 1).astype(jnp.int32)
    owner = set_ends(skewed_ids(part_splits[6], (FRAMES,), FRAMES, 2), jax.random.fold_in(part_splits[6], 3), 0, FRAMES - 1).astype(jnp.int32)
    return {"features": features, "norm_gain": norm_gain, "w_qkv": w_qkv, "w_out": w_out, "counts": counts, "query_index": query_index, "owner": owner}


def normalize(x, gain):
    xf = x.astype(jnp.float32)
    mean = lax.optimization_barrier(jnp.mean(xf, axis=-1, keepdims=True))
    var = lax.optimization_barrier(jnp.mean((xf - mean) ** 2, axis=-1, keepdims=True))
    return ((xf - mean) * lax.rsqrt(var + 1e-05) * gain).astype(jnp.bfloat16)

def reference(features, norm_gain, w_qkv, w_out, counts, query_index, owner):
    normed = normalize(features, norm_gain)
    proj = jnp.dot(normed, w_qkv, preferred_element_type=jnp.float32)
    scale = 1.0 / HDIM ** 0.5
    q = (proj[:, :D] * scale).astype(jnp.bfloat16)
    k = proj[:, D:2 * D].astype(jnp.bfloat16).reshape(TOKENS, HEADS, HDIM).astype(jnp.float32)
    v = proj[:, 2 * D:].astype(jnp.bfloat16).reshape(TOKENS, HEADS, HDIM).astype(jnp.float32)
    q_frames = q.reshape(FRAMES, TOK_DEV, HEADS, HDIM)

    def attend(q_block):
        s = jnp.einsum('thd,shd->hts', q_block.astype(jnp.float32), k)
        m = lax.optimization_barrier(jnp.max(s, axis=-1, keepdims=True))
        p = jnp.exp(s - m)
        l = lax.optimization_barrier(jnp.sum(p, axis=-1))
        pw = lax.optimization_barrier(p.astype(jnp.bfloat16)).astype(jnp.float32)
        pv = jnp.einsum('hts,shd->thd', pw, v)
        o = pv / jnp.transpose(l)[:, :, None]
        return o.reshape(TOK_DEV, D).astype(jnp.bfloat16)
    attended = lax.map(attend, q_frames).reshape(TOKENS, D)
    mixed = (features.astype(jnp.float32) + jnp.dot(attended, w_out, preferred_element_type=jnp.float32)).astype(jnp.bfloat16)
    framed = mixed.reshape(FRAMES, TOK_DEV, D)
    rows = framed[jnp.arange(FRAMES)[:, None], query_index]
    valid = jnp.arange(QMAX)[None, :] < counts[:, None]
    rows = jnp.where(valid[:, :, None], rows, jnp.zeros_like(rows))
    corr = jnp.einsum('fqd,gtd->gfqt', rows.astype(jnp.float32), framed.astype(jnp.float32)) / D ** 0.5
    owned = owner[None, :] == jnp.arange(FRAMES)[:, None]
    corr = jnp.where(owned[:, :, None, None], corr, jnp.float32(0.0))
    return (mixed, corr)
```

```python
import functools

import jax
import jax.numpy as jnp
from jax import lax
from jax.experimental import pallas as pl
from jax.experimental.pallas import tpu as pltpu
from jax.sharding import PartitionSpec as P

D = 1024
HEADS = 16
HDIM = 64
TOK = 256
FRAMES = 32
QMAX = 32
LANES = 128
LOG2E = 1.4426950408889634
MARGIN = 64.0
NT = (((1,), (1,)), ((), ()))
F32 = jnp.float32
BF16 = jnp.bfloat16


def low_half(rows):
    return lax.broadcasted_iota(jnp.int32, (rows, LANES), 1) < HDIM


def swap(x):
    return pltpu.roll(x, HDIM, 1)


def project_kernel(x_ref, g_ref, wq_ref, wk_ref, wv_ref, o_ref, n_ref):
    @pl.when(pl.program_id(0) == 0)
    def _():
        xf = x_ref[...].astype(F32)
        mean = jnp.mean(xf, axis=-1, keepdims=True)
        cen = xf - mean
        var = jnp.mean(cen * cen, axis=-1, keepdims=True)
        n_ref[...] = (cen * lax.rsqrt(var + 1e-05) * g_ref[...]).astype(BF16)

    n = n_ref[...]
    q = jnp.dot(n, wq_ref[...], preferred_element_type=F32) * (1.0 / HDIM**0.5)
    k = jnp.dot(n, wk_ref[...], preferred_element_type=F32)
    v = jnp.dot(n, wv_ref[...], preferred_element_type=F32)
    half = TOK // 2
    low = low_half(TOK)
    lowh = low_half(half)
    for c in range(wq_ref.shape[1] // LANES):
        cols = slice(c * LANES, (c + 1) * LANES)
        kp, vp = k[:, cols], v[:, cols]
        qa, qb = q[:half, cols], q[half:, cols]
        o_ref[2 * c, :TOK] = jnp.where(low, kp, swap(vp)).astype(BF16)
        o_ref[2 * c + 1, :TOK] = jnp.where(low, swap(kp), vp).astype(BF16)
        o_ref[2 * c, TOK:] = jnp.where(lowh, qa, swap(qb)).astype(BF16)
        o_ref[2 * c + 1, TOK:] = jnp.where(lowh, swap(qa), qb).astype(BF16)


def project(x, gain, w_qkv):
    steps = 4
    width = D // steps
    return pl.pallas_call(
        project_kernel,
        grid=(steps,),
        in_specs=[
            pl.BlockSpec((TOK, D), lambda i: (0, 0)),
            pl.BlockSpec((1, D), lambda i: (0, 0)),
            pl.BlockSpec((D, width), lambda i: (0, i)),
            pl.BlockSpec((D, width), lambda i: (0, i + steps)),
            pl.BlockSpec((D, width), lambda i: (0, i + 2 * steps)),
        ],
        out_specs=pl.BlockSpec((HEADS // steps, TOK + TOK // 2, LANES), lambda i: (i, 0, 0)),
        out_shape=jax.ShapeDtypeStruct((HEADS, TOK + TOK // 2, LANES), BF16),
        scratch_shapes=[pltpu.VMEM((TOK, D), BF16)],
        compiler_params=pltpu.CompilerParams(vmem_limit_bytes=32 << 20),
        name="project",
    )(x, gain.reshape(1, D), w_qkv, w_qkv, w_qkv)


TILE_FRAMES = 4
BLOCK_FRAMES = 4
GROUP = FRAMES // 2


def load_queries(q_ref):
    packed = q_ref[...].reshape(TILE_FRAMES * TOK // 2, LANES).astype(F32)
    low = low_half(packed.shape[0])
    zero = jnp.zeros_like(packed)
    both = [jnp.where(low, packed, zero), jnp.where(low, swap(packed), zero)]
    return jnp.concatenate(both, axis=0).astype(BF16)


def kv_block(kv_ref, j, count):
    return kv_ref[pl.ds(j * count, count), :TOK].reshape(count * TOK, LANES)


def with_ones(kv):
    low = low_half(kv.shape[0])
    return jnp.where(low, jnp.ones_like(kv), kv)


def fill_values(kv_ref, va_ref):
    @pl.when(pl.program_id(0) == 0)
    def _():
        for j in range(GROUP):
            va_ref[j] = with_ones(kv_ref[j, :TOK])


def partial_sums(q, ref_point, kv_ref, va_ref):
    acc = jnp.zeros((q.shape[0], LANES), F32)
    for j in range(GROUP // BLOCK_FRAMES):
        s = lax.dot_general(q, kv_block(kv_ref, j, BLOCK_FRAMES), NT, preferred_element_type=F32)
        p = jnp.exp2(s * LOG2E - ref_point).astype(BF16)
        acc += jnp.dot(p, kv_block(va_ref, j, BLOCK_FRAMES), preferred_element_type=F32)
    return acc


def first_kernel(q_ref, kv_ref, acc_ref, va_ref):
    fill_values(kv_ref, va_ref)
    q = load_queries(q_ref)
    s = lax.dot_general(q, kv_block(kv_ref, 0, 2), NT, preferred_element_type=F32)
    ref_point = jnp.max(s, axis=-1, keepdims=True) * LOG2E + MARGIN
    acc = partial_sums(q, ref_point, kv_ref, va_ref)
    lane = lax.broadcasted_iota(jnp.int32, acc.shape, 1)
    acc_ref[...] = jnp.where(lane == 1, ref_point, acc)


def second_kernel(q_ref, kv_ref, kv2_ref, first_ref, o_ref, va_ref):
    fill_values(kv2_ref, va_ref)
    q = load_queries(q_ref)
    rows = q.shape[0]

    def store(total):
        out = total / total[:, :1]
        packed = jnp.where(low_half(rows // 2), swap(out[: rows // 2]), out[rows // 2 :])
        o_ref[...] = packed.astype(BF16).reshape(o_ref.shape)

    ref_point = first_ref[:, 1:2]
    total = first_ref[...] + partial_sums(q, ref_point, kv2_ref, va_ref)
    sums = total[:, :1]
    store(total)
    safe = jnp.min(jnp.where((sums < 2.0**100) & (sums > 2.0**-100), 1.0, 0.0)) > 0.5

    @pl.when(jnp.logical_not(safe))
    def _():
        def absorb(ref):
            def step(j, carry):
                top, acc = carry
                kv = ref[j, :TOK]
                s = lax.dot_general(q, kv, NT, preferred_element_type=F32)
                newtop = jnp.maximum(top, jnp.max(s, axis=-1, keepdims=True))
                p = jnp.exp(s - newtop).astype(BF16)
                acc = acc * jnp.exp(top - newtop)
                acc += jnp.dot(p, with_ones(kv), preferred_element_type=F32)
                return newtop, acc

            return step

        start = (jnp.full((rows, 1), -1e30, F32), jnp.zeros((rows, LANES), F32))
        carry = lax.fori_loop(0, GROUP, absorb(kv_ref), start)
        top, acc = lax.fori_loop(0, GROUP, absorb(kv2_ref), carry)
        store(acc)


def attend(mine, other):
    tiles = GROUP // TILE_FRAMES
    rows = TILE_FRAMES * TOK
    q_spec = pl.BlockSpec((TILE_FRAMES, TOK // 2, LANES), lambda i: (i, 2, 0))
    own_spec = pl.BlockSpec((GROUP, TOK + TOK // 2, LANES), lambda i: (0, 0, 0))
    other_spec = pl.BlockSpec((GROUP, TOK, LANES), lambda i: (0, 0, 0))
    acc_spec = pl.BlockSpec((rows, LANES), lambda i: (i, 0))
    params = pltpu.CompilerParams(vmem_limit_bytes=56 << 20)
    pairs = GROUP * TOK * GROUP * TOK
    cost = pl.CostEstimate(
        flops=4 * pairs * LANES * 2, bytes_accessed=8 << 20, transcendentals=pairs
    )
    scratch = [pltpu.VMEM((GROUP, TOK, LANES), BF16)]
    first = pl.pallas_call(
        first_kernel,
        grid=(tiles,),
        in_specs=[q_spec, own_spec],
        out_specs=acc_spec,
        out_shape=jax.ShapeDtypeStruct((GROUP * TOK, LANES), F32),
        scratch_shapes=scratch,
        compiler_params=params,
        cost_estimate=cost,
        name="attend_first",
    )(mine, mine)
    return pl.pallas_call(
        second_kernel,
        grid=(tiles,),
        in_specs=[q_spec, own_spec, other_spec, acc_spec],
        out_specs=pl.BlockSpec((TILE_FRAMES, TOK // 2, LANES), lambda i: (i, 0, 0)),
        out_shape=jax.ShapeDtypeStruct((GROUP, TOK // 2, LANES), BF16),
        scratch_shapes=scratch,
        compiler_params=params,
        cost_estimate=cost,
        name="attend_second",
    )(mine, mine, other, first)


def mix_kernel(at_ref, x_ref, w_ref, slots_ref, counts_ref, owner_ref, me_ref, mixed_ref, send_ref):
    half = TOK // 2
    low = low_half(half)
    top, bottom = [], []
    for i in range(HEADS // 2):
        even, odd = at_ref[2 * i].astype(F32), at_ref[2 * i + 1].astype(F32)
        top.append(jnp.where(low, even, swap(odd)).astype(BF16))
        bottom.append(jnp.where(low, swap(even), odd).astype(BF16))
    att = jnp.concatenate([jnp.concatenate(top, axis=1), jnp.concatenate(bottom, axis=1)], axis=0)
    mixed = (
        x_ref[...].astype(F32) + jnp.dot(att, w_ref[...], preferred_element_type=F32)
    ).astype(BF16)
    mixed_ref[...] = mixed
    me = me_ref[0]
    count = counts_ref[me]
    token = lax.broadcasted_iota(jnp.int32, (TOK, QMAX), 0)
    slot = lax.broadcasted_iota(jnp.int32, (TOK, QMAX), 1)
    chosen = (token == slots_ref[...]) & (slot < count)
    rows = lax.dot_general(
        jnp.where(chosen, 1.0, 0.0).astype(BF16),
        mixed,
        (((0,), (0,)), ((), ())),
        preferred_element_type=F32,
    ).astype(BF16)
    dest = owner_ref[me]
    send_ref[...] = jnp.zeros_like(send_ref)
    send_ref[dest] = rows


def mix(att, x, w_out, slots, counts, owner, me):
    smem = pl.BlockSpec(memory_space=pltpu.SMEM)
    vmem = pl.BlockSpec(memory_space=pltpu.VMEM)
    return pl.pallas_call(
        mix_kernel,
        in_specs=[vmem, vmem, vmem, vmem, smem, smem, smem],
        out_specs=[vmem, vmem],
        out_shape=[
            jax.ShapeDtypeStruct((TOK, D), BF16),
            jax.ShapeDtypeStruct((FRAMES, QMAX, D), BF16),
        ],
        compiler_params=pltpu.CompilerParams(vmem_limit_bytes=32 << 20),
        name="mix",
    )(att, x, w_out, slots, counts, owner, me)


def correlate_kernel(rows_ref, mixed_ref, o_ref):
    rows = rows_ref[...].reshape(-1, D)
    corr = lax.dot_general(rows, mixed_ref[...], NT, preferred_element_type=F32)
    o_ref[...] = (corr * (1.0 / D**0.5)).reshape(o_ref.shape)


def correlate(arrived, mixed):
    step = 8
    return pl.pallas_call(
        correlate_kernel,
        grid=(FRAMES // step,),
        in_specs=[
            pl.BlockSpec((step, QMAX, D), lambda i: (i, 0, 0)),
            pl.BlockSpec((TOK, D), lambda i: (0, 0)),
        ],
        out_specs=pl.BlockSpec((1, step, QMAX, TOK), lambda i: (0, i, 0, 0)),
        out_shape=jax.ShapeDtypeStruct((1, FRAMES, QMAX, TOK), F32),
        name="correlate",
    )(arrived, mixed)


def per_device(features, norm_gain, w_qkv, w_out, counts, query_index, owner):
    groups = [[2 * i + side for i in range(GROUP)] for side in range(2)]
    packed = project(features, norm_gain, w_qkv)
    mine = lax.all_to_all(packed, "frame", 0, 0, tiled=True, axis_index_groups=groups)
    other = lax.ppermute(mine[:, :TOK], "frame", [(d, d ^ 1) for d in range(FRAMES)])
    out = attend(mine, other)
    att = lax.all_to_all(out, "frame", 0, 0, tiled=True, axis_index_groups=groups)
    me = lax.axis_index("frame").astype(jnp.int32).reshape(1)
    mixed, send = mix(att, features, w_out, query_index, counts, owner, me)
    arrived = lax.all_to_all(send, "frame", 0, 0, tiled=True)
    return mixed, correlate(arrived, mixed)


def solution(mesh):
    rows = P(("scene", "frame"), None)
    in_specs = (rows, P(), P(), P(), P("scene"), rows, P("scene"))
    out_specs = (rows, P(("scene", "frame"), None, None, None))
    return jax.shard_map(
        per_device, mesh=mesh, in_specs=in_specs, out_specs=out_specs, check_vma=False
    )
```

```python
import functools

import jax
import jax.numpy as jnp
from jax import lax
from jax.experimental import pallas as pl
from jax.experimental.pallas import tpu as pltpu
from jax.sharding import PartitionSpec as P

D = 1024
HEADS = 16
HDIM = 64
TOK = 256
FRAMES = 32
QMAX = 32
LANES = 128
LOG2E = 1.4426950408889634
NT = (((1,), (1,)), ((), ()))
F32 = jnp.float32
BF16 = jnp.bfloat16


def low_half(rows):
    return lax.broadcasted_iota(jnp.int32, (rows, LANES), 1) < HDIM


def swap(x):
    return pltpu.roll(x, HDIM, 1)


def project_kernel(x_ref, g_ref, wq_ref, wk_ref, wv_ref, o_ref, n_ref):
    @pl.when(pl.program_id(0) == 0)
    def _():
        xf = x_ref[...].astype(F32)
        mean = jnp.mean(xf, axis=-1, keepdims=True)
        cen = xf - mean
        var = jnp.mean(cen * cen, axis=-1, keepdims=True)
        n_ref[...] = (cen * lax.rsqrt(var + 1e-05) * g_ref[...]).astype(BF16)

    n = n_ref[...]
    q = jnp.dot(n, wq_ref[...], preferred_element_type=F32) * (1.0 / HDIM**0.5)
    k = jnp.dot(n, wk_ref[...], preferred_element_type=F32)
    v = jnp.dot(n, wv_ref[...], preferred_element_type=F32)
    half = TOK // 2
    low = low_half(TOK)
    lowh = low_half(half)
    for c in range(wq_ref.shape[1] // LANES):
        cols = slice(c * LANES, (c + 1) * LANES)
        kp, vp = k[:, cols], v[:, cols]
        qa, qb = q[:half, cols], q[half:, cols]
        o_ref[2 * c, :TOK] = jnp.where(low, kp, swap(vp)).astype(BF16)
        o_ref[2 * c + 1, :TOK] = jnp.where(low, swap(kp), vp).astype(BF16)
        o_ref[2 * c, TOK:] = jnp.where(lowh, qa, swap(qb)).astype(BF16)
        o_ref[2 * c + 1, TOK:] = jnp.where(lowh, swap(qa), qb).astype(BF16)


def project(x, gain, w_qkv):
    steps = 4
    width = D // steps
    return pl.pallas_call(
        project_kernel,
        grid=(steps,),
        in_specs=[
            pl.BlockSpec((TOK, D), lambda i: (0, 0)),
            pl.BlockSpec((1, D), lambda i: (0, 0)),
            pl.BlockSpec((D, width), lambda i: (0, i)),
            pl.BlockSpec((D, width), lambda i: (0, i + steps)),
            pl.BlockSpec((D, width), lambda i: (0, i + 2 * steps)),
        ],
        out_specs=pl.BlockSpec((HEADS // steps, TOK + TOK // 2, LANES), lambda i: (i, 0, 0)),
        out_shape=jax.ShapeDtypeStruct((HEADS, TOK + TOK // 2, LANES), BF16),
        scratch_shapes=[pltpu.VMEM((TOK, D), BF16)],
        compiler_params=pltpu.CompilerParams(vmem_limit_bytes=60 << 20),
        name="project",
    )(x, gain.reshape(1, D), w_qkv, w_qkv, w_qkv)


TILE_FRAMES = 4
BLOCK_FRAMES = 4
GROUP = FRAMES // 2


def load_queries(q_ref):
    packed = q_ref[...].reshape(TILE_FRAMES * TOK // 2, LANES).astype(F32)
    low = low_half(packed.shape[0])
    zero = jnp.zeros_like(packed)
    both = [jnp.where(low, packed, zero), jnp.where(low, swap(packed), zero)]
    return jnp.concatenate(both, axis=0).astype(BF16)


def kv_block(kv_ref, j, count):
    return kv_ref[pl.ds(j * count, count), :TOK].reshape(count * TOK, LANES)


def with_ones(kv):
    low = low_half(kv.shape[0])
    return jnp.where(low, jnp.ones_like(kv), kv)


def fill_values(kv_ref, va_ref):
    @pl.when(pl.program_id(0) == 0)
    def _():
        for j in range(GROUP):
            va_ref[j] = with_ones(kv_ref[j, :TOK])


def absorb(q, kv_ref, va_ref, top, acc):
    def scores(j):
        block = kv_block(kv_ref, j, BLOCK_FRAMES)
        return lax.dot_general(q, block, NT, preferred_element_type=F32)

    blocks = GROUP // BLOCK_FRAMES
    s = scores(0)
    for j in range(blocks):
        ahead = scores(j + 1) if j + 1 < blocks else None
        newtop = jnp.max(s, axis=-1, keepdims=True) * LOG2E
        if top is not None:
            newtop = jnp.maximum(top, newtop)
        p = jnp.exp2(s * LOG2E - newtop).astype(BF16)
        pv = jnp.dot(p, kv_block(va_ref, j, BLOCK_FRAMES), preferred_element_type=F32)
        acc = pv if top is None else acc * jnp.exp2(top - newtop) + pv
        top, s = newtop, ahead
    return top, acc


def first_kernel(q_ref, kv_ref, acc_ref, va_ref):
    fill_values(kv_ref, va_ref)
    top, acc = absorb(load_queries(q_ref), kv_ref, va_ref, None, None)
    lane = lax.broadcasted_iota(jnp.int32, acc.shape, 1)
    acc_ref[...] = jnp.where(lane == 1, top, acc)


def second_kernel(q_ref, kv_ref, first_ref, o_ref, va_ref):
    fill_values(kv_ref, va_ref)
    q = load_queries(q_ref)
    rows = q.shape[0]
    first = first_ref[...]
    top, acc = absorb(q, kv_ref, va_ref, first[:, 1:2], first)
    out = acc / acc[:, :1]
    packed = jnp.where(low_half(rows // 2), swap(out[: rows // 2]), out[rows // 2 :])
    o_ref[...] = packed.astype(BF16).reshape(o_ref.shape)


def attend(mine, other):
    tiles = GROUP // TILE_FRAMES
    rows = TILE_FRAMES * TOK
    q_spec = pl.BlockSpec((TILE_FRAMES, TOK // 2, LANES), lambda i: (i, 2, 0))
    own_spec = pl.BlockSpec((GROUP, TOK + TOK // 2, LANES), lambda i: (0, 0, 0))
    other_spec = pl.BlockSpec((GROUP, TOK, LANES), lambda i: (0, 0, 0))
    acc_spec = pl.BlockSpec((rows, LANES), lambda i: (i, 0))
    params = pltpu.CompilerParams(vmem_limit_bytes=56 << 20)
    pairs = GROUP * TOK * GROUP * TOK
    cost = pl.CostEstimate(
        flops=4 * pairs * LANES * 2, bytes_accessed=8 << 20, transcendentals=pairs
    )
    scratch = [pltpu.VMEM((GROUP, TOK, LANES), BF16)]
    first = pl.pallas_call(
        first_kernel,
        grid=(tiles,),
        in_specs=[q_spec, own_spec],
        out_specs=acc_spec,
        out_shape=jax.ShapeDtypeStruct((GROUP * TOK, LANES), F32),
        scratch_shapes=scratch,
        compiler_params=params,
        cost_estimate=cost,
        name="attend_first",
    )(mine, mine)
    return pl.pallas_call(
        second_kernel,
        grid=(tiles,),
        in_specs=[q_spec, other_spec, acc_spec],
        out_specs=pl.BlockSpec((TILE_FRAMES, TOK // 2, LANES), lambda i: (i, 0, 0)),
        out_shape=jax.ShapeDtypeStruct((GROUP, TOK // 2, LANES), BF16),
        scratch_shapes=scratch,
        compiler_params=params,
        cost_estimate=cost,
        name="attend_second",
    )(mine, other, first)


def mix_kernel(at_ref, x_ref, w_ref, slots_ref, counts_ref, owner_ref, me_ref, mixed_ref, send_ref):
    half = TOK // 2
    low = low_half(half)
    top, bottom = [], []
    for i in range(HEADS // 2):
        even, odd = at_ref[2 * i].astype(F32), at_ref[2 * i + 1].astype(F32)
        top.append(jnp.where(low, even, swap(odd)).astype(BF16))
        bottom.append(jnp.where(low, swap(even), odd).astype(BF16))
    att = jnp.concatenate([jnp.concatenate(top, axis=1), jnp.concatenate(bottom, axis=1)], axis=0)
    mixed = (
        x_ref[...].astype(F32) + jnp.dot(att, w_ref[...], preferred_element_type=F32)
    ).astype(BF16)
    mixed_ref[...] = mixed
    me = me_ref[0]
    count = counts_ref[me]
    token = lax.broadcasted_iota(jnp.int32, (TOK, QMAX), 0)
    slot = lax.broadcasted_iota(jnp.int32, (TOK, QMAX), 1)
    chosen = (token == slots_ref[...]) & (slot < count)
    rows = lax.dot_general(
        jnp.where(chosen, 1.0, 0.0).astype(BF16),
        mixed,
        (((0,), (0,)), ((), ())),
        preferred_element_type=F32,
    ).astype(BF16)
    dest = owner_ref[me]
    send_ref[...] = jnp.zeros_like(send_ref)
    send_ref[dest] = rows


def mix(att, x, w_out, slots, counts, owner, me):
    smem = pl.BlockSpec(memory_space=pltpu.SMEM)
    vmem = pl.BlockSpec(memory_space=pltpu.VMEM)
    return pl.pallas_call(
        mix_kernel,
        in_specs=[vmem, vmem, vmem, vmem, smem, smem, smem],
        out_specs=[vmem, vmem],
        out_shape=[
            jax.ShapeDtypeStruct((TOK, D), BF16),
            jax.ShapeDtypeStruct((FRAMES, QMAX, D), BF16),
        ],
        compiler_params=pltpu.CompilerParams(vmem_limit_bytes=32 << 20),
        name="mix",
    )(att, x, w_out, slots, counts, owner, me)


def correlate_kernel(rows_ref, mixed_ref, o_ref):
    rows = rows_ref[...].reshape(-1, D)
    corr = lax.dot_general(rows, mixed_ref[...], NT, preferred_element_type=F32)
    o_ref[...] = (corr * (1.0 / D**0.5)).reshape(o_ref.shape)


def correlate(arrived, mixed):
    step = 8
    return pl.pallas_call(
        correlate_kernel,
        grid=(FRAMES // step,),
        in_specs=[
            pl.BlockSpec((step, QMAX, D), lambda i: (i, 0, 0)),
            pl.BlockSpec((TOK, D), lambda i: (0, 0)),
        ],
        out_specs=pl.BlockSpec((1, step, QMAX, TOK), lambda i: (0, i, 0, 0)),
        out_shape=jax.ShapeDtypeStruct((1, FRAMES, QMAX, TOK), F32),
        name="correlate",
    )(arrived, mixed)


def per_device(features, norm_gain, w_qkv, w_out, counts, query_index, owner):
    groups = [[2 * i + side for i in range(GROUP)] for side in range(2)]
    packed = project(features, norm_gain, w_qkv)
    mine = lax.all_to_all(packed, "frame", 0, 0, tiled=True, axis_index_groups=groups)
    other = lax.ppermute(mine[:, :TOK], "frame", [(d, d ^ 1) for d in range(FRAMES)])
    out = attend(mine, other)
    att = lax.all_to_all(out, "frame", 0, 0, tiled=True, axis_index_groups=groups)
    me = lax.axis_index("frame").astype(jnp.int32).reshape(1)
    mixed, send = mix(att, features, w_out, query_index, counts, owner, me)
    arrived = lax.all_to_all(send, "frame", 0, 0, tiled=True)
    return mixed, correlate(arrived, mixed)


def solution(mesh):
    rows = P(("scene", "frame"), None)
    in_specs = (rows, P(), P(), P(), P("scene"), rows, P("scene"))
    out_specs = (rows, P(("scene", "frame"), None, None, None))
    return jax.shard_map(
        per_device, mesh=mesh, in_specs=in_specs, out_specs=out_specs, check_vma=False
    )
```

```python
import functools

import jax
import jax.numpy as jnp
from jax import lax
from jax.experimental import pallas as pl
from jax.experimental.pallas import tpu as pltpu
from jax.sharding import PartitionSpec as P

D = 1024
HEADS = 16
HDIM = 64
TOK = 256
FRAMES = 32
QMAX = 32
LANES = 128
LOG2E = 1.4426950408889634
NT = (((1,), (1,)), ((), ()))
TN = (((0,), (0,)), ((), ()))
CHUNK = 16
F32 = jnp.float32
BF16 = jnp.bfloat16


def low_half(rows):
    return lax.broadcasted_iota(jnp.int32, (rows, LANES), 1) < HDIM


def swap(x):
    return pltpu.roll(x, HDIM, 1)


def slot_of_token(slots):
    return lax.broadcasted_iota(jnp.int32, (TOK, QMAX), 0) == slots


def arrange(slots):
    picked = jnp.max(jnp.where(slot_of_token(slots), 1.0, 0.0), axis=1, keepdims=True)
    row = lax.broadcasted_iota(jnp.int32, (TOK, TOK), 0)
    col = lax.broadcasted_iota(jnp.int32, (TOK, TOK), 1)
    wide = jnp.broadcast_to(picked, (TOK, LANES)).astype(BF16)
    before = jnp.dot(jnp.where(col < row, 1.0, 0.0).astype(BF16), wide, preferred_element_type=F32)
    before = before[:, :1].astype(jnp.int32)
    total = jnp.sum(picked).astype(jnp.int32)
    token = lax.broadcasted_iota(jnp.int32, (TOK, 1), 0)
    rank = jnp.where(picked > 0.5, before, total + token - before)
    within = rank & 31
    place = (rank >> 5) * CHUNK + (within & 15) + jnp.where(within >= CHUNK, TOK // 2, 0)
    return jnp.where(place == col, 1.0, 0.0).astype(BF16)


def project_kernel(x_ref, g_ref, slots_ref, wq_ref, wk_ref, wv_ref, o_ref, place_ref, n_ref):
    @pl.when(pl.program_id(0) == 0)
    def _():
        place = arrange(slots_ref[...])
        place_ref[...] = place
        xf = x_ref[...].astype(F32)
        mean = jnp.mean(xf, axis=-1, keepdims=True)
        cen = xf - mean
        var = jnp.mean(cen * cen, axis=-1, keepdims=True)
        normed = (cen * lax.rsqrt(var + 1e-05) * g_ref[...]).astype(BF16)
        n_ref[...] = lax.dot_general(place, normed, TN, preferred_element_type=F32).astype(BF16)

    n = n_ref[...]
    q = jnp.dot(n, wq_ref[...], preferred_element_type=F32) * (1.0 / HDIM**0.5)
    k = jnp.dot(n, wk_ref[...], preferred_element_type=F32)
    v = jnp.dot(n, wv_ref[...], preferred_element_type=F32)
    half = TOK // 2
    low = low_half(TOK)
    lowh = low_half(half)
    for c in range(wq_ref.shape[1] // LANES):
        cols = slice(c * LANES, (c + 1) * LANES)
        kp, vp = k[:, cols], v[:, cols]
        qa, qb = q[:half, cols], q[half:, cols]
        o_ref[2 * c, :TOK] = jnp.where(low, kp, swap(vp)).astype(BF16)
        o_ref[2 * c + 1, :TOK] = jnp.where(low, swap(kp), vp).astype(BF16)
        o_ref[2 * c, TOK:] = jnp.where(lowh, qa, swap(qb)).astype(BF16)
        o_ref[2 * c + 1, TOK:] = jnp.where(lowh, swap(qa), qb).astype(BF16)


def project(x, gain, slots, w_qkv):
    steps = 4
    width = D // steps
    return pl.pallas_call(
        project_kernel,
        grid=(steps,),
        in_specs=[
            pl.BlockSpec((TOK, D), lambda i: (0, 0)),
            pl.BlockSpec((1, D), lambda i: (0, 0)),
            pl.BlockSpec((1, QMAX), lambda i: (0, 0)),
            pl.BlockSpec((D, width), lambda i: (0, i)),
            pl.BlockSpec((D, width), lambda i: (0, i + steps)),
            pl.BlockSpec((D, width), lambda i: (0, i + 2 * steps)),
        ],
        out_specs=[
            pl.BlockSpec((HEADS // steps, TOK + TOK // 2, LANES), lambda i: (i, 0, 0)),
            pl.BlockSpec((TOK, TOK), lambda i: (0, 0)),
        ],
        out_shape=[
            jax.ShapeDtypeStruct((HEADS, TOK + TOK // 2, LANES), BF16),
            jax.ShapeDtypeStruct((TOK, TOK), BF16),
        ],
        scratch_shapes=[pltpu.VMEM((TOK, D), BF16)],
        compiler_params=pltpu.CompilerParams(vmem_limit_bytes=60 << 20),
        name="project",
    )(x, gain.reshape(1, D), slots, w_qkv, w_qkv, w_qkv)


BLOCK_FRAMES = 4
GROUP = FRAMES // 2
CHUNKS = TOK // (2 * CHUNK)
ROWS = GROUP * 2 * CHUNK
SPLIT = 6


def unpack_queries(packed):
    packed = packed.reshape(GROUP * CHUNK, LANES).astype(F32)
    low = low_half(packed.shape[0])
    zero = jnp.zeros_like(packed)
    both = [jnp.where(low, packed, zero), jnp.where(low, swap(packed), zero)]
    return jnp.concatenate(both, axis=0).astype(BF16)


def load_queries(mine_ref, chunk):
    start = pl.multiple_of(TOK + chunk * CHUNK, CHUNK)
    return unpack_queries(mine_ref[:, pl.ds(start, CHUNK), :])


def kv_block(kv_ref, j, count):
    return kv_ref[pl.ds(j * count, count), :TOK].reshape(count * TOK, LANES)


def fill_values(kv_ref, va_ref):
    @pl.when(pl.program_id(0) == 0)
    def _():
        for j in range(GROUP):
            kv = kv_ref[j, :TOK]
            va_ref[j] = jnp.where(low_half(TOK), jnp.ones_like(kv), kv)


def absorb(q, kv_ref, va_ref, top, acc):
    def scores(j):
        block = kv_block(kv_ref, j, BLOCK_FRAMES)
        return lax.dot_general(q, block, NT, preferred_element_type=F32)

    blocks = GROUP // BLOCK_FRAMES
    s = scores(0)
    for j in range(blocks):
        ahead = scores(j + 1) if j + 1 < blocks else None
        newtop = jnp.max(s, axis=-1, keepdims=True) * LOG2E
        if top is not None:
            newtop = jnp.maximum(top, newtop)
        p = jnp.exp2(s * LOG2E - newtop).astype(BF16)
        pv = jnp.dot(p, kv_block(va_ref, j, BLOCK_FRAMES), preferred_element_type=F32)
        acc = pv if top is None else acc * jnp.exp2(top - newtop) + pv
        top, s = newtop, ahead
    return top, acc


def own_kernel(first, mine_ref, *rest):
    state_ref, va_ref = rest[-2:]
    fill_values(mine_ref, va_ref)
    q = load_queries(mine_ref, pl.program_id(0) + first)
    top, acc = absorb(q, mine_ref, va_ref, None, None)
    lane = lax.broadcasted_iota(jnp.int32, acc.shape, 1)
    state_ref[...] = jnp.where(lane == 1, top, acc)


def other_kernel(starts, mine_ref, other_ref, *rest):
    state_refs = rest[: len(starts)]
    o_ref, va_ref = rest[-2:]
    fill_values(other_ref, va_ref)
    chunk = pl.program_id(0) + starts[0]
    q = load_queries(mine_ref, chunk)
    state = state_refs[0][...]
    for start, ref in zip(starts[1:], state_refs[1:], strict=True):
        state = jnp.where(chunk >= start, ref[...], state)
    top, acc = absorb(q, other_ref, va_ref, state[:, 1:2], state)
    out = acc / acc[:, :1]
    packed = jnp.where(low_half(ROWS // 2), swap(out[: ROWS // 2]), out[ROWS // 2 :])
    o_ref[...] = packed.astype(BF16).reshape(o_ref.shape)


def picks_kernel(mine_ref, picks_ref, me_ref, *rest):
    o_ref, va_ref = rest[-2:]
    fill_values(mine_ref, va_ref)
    step = pl.program_id(0)
    own = mine_ref[:, TOK : TOK + CHUNK, :]
    q = unpack_queries(jnp.where(step == 0, own, picks_ref[...]))
    top, acc = absorb(q, mine_ref, va_ref, None, None)
    sums = acc[:, :1]
    mean = acc / sums
    level = top + jnp.log2(sums)
    part0 = level.astype(BF16).astype(F32)
    part1 = (level - part0).astype(BF16).astype(F32)
    part2 = level - part0 - part1
    lane = lax.broadcasted_iota(jnp.int32, acc.shape, 1)
    low = jnp.where(lane == 0, part0, jnp.where(lane == 1, part1, part2))
    out = jnp.where(lane < HDIM, low, mean).astype(BF16).reshape(2, GROUP, CHUNK, LANES)
    side = me_ref[0] & 1
    side = jnp.where(step == 0, side, 1 - side)
    for half in range(2):
        o_ref[:, side, half * CHUNK : (half + 1) * CHUNK] = out[half]


VMEM = pl.BlockSpec(memory_space=pltpu.VMEM)
SMEM = pl.BlockSpec(memory_space=pltpu.SMEM)


def attend_settings(chunks):
    pairs = chunks * ROWS * GROUP * TOK
    return dict(
        grid=(chunks,),
        scratch_shapes=[pltpu.VMEM((GROUP, TOK, LANES), BF16)],
        compiler_params=pltpu.CompilerParams(vmem_limit_bytes=36 << 20),
        cost_estimate=pl.CostEstimate(
            flops=2 * pairs * LANES * 4, bytes_accessed=1 << 20, transcendentals=pairs
        ),
    )


ANY = pl.BlockSpec(memory_space=pl.ANY)


def attend_own(mine, first, last, after=()):
    return pl.pallas_call(
        functools.partial(own_kernel, first),
        in_specs=[VMEM] + [ANY] * len(after),
        out_specs=pl.BlockSpec((ROWS, LANES), lambda i: (i, 0)),
        out_shape=jax.ShapeDtypeStruct(((last - first) * ROWS, LANES), F32),
        name=f"attend_own_{first}",
        **attend_settings(last - first),
    )(mine, *after)


def attend_picks(mine, picks, me, after):
    return pl.pallas_call(
        picks_kernel,
        in_specs=[VMEM, VMEM, SMEM] + [ANY] * len(after),
        out_specs=VMEM,
        out_shape=jax.ShapeDtypeStruct((GROUP, 2, QMAX, LANES), BF16),
        name="attend_picks",
        **attend_settings(2),
    )(mine, picks, me, *after)


def attend_other(mine, other, states, after=()):
    counts = [state.shape[0] // ROWS for state in states]
    chunks = sum(counts)
    starts = [CHUNKS - sum(counts[i:]) for i in range(len(counts))]

    def state_spec(start, count):
        shift = start - starts[0]
        return pl.BlockSpec((ROWS, LANES), lambda i: (jnp.clip(i - shift, 0, count - 1), 0))

    return pl.pallas_call(
        functools.partial(other_kernel, starts),
        in_specs=[VMEM, VMEM]
        + [state_spec(*pair) for pair in zip(starts, counts, strict=True)]
        + [ANY] * len(after),
        out_specs=pl.BlockSpec((GROUP, CHUNK, LANES), lambda i: (0, i, 0)),
        out_shape=jax.ShapeDtypeStruct((GROUP, chunks * CHUNK, LANES), BF16),
        name="attend_other",
        **attend_settings(chunks),
    )(mine, other, *states, *after)


def join_heads(even_odd):
    top, bottom = [], []
    for even, odd in even_odd:
        low = low_half(even.shape[0])
        top.append(jnp.where(low, even, swap(odd)).astype(BF16))
        bottom.append(jnp.where(low, swap(even), odd).astype(BF16))
    return jnp.concatenate(top, axis=1), jnp.concatenate(bottom, axis=1)


def level_of(part):
    return part[:, 0:1] + part[:, 1:2] + part[:, 2:3]


def rows_kernel(part_ref, x_ref, w_ref, place_ref, slots_ref, counts_ref, owner_ref, me_ref, *rest):
    send_ref, att_ref = rest[-2:]
    heads = []
    for h in range(HEADS):
        a, b = part_ref[2 * h].astype(F32), part_ref[2 * h + 1].astype(F32)
        la, lb = level_of(a), level_of(b)
        most = jnp.maximum(la, lb)
        wa, wb = jnp.exp2(la - most), jnp.exp2(lb - most)
        heads.append((a * wa + b * wb) / (wa + wb))
    att = jnp.concatenate(
        [
            jnp.where(low_half(QMAX), swap(heads[2 * i]), heads[2 * i + 1]).astype(BF16)
            for i in range(HEADS // 2)
        ],
        axis=1,
    )
    att_ref[...] = att
    gap = jnp.zeros((TOK // 2 - CHUNK, D), BF16)
    placed = jnp.concatenate([att[:CHUNK], gap, att[CHUNK:], gap], axis=0)
    token_slot = jnp.where(slot_of_token(slots_ref[...]), 1.0, 0.0).astype(BF16)
    where = lax.dot_general(token_slot, place_ref[...], TN, preferred_element_type=F32).astype(BF16)
    chosen = jnp.dot(where, placed, preferred_element_type=F32).astype(BF16)
    x = lax.dot_general(token_slot, x_ref[...], TN, preferred_element_type=F32)
    rows = (x + jnp.dot(chosen, w_ref[...], preferred_element_type=F32)).astype(BF16)
    me = me_ref[0]
    slot = lax.broadcasted_iota(jnp.int32, rows.shape, 0)
    send_ref[...] = jnp.zeros_like(send_ref)
    send_ref[owner_ref[me]] = jnp.where(slot < counts_ref[me], rows, jnp.zeros_like(rows))


def track_rows(parts, x, w_out, place, slots, counts, owner, me, after):
    return pl.pallas_call(
        rows_kernel,
        in_specs=[VMEM] * 5 + [SMEM] * 3 + [ANY] * len(after),
        out_specs=[VMEM, VMEM],
        out_shape=[
            jax.ShapeDtypeStruct((FRAMES, QMAX, D), BF16),
            jax.ShapeDtypeStruct((QMAX, D), BF16),
        ],
        compiler_params=pltpu.CompilerParams(vmem_limit_bytes=20 << 20),
        cost_estimate=pl.CostEstimate(flops=2 << 30, bytes_accessed=4 << 20, transcendentals=0),
        name="track_rows",
    )(parts, x, w_out, place, slots, counts, owner, me, *after)


def mix_kernel(att1_ref, at2_ref, x_ref, w_ref, place_ref, mixed_ref):
    pairs = [(at2_ref[2 * i].astype(F32), at2_ref[2 * i + 1].astype(F32)) for i in range(HEADS // 2)]
    top, bottom = join_heads(pairs)
    placed = jnp.concatenate([att1_ref[:CHUNK], top, att1_ref[CHUNK:], bottom], axis=0)
    att = jnp.dot(place_ref[...], placed, preferred_element_type=F32).astype(BF16)
    mixed_ref[...] = (
        x_ref[...].astype(F32) + jnp.dot(att, w_ref[...], preferred_element_type=F32)
    ).astype(BF16)


def mix(att1, att2, x, w_out, place):
    return pl.pallas_call(
        mix_kernel,
        in_specs=[VMEM] * 5,
        out_specs=VMEM,
        out_shape=jax.ShapeDtypeStruct((TOK, D), BF16),
        compiler_params=pltpu.CompilerParams(vmem_limit_bytes=20 << 20),
        name="mix",
    )(att1, att2, x, w_out, place)


def correlate_kernel(rows_ref, mixed_ref, o_ref):
    step = o_ref.shape[1]
    start = pl.program_id(0) * step
    rows = rows_ref[pl.ds(start, step)].reshape(-1, D)
    corr = lax.dot_general(rows, mixed_ref[...], NT, preferred_element_type=F32)
    o_ref[...] = (corr * (1.0 / D**0.5)).reshape(o_ref.shape)


def correlate(arrived, mixed):
    step = 8
    return pl.pallas_call(
        correlate_kernel,
        grid=(FRAMES // step,),
        in_specs=[VMEM, VMEM],
        out_specs=pl.BlockSpec((1, step, QMAX, TOK), lambda i: (0, i, 0, 0)),
        out_shape=jax.ShapeDtypeStruct((1, FRAMES, QMAX, TOK), F32),
        compiler_params=pltpu.CompilerParams(vmem_limit_bytes=20 << 20),
        name="correlate",
    )(arrived, mixed)


def per_device(features, norm_gain, w_qkv, w_out, counts, query_index, owner):
    groups = [[2 * i + side for i in range(GROUP)] for side in range(2)]
    swap_sides = [(d, d ^ 1) for d in range(FRAMES)]
    me = lax.axis_index("frame").astype(jnp.int32).reshape(1)
    packed, place = project(features, norm_gain, query_index, w_qkv)
    mine = lax.all_to_all(packed, "frame", 0, 0, tiled=True, axis_index_groups=groups)
    picks = lax.ppermute(mine[:, TOK : TOK + CHUNK], "frame", swap_sides)
    other = lax.ppermute(mine[:, :TOK], "frame", swap_sides)
    state1 = attend_own(mine, 1, 3)
    parts = attend_picks(mine, picks, me, [state1])
    parts_here = lax.all_to_all(
        parts.reshape(FRAMES, QMAX, LANES), "frame", 0, 0, tiled=True
    )
    state2 = attend_own(mine, 3, SPLIT, [parts])
    send, att1 = track_rows(
        parts_here, features, w_out, place, query_index, counts, owner, me, [state2]
    )
    arrived = lax.all_to_all(send, "frame", 0, 0, tiled=True)
    state3 = attend_own(mine, SPLIT, CHUNKS, [att1])
    rest = attend_other(mine, other, [state1, state2, state3])
    rest, arrived = lax.optimization_barrier((rest, arrived))
    att2 = lax.all_to_all(rest, "frame", 0, 0, tiled=True, axis_index_groups=groups)
    mixed = mix(att1, att2, features, w_out, place)
    return mixed, correlate(arrived, mixed)


def solution(mesh):
    rows = P(("scene", "frame"), None)
    in_specs = (rows, P(), P(), P(), P("scene"), rows, P("scene"))
    out_specs = (rows, P(("scene", "frame"), None, None, None))
    return jax.shard_map(
        per_device, mesh=mesh, in_specs=in_specs, out_specs=out_specs, check_vma=False
    )
```

```python
import functools

import jax
import jax.numpy as jnp
from jax import lax
from jax.experimental import pallas as pl
from jax.experimental.pallas import tpu as pltpu
from jax.sharding import PartitionSpec as P

D = 1024
HEADS = 16
HDIM = 64
TOK = 256
FRAMES = 32
QMAX = 32
LANES = 128
LOG2E = 1.4426950408889634
NT = (((1,), (1,)), ((), ()))
TN = (((0,), (0,)), ((), ()))
CHUNK = 16
F32 = jnp.float32
BF16 = jnp.bfloat16


def low_half(rows):
    return lax.broadcasted_iota(jnp.int32, (rows, LANES), 1) < HDIM


def swap(x):
    return pltpu.roll(x, HDIM, 1)


def slot_of_token(slots):
    return lax.broadcasted_iota(jnp.int32, (TOK, QMAX), 0) == slots


def arrange(slots):
    picked = jnp.max(jnp.where(slot_of_token(slots), 1.0, 0.0), axis=1, keepdims=True)
    row = lax.broadcasted_iota(jnp.int32, (TOK, TOK), 0)
    col = lax.broadcasted_iota(jnp.int32, (TOK, TOK), 1)
    wide = jnp.broadcast_to(picked, (TOK, LANES)).astype(BF16)
    before = jnp.dot(jnp.where(col < row, 1.0, 0.0).astype(BF16), wide, preferred_element_type=F32)
    before = before[:, :1].astype(jnp.int32)
    total = jnp.sum(picked).astype(jnp.int32)
    token = lax.broadcasted_iota(jnp.int32, (TOK, 1), 0)
    rank = jnp.where(picked > 0.5, before, total + token - before)
    within = rank & 31
    place = (rank >> 5) * CHUNK + (within & 15) + jnp.where(within >= CHUNK, TOK // 2, 0)
    return jnp.where(place == col, 1.0, 0.0).astype(BF16)


STEPS = 4
WIDTH = D // STEPS


def project_kernel(x_ref, g_ref, slots_ref, w_hbm, o_ref, place_ref, n_ref, w_ref, sems):
    def load(step, part):
        cols = pl.ds(pl.multiple_of(part * D + step * WIDTH, WIDTH), WIDTH)
        return pltpu.make_async_copy(w_hbm.at[:, cols], w_ref.at[step, part], sems.at[step, part])

    step = pl.program_id(0)

    @pl.when(step == 0)
    def _():
        for i in range(STEPS):
            for part in range(3):
                load(i, part).start()
        place = arrange(slots_ref[...])
        place_ref[...] = place
        xf = x_ref[...].astype(F32)
        mean = jnp.mean(xf, axis=-1, keepdims=True)
        cen = xf - mean
        var = jnp.mean(cen * cen, axis=-1, keepdims=True)
        normed = (cen * lax.rsqrt(var + 1e-05) * g_ref[...]).astype(BF16)
        n_ref[...] = lax.dot_general(place, normed, TN, preferred_element_type=F32).astype(BF16)

    n = n_ref[...]

    def product(part):
        load(step, part).wait()
        return jnp.dot(n, w_ref[step, part], preferred_element_type=F32)

    q = product(0) * (1.0 / HDIM**0.5)
    k = product(1)
    v = product(2)
    half = TOK // 2
    low = low_half(TOK)
    lowh = low_half(half)
    for c in range(WIDTH // LANES):
        cols = slice(c * LANES, (c + 1) * LANES)
        kp, vp = k[:, cols], v[:, cols]
        qa, qb = q[:half, cols], q[half:, cols]
        o_ref[2 * c, :TOK] = jnp.where(low, kp, swap(vp)).astype(BF16)
        o_ref[2 * c + 1, :TOK] = jnp.where(low, swap(kp), vp).astype(BF16)
        o_ref[2 * c, TOK:] = jnp.where(lowh, qa, swap(qb)).astype(BF16)
        o_ref[2 * c + 1, TOK:] = jnp.where(lowh, swap(qa), qb).astype(BF16)


def project(x, gain, slots, w_qkv):
    rows = TOK + TOK // 2
    return pl.pallas_call(
        project_kernel,
        grid=(STEPS,),
        in_specs=[
            pl.BlockSpec((TOK, D), lambda i: (0, 0)),
            pl.BlockSpec((1, D), lambda i: (0, 0)),
            pl.BlockSpec((1, QMAX), lambda i: (0, 0)),
            pl.BlockSpec(memory_space=pl.ANY),
        ],
        out_specs=[
            pl.BlockSpec((HEADS // STEPS, rows, LANES), lambda i: (i, 0, 0)),
            pl.BlockSpec((TOK, TOK), lambda i: (0, 0)),
        ],
        out_shape=[
            jax.ShapeDtypeStruct((HEADS, rows, LANES), BF16),
            jax.ShapeDtypeStruct((TOK, TOK), BF16),
        ],
        scratch_shapes=[
            pltpu.VMEM((TOK, D), BF16),
            pltpu.VMEM((STEPS, 3, D, WIDTH), BF16),
            pltpu.SemaphoreType.DMA((STEPS, 3)),
        ],
        compiler_params=pltpu.CompilerParams(vmem_limit_bytes=60 << 20),
        name="project",
    )(x, gain.reshape(1, D), slots, w_qkv)


BLOCK_FRAMES = 4
GROUP = FRAMES // 2
CHUNKS = TOK // (2 * CHUNK)
ROWS = GROUP * 2 * CHUNK
SPLIT = 6


def unpack_queries(packed):
    packed = packed.reshape(GROUP * CHUNK, LANES).astype(F32)
    low = low_half(packed.shape[0])
    zero = jnp.zeros_like(packed)
    both = [jnp.where(low, packed, zero), jnp.where(low, swap(packed), zero)]
    return jnp.concatenate(both, axis=0).astype(BF16)


class Source:
    def __init__(self, kv_hbm, q_hbm, first, count, kv_ref, va_ref, q_ref, sems):
        self.kv_ref, self.va_ref, self.q_ref = kv_ref, va_ref, q_ref
        self.copies, self.waited = {}, set()
        rows = pl.ds(TOK + first * CHUNK, count * CHUNK)
        self.start("q", q_hbm.at[:, rows], q_ref, sems.at[0])
        for j in range(BLOCKS):
            frames = pl.ds(j * BLOCK_FRAMES, BLOCK_FRAMES)
            self.start(j, kv_hbm.at[frames, pl.ds(0, TOK)], kv_ref.at[frames], sems.at[1 + j])

    def start(self, name, source, target, sem):
        self.copies[name] = pltpu.make_async_copy(source, target, sem)
        self.copies[name].start()

    def wait(self, name):
        if name not in self.waited:
            self.waited.add(name)
            self.copies[name].wait()

    def keys(self, j):
        if j not in self.waited:
            self.wait(j)
            for f in range(j * BLOCK_FRAMES, (j + 1) * BLOCK_FRAMES):
                kv = self.kv_ref[f]
                self.va_ref[f] = jnp.where(low_half(TOK), jnp.ones_like(kv), kv)
        return self.block(self.kv_ref, j)

    def values(self, j):
        return self.block(self.va_ref, j)

    def block(self, ref, j):
        return ref[j * BLOCK_FRAMES : (j + 1) * BLOCK_FRAMES].reshape(BLOCK_FRAMES * TOK, LANES)

    def queries(self, i):
        self.wait("q")
        return unpack_queries(self.q_ref[:, i * CHUNK : (i + 1) * CHUNK])


BLOCKS = GROUP // BLOCK_FRAMES


def attend(items, source):
    steps = [(i, j) for i in range(len(items)) for j in range(BLOCKS)]
    queries = {}

    def scores(i, j):
        if i not in queries:
            queries[i] = items[i][0]()
        return lax.dot_general(queries[i], source.keys(j), NT, preferred_element_type=F32)

    s = scores(0, 0)
    top = acc = None
    for n, (i, j) in enumerate(steps):
        ahead = scores(*steps[n + 1]) if n + 1 < len(steps) else None
        if j == 0:
            acc = None if items[i][1] is None else items[i][1]()
            top = None if acc is None else acc[:, 1:2]
        newtop = jnp.max(s, axis=-1, keepdims=True) * LOG2E
        if top is not None:
            newtop = jnp.maximum(top, newtop)
        p = jnp.exp2(s * LOG2E - newtop).astype(BF16)
        pv = jnp.dot(p, source.values(j), preferred_element_type=F32)
        acc = pv if top is None else acc * jnp.exp2(top - newtop) + pv
        top, s = newtop, ahead
        if j == BLOCKS - 1:
            items[i][2](top, acc)


def own_kernel(first, count, mine_hbm, *rest):
    state_ref, tick_ref, kv_ref, va_ref, q_ref, sems = rest[-6:]
    tick_ref[...] = jnp.zeros_like(tick_ref)
    source = Source(mine_hbm, mine_hbm, first, count, kv_ref, va_ref, q_ref, sems)

    def item(i):
        def finish(top, acc):
            lane = lax.broadcasted_iota(jnp.int32, acc.shape, 1)
            state_ref[i * ROWS : (i + 1) * ROWS] = jnp.where(lane == 1, top, acc)

        return lambda: source.queries(i), None, finish

    attend([item(i) for i in range(count)], source)


def other_kernel(counts, mine_hbm, other_hbm, *rest):
    o_ref, kv_ref, va_ref, q_ref, sems, state_ref, state_sems = rest[-7:]
    chunks = sum(counts)
    source = Source(other_hbm, mine_hbm, CHUNKS - chunks, chunks, kv_ref, va_ref, q_ref, sems)
    places = [(n, k) for n, count in enumerate(counts) for k in range(count)]
    for n, count in enumerate(counts):
        target = state_ref.at[pl.ds(sum(counts[:n]) * ROWS, count * ROWS)]
        source.start(("state", n), rest[n], target, state_sems.at[n])

    def item(i):
        def state():
            source.wait(("state", places[i][0]))
            return state_ref[i * ROWS : (i + 1) * ROWS]

        def finish(top, acc):
            out = acc / acc[:, :1]
            packed = jnp.where(low_half(ROWS // 2), swap(out[: ROWS // 2]), out[ROWS // 2 :])
            packed = packed.astype(BF16).reshape(GROUP, CHUNK, LANES)
            o_ref[:, i * CHUNK : (i + 1) * CHUNK] = packed

        return lambda: source.queries(i), state, finish

    attend([item(i) for i in range(chunks)], source)


def picks_kernel(mine_hbm, picks_ref, me_ref, *rest):
    o_ref, tick_ref, kv_ref, va_ref, q_ref, sems = rest[-6:]
    tick_ref[...] = jnp.zeros_like(tick_ref)
    source = Source(mine_hbm, mine_hbm, 0, 1, kv_ref, va_ref, q_ref, sems)
    mine_side = me_ref[0] & 1

    def item(side, queries):
        def finish(top, acc):
            sums = acc[:, :1]
            mean = acc / sums
            level = top + jnp.log2(sums)
            part0 = level.astype(BF16).astype(F32)
            part1 = (level - part0).astype(BF16).astype(F32)
            part2 = level - part0 - part1
            lane = lax.broadcasted_iota(jnp.int32, acc.shape, 1)
            low = jnp.where(lane == 0, part0, jnp.where(lane == 1, part1, part2))
            out = jnp.where(lane < HDIM, low, mean).astype(BF16).reshape(2, GROUP, CHUNK, LANES)
            for half in range(2):
                o_ref[:, side, half * CHUNK : (half + 1) * CHUNK] = out[half]

        return queries, None, finish

    items = [
        item(mine_side, lambda: source.queries(0)),
        item(1 - mine_side, lambda: unpack_queries(picks_ref[...])),
    ]
    attend(items, source)


SMEM = pl.BlockSpec(memory_space=pltpu.SMEM)
ANY = pl.BlockSpec(memory_space=pl.ANY)
WHOLE = pl.BlockSpec()
TICK = jax.ShapeDtypeStruct((8, LANES), F32)
PARAMS = pltpu.CompilerParams(vmem_limit_bytes=60 << 20)


def attend_settings(chunks, work):
    pairs = work * ROWS * GROUP * TOK
    return dict(
        scratch_shapes=[
            pltpu.VMEM((GROUP, TOK, LANES), BF16),
            pltpu.VMEM((GROUP, TOK, LANES), BF16),
            pltpu.VMEM((GROUP, chunks * CHUNK, LANES), BF16),
            pltpu.SemaphoreType.DMA((1 + BLOCKS,)),
        ],
        compiler_params=PARAMS,
        cost_estimate=pl.CostEstimate(
            flops=2 * pairs * LANES * 4, bytes_accessed=1 << 20, transcendentals=pairs
        ),
    )


def attend_own(mine, first, last, after=()):
    count = last - first
    return pl.pallas_call(
        functools.partial(own_kernel, first, count),
        in_specs=[ANY] + [WHOLE] * len(after),
        out_specs=[WHOLE, WHOLE],
        out_shape=[jax.ShapeDtypeStruct((count * ROWS, LANES), F32), TICK],
        name=f"attend_own_{first}",
        **attend_settings(count, count),
    )(mine, *after)


def attend_picks(mine, picks, me, after):
    return pl.pallas_call(
        picks_kernel,
        in_specs=[ANY, WHOLE, SMEM] + [WHOLE] * len(after),
        out_specs=[WHOLE, WHOLE],
        out_shape=[jax.ShapeDtypeStruct((GROUP, 2, QMAX, LANES), BF16), TICK],
        name="attend_picks",
        **attend_settings(1, 2),
    )(mine, picks, me, *after)


def attend_other(mine, other, states):
    counts = [state.shape[0] // ROWS for state in states]
    chunks = sum(counts)
    settings = attend_settings(chunks, chunks)
    settings["scratch_shapes"] += [
        pltpu.VMEM((chunks * ROWS, LANES), F32),
        pltpu.SemaphoreType.DMA((len(states),)),
    ]
    return pl.pallas_call(
        functools.partial(other_kernel, counts),
        in_specs=[ANY] * (2 + len(states)),
        out_specs=WHOLE,
        out_shape=jax.ShapeDtypeStruct((GROUP, chunks * CHUNK, LANES), BF16),
        name="attend_other",
        **settings,
    )(mine, other, *states)


def join_heads(even_odd):
    top, bottom = [], []
    for even, odd in even_odd:
        low = low_half(even.shape[0])
        top.append(jnp.where(low, even, swap(odd)).astype(BF16))
        bottom.append(jnp.where(low, swap(even), odd).astype(BF16))
    return jnp.concatenate(top, axis=1), jnp.concatenate(bottom, axis=1)


def level_of(part):
    return part[:, 0:1] + part[:, 1:2] + part[:, 2:3]


def rows_kernel(part_ref, x_hbm, w_hbm, place_ref, slots_ref, counts_ref, owner_ref, me_ref, *rest):
    send_hbm, att_ref, x_ref, w_ref, zero_ref, rows_ref, sems = rest[-7:]
    load_w = pltpu.make_async_copy(w_hbm, w_ref, sems.at[0])
    load_x = pltpu.make_async_copy(x_hbm, x_ref, sems.at[1])
    load_w.start()
    load_x.start()
    zero_ref[...] = jnp.zeros_like(zero_ref)
    count = zero_ref.shape[0]
    clears = [
        pltpu.make_async_copy(zero_ref, send_hbm.at[pl.ds(i * count, count)], sems.at[2 + i])
        for i in range(FRAMES // count)
    ]
    for clear in clears:
        clear.start()
    heads = []
    for h in range(HEADS):
        a, b = part_ref[2 * h].astype(F32), part_ref[2 * h + 1].astype(F32)
        la, lb = level_of(a), level_of(b)
        most = jnp.maximum(la, lb)
        wa, wb = jnp.exp2(la - most), jnp.exp2(lb - most)
        heads.append((a * wa + b * wb) / (wa + wb))
    att = jnp.concatenate(
        [
            jnp.where(low_half(QMAX), swap(heads[2 * i]), heads[2 * i + 1]).astype(BF16)
            for i in range(HEADS // 2)
        ],
        axis=1,
    )
    att_ref[...] = att
    gap = jnp.zeros((TOK // 2 - CHUNK, D), BF16)
    placed = jnp.concatenate([att[:CHUNK], gap, att[CHUNK:], gap], axis=0)
    token_slot = jnp.where(slot_of_token(slots_ref[...]), 1.0, 0.0).astype(BF16)
    where = lax.dot_general(token_slot, place_ref[...], TN, preferred_element_type=F32).astype(BF16)
    chosen = jnp.dot(where, placed, preferred_element_type=F32).astype(BF16)
    load_x.wait()
    x = lax.dot_general(token_slot, x_ref[...], TN, preferred_element_type=F32)
    load_w.wait()
    rows = (x + jnp.dot(chosen, w_ref[...], preferred_element_type=F32)).astype(BF16)
    me = me_ref[0]
    slot = lax.broadcasted_iota(jnp.int32, rows.shape, 0)
    rows_ref[...] = jnp.where(slot < counts_ref[me], rows, jnp.zeros_like(rows))
    for clear in clears:
        clear.wait()
    put = pltpu.make_async_copy(rows_ref, send_hbm.at[owner_ref[me]], sems.at[0])
    put.start()
    put.wait()


def track_rows(parts, x, w_out, place, slots, counts, owner, me, after):
    return pl.pallas_call(
        rows_kernel,
        in_specs=[WHOLE, ANY, ANY, WHOLE, WHOLE] + [SMEM] * 3 + [WHOLE] * len(after),
        out_specs=[ANY, WHOLE],
        scratch_shapes=[
            pltpu.VMEM((TOK, D), BF16),
            pltpu.VMEM((D, D), BF16),
            pltpu.VMEM((8, QMAX, D), BF16),
            pltpu.VMEM((QMAX, D), BF16),
            pltpu.SemaphoreType.DMA((2 + FRAMES // 8,)),
        ],
        out_shape=[
            jax.ShapeDtypeStruct((FRAMES, QMAX, D), BF16),
            jax.ShapeDtypeStruct((QMAX, D), BF16),
        ],
        compiler_params=PARAMS,
        cost_estimate=pl.CostEstimate(flops=2 << 30, bytes_accessed=4 << 20, transcendentals=0),
        name="track_rows",
    )(parts, x, w_out, place, slots, counts, owner, me, *after)


def finish_kernel(att1_ref, at2_ref, place_ref, rows_hbm, x_hbm, w_hbm, mixed_ref, corr_ref, x_ref, w_ref, rows_ref, sems):
    load_rows = pltpu.make_async_copy(rows_hbm, rows_ref, sems.at[2])

    @pl.when(pl.program_id(0) == 0)
    def _():
        load_w = pltpu.make_async_copy(w_hbm, w_ref, sems.at[0])
        load_x = pltpu.make_async_copy(x_hbm, x_ref, sems.at[1])
        load_w.start()
        load_x.start()
        load_rows.start()
        pairs = [
            (at2_ref[2 * i].astype(F32), at2_ref[2 * i + 1].astype(F32)) for i in range(HEADS // 2)
        ]
        top, bottom = join_heads(pairs)
        placed = jnp.concatenate([att1_ref[:CHUNK], top, att1_ref[CHUNK:], bottom], axis=0)
        att = jnp.dot(place_ref[...], placed, preferred_element_type=F32).astype(BF16)
        load_x.wait()
        load_w.wait()
        mixed_ref[...] = (
            x_ref[...].astype(F32) + jnp.dot(att, w_ref[...], preferred_element_type=F32)
        ).astype(BF16)
        load_rows.wait()

    step = corr_ref.shape[1]
    rows = rows_ref[pl.ds(pl.program_id(0) * step, step)].reshape(-1, D)
    corr = lax.dot_general(rows, mixed_ref[...], NT, preferred_element_type=F32)
    corr_ref[...] = (corr * (1.0 / D**0.5)).reshape(corr_ref.shape)


def finish(att1, att2, x, w_out, place, arrived):
    step = 8
    return pl.pallas_call(
        finish_kernel,
        grid=(FRAMES // step,),
        in_specs=[
            pl.BlockSpec(att1.shape, lambda i: (0, 0)),
            pl.BlockSpec(att2.shape, lambda i: (0, 0, 0)),
            pl.BlockSpec(place.shape, lambda i: (0, 0)),
        ]
        + [ANY] * 3,
        out_specs=[
            pl.BlockSpec((TOK, D), lambda i: (0, 0)),
            pl.BlockSpec((1, step, QMAX, TOK), lambda i: (0, i, 0, 0)),
        ],
        out_shape=[
            jax.ShapeDtypeStruct((TOK, D), BF16),
            jax.ShapeDtypeStruct((1, FRAMES, QMAX, TOK), F32),
        ],
        scratch_shapes=[
            pltpu.VMEM((TOK, D), BF16),
            pltpu.VMEM((D, D), BF16),
            pltpu.VMEM((FRAMES, QMAX, D), BF16),
            pltpu.SemaphoreType.DMA((3,)),
        ],
        compiler_params=PARAMS,
        name="finish",
    )(att1, att2, place, arrived, x, w_out)


def per_device(features, norm_gain, w_qkv, w_out, counts, query_index, owner):
    groups = [[2 * i + side for i in range(GROUP)] for side in range(2)]
    swap_sides = [(d, d ^ 1) for d in range(FRAMES)]
    me = lax.axis_index("frame").astype(jnp.int32).reshape(1)
    packed, place = project(features, norm_gain, query_index, w_qkv)
    mine = lax.all_to_all(packed, "frame", 0, 0, tiled=True, axis_index_groups=groups)
    picks = lax.ppermute(mine[:, TOK : TOK + CHUNK], "frame", swap_sides)
    other = lax.ppermute(mine[:, :TOK], "frame", swap_sides)
    state1, tick = attend_own(mine, 1, 3)
    parts, tick = attend_picks(mine, picks, me, [tick])
    parts_here = lax.all_to_all(
        parts.reshape(FRAMES, QMAX, LANES), "frame", 0, 0, tiled=True
    )
    state2, tick = attend_own(mine, 3, SPLIT, [tick])
    send, att1 = track_rows(
        parts_here, features, w_out, place, query_index, counts, owner, me, [tick]
    )
    arrived = lax.all_to_all(send, "frame", 0, 0, tiled=True)
    state3, _ = attend_own(mine, SPLIT, CHUNKS, [att1])
    rest = attend_other(mine, other, [state1, state2, state3])
    rest, arrived = lax.optimization_barrier((rest, arrived))
    att2 = lax.all_to_all(rest, "frame", 0, 0, tiled=True, axis_index_groups=groups)
    return tuple(finish(att1, att2, features, w_out, place, arrived))


def solution(mesh):
    rows = P(("scene", "frame"), None)
    in_specs = (rows, P(), P(), P(), P("scene"), rows, P("scene"))
    out_specs = (rows, P(("scene", "frame"), None, None, None))
    return jax.shard_map(
        per_device, mesh=mesh, in_specs=in_specs, out_specs=out_specs, check_vma=False
    )
```

```python
import functools

import jax
import jax.numpy as jnp
from jax import lax
from jax.experimental import pallas as pl
from jax.experimental.pallas import tpu as pltpu
from jax.sharding import PartitionSpec as P

D = 1024
HEADS = 16
HDIM = 64
TOK = 256
FRAMES = 32
QMAX = 32
LANES = 128
LOG2E = 1.4426950408889634
NT = (((1,), (1,)), ((), ()))
TN = (((0,), (0,)), ((), ()))
CHUNK = 16
F32 = jnp.float32
BF16 = jnp.bfloat16


def low_half(rows):
    return lax.broadcasted_iota(jnp.int32, (rows, LANES), 1) < HDIM


def swap(x):
    return pltpu.roll(x, HDIM, 1)


def slot_of_token(slots):
    return lax.broadcasted_iota(jnp.int32, (TOK, QMAX), 0) == slots


def arrange(slots):
    picked = jnp.max(jnp.where(slot_of_token(slots), 1.0, 0.0), axis=1, keepdims=True)
    row = lax.broadcasted_iota(jnp.int32, (TOK, TOK), 0)
    col = lax.broadcasted_iota(jnp.int32, (TOK, TOK), 1)
    wide = jnp.broadcast_to(picked, (TOK, LANES)).astype(BF16)
    before = jnp.dot(jnp.where(col < row, 1.0, 0.0).astype(BF16), wide, preferred_element_type=F32)
    before = before[:, :1].astype(jnp.int32)
    total = jnp.sum(picked).astype(jnp.int32)
    token = lax.broadcasted_iota(jnp.int32, (TOK, 1), 0)
    rank = jnp.where(picked > 0.5, before, total + token - before)
    within = rank & 31
    place = (rank >> 5) * CHUNK + (within & 15) + jnp.where(within >= CHUNK, TOK // 2, 0)
    return jnp.where(place == col, 1.0, 0.0).astype(BF16)


def project_kernel(x_ref, g_ref, slots_ref, wq_ref, wk_ref, wv_ref, o_ref, place_ref, n_ref):
    @pl.when(pl.program_id(0) == 0)
    def _():
        place = arrange(slots_ref[...])
        place_ref[...] = place
        xf = x_ref[...].astype(F32)
        mean = jnp.mean(xf, axis=-1, keepdims=True)
        cen = xf - mean
        var = jnp.mean(cen * cen, axis=-1, keepdims=True)
        normed = (cen * lax.rsqrt(var + 1e-05) * g_ref[...]).astype(BF16)
        n_ref[...] = lax.dot_general(place, normed, TN, preferred_element_type=F32).astype(BF16)

    n = n_ref[...]
    q = jnp.dot(n, wq_ref[...], preferred_element_type=F32) * (1.0 / HDIM**0.5)
    k = jnp.dot(n, wk_ref[...], preferred_element_type=F32)
    v = jnp.dot(n, wv_ref[...], preferred_element_type=F32)
    half = TOK // 2
    low = low_half(TOK)
    lowh = low_half(half)
    for c in range(wq_ref.shape[1] // LANES):
        cols = slice(c * LANES, (c + 1) * LANES)
        kp, vp = k[:, cols], v[:, cols]
        qa, qb = q[:half, cols], q[half:, cols]
        o_ref[2 * c, :TOK] = jnp.where(low, kp, swap(vp)).astype(BF16)
        o_ref[2 * c + 1, :TOK] = jnp.where(low, swap(kp), vp).astype(BF16)
        o_ref[2 * c, TOK:] = jnp.where(lowh, qa, swap(qb)).astype(BF16)
        o_ref[2 * c + 1, TOK:] = jnp.where(lowh, swap(qa), qb).astype(BF16)


def project(x, gain, slots, w_qkv):
    steps = 4
    width = D // steps
    return pl.pallas_call(
        project_kernel,
        grid=(steps,),
        in_specs=[
            pl.BlockSpec((TOK, D), lambda i: (0, 0)),
            pl.BlockSpec((1, D), lambda i: (0, 0)),
            pl.BlockSpec((1, QMAX), lambda i: (0, 0)),
            pl.BlockSpec((D, width), lambda i: (0, i)),
            pl.BlockSpec((D, width), lambda i: (0, i + steps)),
            pl.BlockSpec((D, width), lambda i: (0, i + 2 * steps)),
        ],
        out_specs=[
            pl.BlockSpec((HEADS // steps, TOK + TOK // 2, LANES), lambda i: (i, 0, 0)),
            pl.BlockSpec((TOK, TOK), lambda i: (0, 0)),
        ],
        out_shape=[
            jax.ShapeDtypeStruct((HEADS, TOK + TOK // 2, LANES), BF16),
            jax.ShapeDtypeStruct((TOK, TOK), BF16),
        ],
        scratch_shapes=[pltpu.VMEM((TOK, D), BF16)],
        compiler_params=pltpu.CompilerParams(vmem_limit_bytes=60 << 20),
        name="project",
    )(x, gain.reshape(1, D), slots, w_qkv, w_qkv, w_qkv)


BLOCK_FRAMES = 4
GROUP = FRAMES // 2
CHUNKS = TOK // (2 * CHUNK)
ROWS = GROUP * 2 * CHUNK
SPLIT = 6


def unpack_queries(packed):
    packed = packed.reshape(GROUP * CHUNK, LANES).astype(F32)
    low = low_half(packed.shape[0])
    zero = jnp.zeros_like(packed)
    both = [jnp.where(low, packed, zero), jnp.where(low, swap(packed), zero)]
    return jnp.concatenate(both, axis=0).astype(BF16)


def load_queries(mine_ref, chunk):
    start = pl.multiple_of(TOK + chunk * CHUNK, CHUNK)
    return unpack_queries(mine_ref[:, pl.ds(start, CHUNK), :])


def kv_block(kv_ref, j, count):
    return kv_ref[pl.ds(j * count, count), :TOK].reshape(count * TOK, LANES)


def fill_values(kv_ref, va_ref):
    @pl.when(pl.program_id(0) == 0)
    def _():
        for j in range(GROUP):
            kv = kv_ref[j, :TOK]
            va_ref[j] = jnp.where(low_half(TOK), jnp.ones_like(kv), kv)


def absorb(q, kv_ref, va_ref, top, acc):
    def scores(j):
        block = kv_block(kv_ref, j, BLOCK_FRAMES)
        return lax.dot_general(q, block, NT, preferred_element_type=F32)

    blocks = GROUP // BLOCK_FRAMES
    s = scores(0)
    for j in range(blocks):
        ahead = scores(j + 1) if j + 1 < blocks else None
        newtop = jnp.max(s, axis=-1, keepdims=True) * LOG2E
        if top is not None:
            newtop = jnp.maximum(top, newtop)
        p = jnp.exp2(s * LOG2E - newtop).astype(BF16)
        pv = jnp.dot(p, kv_block(va_ref, j, BLOCK_FRAMES), preferred_element_type=F32)
        acc = pv if top is None else acc * jnp.exp2(top - newtop) + pv
        top, s = newtop, ahead
    return top, acc


def own_kernel(first, mine_ref, *rest):
    state_ref, tick_ref, va_ref = rest[-3:]
    tick_ref[...] = jnp.zeros_like(tick_ref)
    fill_values(mine_ref, va_ref)
    q = load_queries(mine_ref, pl.program_id(0) + first)
    top, acc = absorb(q, mine_ref, va_ref, None, None)
    lane = lax.broadcasted_iota(jnp.int32, acc.shape, 1)
    state_ref[...] = jnp.where(lane == 1, top, acc)


def other_kernel(starts, mine_ref, other_ref, *rest):
    state_refs = rest[: len(starts)]
    o_ref, va_ref = rest[-2:]
    fill_values(other_ref, va_ref)
    chunk = pl.program_id(0) + starts[0]
    q = load_queries(mine_ref, chunk)
    state = state_refs[0][...]
    for start, ref in zip(starts[1:], state_refs[1:], strict=True):
        state = jnp.where(chunk >= start, ref[...], state)
    top, acc = absorb(q, other_ref, va_ref, state[:, 1:2], state)
    out = acc / acc[:, :1]
    packed = jnp.where(low_half(ROWS // 2), swap(out[: ROWS // 2]), out[ROWS // 2 :])
    o_ref[...] = packed.astype(BF16).reshape(o_ref.shape)


def picks_kernel(mine_ref, picks_ref, me_ref, *rest):
    o_ref, tick_ref, va_ref = rest[-3:]
    tick_ref[...] = jnp.zeros_like(tick_ref)
    fill_values(mine_ref, va_ref)
    step = pl.program_id(0)
    own = mine_ref[:, TOK : TOK + CHUNK, :]
    q = unpack_queries(jnp.where(step == 0, own, picks_ref[...]))
    top, acc = absorb(q, mine_ref, va_ref, None, None)
    sums = acc[:, :1]
    mean = acc / sums
    level = top + jnp.log2(sums)
    part0 = level.astype(BF16).astype(F32)
    part1 = (level - part0).astype(BF16).astype(F32)
    part2 = level - part0 - part1
    lane = lax.broadcasted_iota(jnp.int32, acc.shape, 1)
    low = jnp.where(lane == 0, part0, jnp.where(lane == 1, part1, part2))
    out = jnp.where(lane < HDIM, low, mean).astype(BF16).reshape(2, GROUP, CHUNK, LANES)
    side = me_ref[0] & 1
    side = jnp.where(step == 0, side, 1 - side)
    for half in range(2):
        o_ref[:, side, half * CHUNK : (half + 1) * CHUNK] = out[half]


VMEM = pl.BlockSpec(memory_space=pltpu.VMEM)
SMEM = pl.BlockSpec(memory_space=pltpu.SMEM)


def attend_settings(chunks):
    pairs = chunks * ROWS * GROUP * TOK
    return dict(
        grid=(chunks,),
        scratch_shapes=[pltpu.VMEM((GROUP, TOK, LANES), BF16)],
        compiler_params=pltpu.CompilerParams(vmem_limit_bytes=20 << 20),
        cost_estimate=pl.CostEstimate(
            flops=2 * pairs * LANES * 4, bytes_accessed=1 << 20, transcendentals=pairs
        ),
    )


HBM = pl.BlockSpec(memory_space=pltpu.HBM)
TICK = jax.ShapeDtypeStruct((8, LANES), F32)


def attend_own(mine, first, last, after=()):
    return pl.pallas_call(
        functools.partial(own_kernel, first),
        in_specs=[VMEM] + [VMEM if tick.ndim == 2 else HBM for tick in after],
        out_specs=[pl.BlockSpec((ROWS, LANES), lambda i: (i, 0)), VMEM],
        out_shape=[jax.ShapeDtypeStruct(((last - first) * ROWS, LANES), F32), TICK],
        name=f"attend_own_{first}",
        **attend_settings(last - first),
    )(mine, *after)


def attend_picks(mine, picks, me, after):
    return pl.pallas_call(
        picks_kernel,
        in_specs=[VMEM, VMEM, SMEM] + [VMEM] * len(after),
        out_specs=[pl.BlockSpec((GROUP, 2, QMAX, LANES), lambda i: (0, 0, 0, 0)), VMEM],
        out_shape=[jax.ShapeDtypeStruct((GROUP, 2, QMAX, LANES), BF16), TICK],
        name="attend_picks",
        **attend_settings(2),
    )(mine, picks, me, *after)


def attend_other(mine, other, states, after=()):
    counts = [state.shape[0] // ROWS for state in states]
    chunks = sum(counts)
    starts = [CHUNKS - sum(counts[i:]) for i in range(len(counts))]

    def state_spec(start, count):
        shift = start - starts[0]
        return pl.BlockSpec((ROWS, LANES), lambda i: (jnp.clip(i - shift, 0, count - 1), 0))

    return pl.pallas_call(
        functools.partial(other_kernel, starts),
        in_specs=[VMEM, VMEM]
        + [state_spec(*pair) for pair in zip(starts, counts, strict=True)]
        + [VMEM] * len(after),
        out_specs=pl.BlockSpec((GROUP, CHUNK, LANES), lambda i: (0, i, 0)),
        out_shape=jax.ShapeDtypeStruct((GROUP, chunks * CHUNK, LANES), BF16),
        name="attend_other",
        **attend_settings(chunks),
    )(mine, other, *states, *after)


def join_heads(even_odd):
    top, bottom = [], []
    for even, odd in even_odd:
        low = low_half(even.shape[0])
        top.append(jnp.where(low, even, swap(odd)).astype(BF16))
        bottom.append(jnp.where(low, swap(even), odd).astype(BF16))
    return jnp.concatenate(top, axis=1), jnp.concatenate(bottom, axis=1)


def level_of(part):
    return part[:, 0:1] + part[:, 1:2] + part[:, 2:3]


def rows_kernel(part_ref, w_hbm, zeros_hbm, x_ref, place_ref, slots_ref, counts_ref, owner_ref, me_ref, *rest):
    send_hbm, att_ref, w_ref, rows_ref, sems = rest[-5:]
    load_w = pltpu.make_async_copy(w_hbm, w_ref, sems.at[0])
    load_w.start()
    heads = []
    for h in range(HEADS):
        a, b = part_ref[2 * h].astype(F32), part_ref[2 * h + 1].astype(F32)
        la, lb = level_of(a), level_of(b)
        most = jnp.maximum(la, lb)
        wa, wb = jnp.exp2(la - most), jnp.exp2(lb - most)
        heads.append((a * wa + b * wb) / (wa + wb))
    att = jnp.concatenate(
        [
            jnp.where(low_half(QMAX), swap(heads[2 * i]), heads[2 * i + 1]).astype(BF16)
            for i in range(HEADS // 2)
        ],
        axis=1,
    )
    att_ref[...] = att
    gap = jnp.zeros((TOK // 2 - CHUNK, D), BF16)
    placed = jnp.concatenate([att[:CHUNK], gap, att[CHUNK:], gap], axis=0)
    token_slot = jnp.where(slot_of_token(slots_ref[...]), 1.0, 0.0).astype(BF16)
    where = lax.dot_general(token_slot, place_ref[...], TN, preferred_element_type=F32).astype(BF16)
    chosen = jnp.dot(where, placed, preferred_element_type=F32).astype(BF16)
    x = lax.dot_general(token_slot, x_ref[...], TN, preferred_element_type=F32)
    load_w.wait()
    rows = (x + jnp.dot(chosen, w_ref[...], preferred_element_type=F32)).astype(BF16)
    me = me_ref[0]
    slot = lax.broadcasted_iota(jnp.int32, rows.shape, 0)
    rows_ref[...] = jnp.where(slot < counts_ref[me], rows, jnp.zeros_like(rows))
    put = pltpu.make_async_copy(rows_ref, send_hbm.at[owner_ref[me]], sems.at[1])
    put.start()
    put.wait()


def track_rows(parts, w_out, zeros, x, place, slots, counts, owner, me, after):
    return pl.pallas_call(
        rows_kernel,
        in_specs=[VMEM, HBM, HBM] + [VMEM] * 3 + [SMEM] * 3 + [VMEM] * len(after),
        out_specs=[HBM, VMEM],
        input_output_aliases={2: 0},
        scratch_shapes=[
            pltpu.VMEM((D, D), BF16),
            pltpu.VMEM((QMAX, D), BF16),
            pltpu.SemaphoreType.DMA((2,)),
        ],
        out_shape=[
            jax.ShapeDtypeStruct((FRAMES, QMAX, D), BF16),
            jax.ShapeDtypeStruct((QMAX, D), BF16),
        ],
        compiler_params=pltpu.CompilerParams(vmem_limit_bytes=58 << 20),
        cost_estimate=pl.CostEstimate(flops=2 << 30, bytes_accessed=4 << 20, transcendentals=0),
        name="track_rows",
    )(parts, w_out, zeros, x, place, slots, counts, owner, me, *after)


def finish_kernel(att1_ref, at2_ref, place_ref, rows_ref, x_ref, w_hbm, mixed_ref, corr_ref, w_ref, sems):

    @pl.when(pl.program_id(0) == 0)
    def _():
        load_w = pltpu.make_async_copy(w_hbm, w_ref, sems)
        load_w.start()
        pairs = [
            (at2_ref[2 * i].astype(F32), at2_ref[2 * i + 1].astype(F32)) for i in range(HEADS // 2)
        ]
        top, bottom = join_heads(pairs)
        placed = jnp.concatenate([att1_ref[:CHUNK], top, att1_ref[CHUNK:], bottom], axis=0)
        att = jnp.dot(place_ref[...], placed, preferred_element_type=F32).astype(BF16)
        load_w.wait()
        mixed_ref[...] = (
            x_ref[...].astype(F32) + jnp.dot(att, w_ref[...], preferred_element_type=F32)
        ).astype(BF16)

    step = corr_ref.shape[1]
    rows = rows_ref[pl.ds(pl.program_id(0) * step, step)].reshape(-1, D)
    corr = lax.dot_general(rows, mixed_ref[...], NT, preferred_element_type=F32)
    corr_ref[...] = (corr * (1.0 / D**0.5)).reshape(corr_ref.shape)


def finish(att1, att2, x, w_out, place, arrived):
    step = 8
    return pl.pallas_call(
        finish_kernel,
        grid=(FRAMES // step,),
        in_specs=[VMEM] * 5 + [HBM],
        out_specs=[
            pl.BlockSpec((TOK, D), lambda i: (0, 0)),
            pl.BlockSpec((1, step, QMAX, TOK), lambda i: (0, i, 0, 0)),
        ],
        out_shape=[
            jax.ShapeDtypeStruct((TOK, D), BF16),
            jax.ShapeDtypeStruct((1, FRAMES, QMAX, TOK), F32),
        ],
        scratch_shapes=[
            pltpu.VMEM((D, D), BF16),
            pltpu.SemaphoreType.DMA,
        ],
        compiler_params=pltpu.CompilerParams(vmem_limit_bytes=58 << 20),
        name="finish",
    )(att1, att2, place, arrived, x, w_out)


def per_device(features, norm_gain, w_qkv, w_out, counts, query_index, owner):
    groups = [[2 * i + side for i in range(GROUP)] for side in range(2)]
    swap_sides = [(d, d ^ 1) for d in range(FRAMES)]
    me = lax.axis_index("frame").astype(jnp.int32).reshape(1)
    packed, place = project(features, norm_gain, query_index, w_qkv)
    mine = lax.all_to_all(packed, "frame", 0, 0, tiled=True, axis_index_groups=groups)
    picks = lax.ppermute(mine[:, TOK : TOK + CHUNK], "frame", swap_sides)
    other = lax.ppermute(mine[:, :TOK], "frame", swap_sides)
    zeros = jnp.zeros((FRAMES, QMAX, D), BF16)
    state1, tick = attend_own(mine, 1, 3, [zeros])
    parts, tick = attend_picks(mine, picks, me, [tick])
    parts_here = lax.all_to_all(
        parts.reshape(FRAMES, QMAX, LANES), "frame", 0, 0, tiled=True
    )
    state2, tick = attend_own(mine, 3, SPLIT, [tick])
    send, att1 = track_rows(
        parts_here, w_out, zeros, features, place, query_index, counts, owner, me, [tick]
    )
    arrived = lax.all_to_all(send, "frame", 0, 0, tiled=True)
    state3, _ = attend_own(mine, SPLIT, CHUNKS, [att1])
    rest = attend_other(mine, other, [state1, state2, state3])
    rest, arrived = lax.optimization_barrier((rest, arrived))
    att2 = lax.all_to_all(rest, "frame", 0, 0, tiled=True, axis_index_groups=groups)
    return tuple(finish(att1, att2, features, w_out, place, arrived))


def solution(mesh):
    rows = P(("scene", "frame"), None)
    in_specs = (rows, P(), P(), P(), P("scene"), rows, P("scene"))
    out_specs = (rows, P(("scene", "frame"), None, None, None))
    return jax.shard_map(
        per_device, mesh=mesh, in_specs=in_specs, out_specs=out_specs, check_vma=False
    )
```

```python
import functools

import jax
import jax.numpy as jnp
from jax import lax
from jax.experimental import pallas as pl
from jax.experimental.pallas import tpu as pltpu
from jax.sharding import PartitionSpec as P

D = 1024
HEADS = 16
HDIM = 64
TOK = 256
FRAMES = 32
QMAX = 32
LANES = 128
LOG2E = 1.4426950408889634
NT = (((1,), (1,)), ((), ()))
TN = (((0,), (0,)), ((), ()))
CHUNK = 16
F32 = jnp.float32
BF16 = jnp.bfloat16


def low_half(rows):
    return lax.broadcasted_iota(jnp.int32, (rows, LANES), 1) < HDIM


def swap(x):
    return pltpu.roll(x, HDIM, 1)


def slot_of_token(slots):
    return lax.broadcasted_iota(jnp.int32, (TOK, QMAX), 0) == slots


def arrange(slots):
    picked = jnp.max(jnp.where(slot_of_token(slots), 1.0, 0.0), axis=1, keepdims=True)
    row = lax.broadcasted_iota(jnp.int32, (TOK, TOK), 0)
    col = lax.broadcasted_iota(jnp.int32, (TOK, TOK), 1)
    wide = jnp.broadcast_to(picked, (TOK, LANES)).astype(BF16)
    before = jnp.dot(jnp.where(col < row, 1.0, 0.0).astype(BF16), wide, preferred_element_type=F32)
    before = before[:, :1].astype(jnp.int32)
    total = jnp.sum(picked).astype(jnp.int32)
    token = lax.broadcasted_iota(jnp.int32, (TOK, 1), 0)
    rank = jnp.where(picked > 0.5, before, total + token - before)
    within = rank & 31
    place = (rank >> 5) * CHUNK + (within & 15) + jnp.where(within >= CHUNK, TOK // 2, 0)
    return jnp.where(place == col, 1.0, 0.0).astype(BF16)


STEPS = 4
WIDTH = D // STEPS


def project_kernel(x_ref, g_ref, slots_ref, w_hbm, o_ref, place_ref, n_ref, w_ref, sems):
    step = pl.program_id(0)

    @pl.when(step == 0)
    def _():
        loads = []
        for i in range(STEPS):
            rows = pl.ds(i * WIDTH, WIDTH)
            loads.append(pltpu.make_async_copy(w_hbm.at[rows], w_ref.at[rows], sems.at[i]))
            loads[i].start()
        place = arrange(slots_ref[...])
        place_ref[...] = place
        xf = x_ref[...].astype(F32)
        mean = jnp.mean(xf, axis=-1, keepdims=True)
        cen = xf - mean
        var = jnp.mean(cen * cen, axis=-1, keepdims=True)
        normed = (cen * lax.rsqrt(var + 1e-05) * g_ref[...]).astype(BF16)
        n_ref[...] = lax.dot_general(place, normed, TN, preferred_element_type=F32).astype(BF16)
        for load in loads:
            load.wait()

    n = n_ref[...]

    def product(part):
        cols = pl.ds(pl.multiple_of(part * D + step * WIDTH, WIDTH), WIDTH)
        return jnp.dot(n, w_ref[:, cols], preferred_element_type=F32)

    q = product(0) * (1.0 / HDIM**0.5)
    k = product(1)
    v = product(2)
    half = TOK // 2
    low = low_half(TOK)
    lowh = low_half(half)
    for c in range(WIDTH // LANES):
        cols = slice(c * LANES, (c + 1) * LANES)
        kp, vp = k[:, cols], v[:, cols]
        qa, qb = q[:half, cols], q[half:, cols]
        o_ref[2 * c, :TOK] = jnp.where(low, kp, swap(vp)).astype(BF16)
        o_ref[2 * c + 1, :TOK] = jnp.where(low, swap(kp), vp).astype(BF16)
        o_ref[2 * c, TOK:] = jnp.where(lowh, qa, swap(qb)).astype(BF16)
        o_ref[2 * c + 1, TOK:] = jnp.where(lowh, swap(qa), qb).astype(BF16)


def project(x, gain, slots, w_qkv):
    rows = TOK + TOK // 2
    return pl.pallas_call(
        project_kernel,
        grid=(STEPS,),
        in_specs=[
            pl.BlockSpec((TOK, D), lambda i: (0, 0)),
            pl.BlockSpec((1, D), lambda i: (0, 0)),
            pl.BlockSpec((1, QMAX), lambda i: (0, 0)),
            pl.BlockSpec(memory_space=pl.ANY),
        ],
        out_specs=[
            pl.BlockSpec((HEADS // STEPS, rows, LANES), lambda i: (i, 0, 0)),
            pl.BlockSpec((TOK, TOK), lambda i: (0, 0)),
        ],
        out_shape=[
            jax.ShapeDtypeStruct((HEADS, rows, LANES), BF16),
            jax.ShapeDtypeStruct((TOK, TOK), BF16),
        ],
        scratch_shapes=[
            pltpu.VMEM((TOK, D), BF16),
            pltpu.VMEM((D, 3 * D), BF16),
            pltpu.SemaphoreType.DMA((STEPS,)),
        ],
        compiler_params=pltpu.CompilerParams(vmem_limit_bytes=60 << 20),
        name="project",
    )(x, gain.reshape(1, D), slots, w_qkv)


BLOCK_FRAMES = 4
GROUP = FRAMES // 2
CHUNKS = TOK // (2 * CHUNK)
ROWS = GROUP * 2 * CHUNK
SPLIT = 6


def unpack_queries(packed):
    packed = packed.reshape(GROUP * CHUNK, LANES).astype(F32)
    low = low_half(packed.shape[0])
    zero = jnp.zeros_like(packed)
    both = [jnp.where(low, packed, zero), jnp.where(low, swap(packed), zero)]
    return jnp.concatenate(both, axis=0).astype(BF16)


def load_queries(mine_ref, chunk):
    start = pl.multiple_of(TOK + chunk * CHUNK, CHUNK)
    return unpack_queries(mine_ref[:, pl.ds(start, CHUNK), :])


def kv_block(kv_ref, j, count):
    return kv_ref[pl.ds(j * count, count), :TOK].reshape(count * TOK, LANES)


def fill_values(kv_ref, va_ref):
    @pl.when(pl.program_id(0) == 0)
    def _():
        for j in range(GROUP):
            kv = kv_ref[j, :TOK]
            va_ref[j] = jnp.where(low_half(TOK), jnp.ones_like(kv), kv)


def absorb(q, kv_ref, va_ref, top, acc):
    def scores(j):
        block = kv_block(kv_ref, j, BLOCK_FRAMES)
        return lax.dot_general(q, block, NT, preferred_element_type=F32)

    blocks = GROUP // BLOCK_FRAMES
    s = scores(0)
    for j in range(blocks):
        ahead = scores(j + 1) if j + 1 < blocks else None
        newtop = jnp.max(s, axis=-1, keepdims=True) * LOG2E
        if top is not None:
            newtop = jnp.maximum(top, newtop)
        p = jnp.exp2(s * LOG2E - newtop).astype(BF16)
        pv = jnp.dot(p, kv_block(va_ref, j, BLOCK_FRAMES), preferred_element_type=F32)
        acc = pv if top is None else acc * jnp.exp2(top - newtop) + pv
        top, s = newtop, ahead
    return top, acc


def own_kernel(first, mine_ref, *rest):
    state_ref, tick_ref, va_ref = rest[-3:]
    tick_ref[...] = jnp.zeros_like(tick_ref)
    fill_values(mine_ref, va_ref)
    q = load_queries(mine_ref, pl.program_id(0) + first)
    top, acc = absorb(q, mine_ref, va_ref, None, None)
    lane = lax.broadcasted_iota(jnp.int32, acc.shape, 1)
    state_ref[...] = jnp.where(lane == 1, top, acc)


def other_kernel(starts, mine_ref, other_ref, *rest):
    state_refs = rest[: len(starts)]
    o_ref, va_ref = rest[-2:]
    fill_values(other_ref, va_ref)
    chunk = pl.program_id(0) + starts[0]
    q = load_queries(mine_ref, chunk)
    state = state_refs[0][...]
    for start, ref in zip(starts[1:], state_refs[1:], strict=True):
        state = jnp.where(chunk >= start, ref[...], state)
    top, acc = absorb(q, other_ref, va_ref, state[:, 1:2], state)
    out = acc / acc[:, :1]
    packed = jnp.where(low_half(ROWS // 2), swap(out[: ROWS // 2]), out[ROWS // 2 :])
    o_ref[...] = packed.astype(BF16).reshape(o_ref.shape)


def picks_kernel(mine_ref, picks_ref, me_ref, *rest):
    o_ref, tick_ref, va_ref = rest[-3:]
    tick_ref[...] = jnp.zeros_like(tick_ref)
    fill_values(mine_ref, va_ref)
    step = pl.program_id(0)
    own = mine_ref[:, TOK : TOK + CHUNK, :]
    q = unpack_queries(jnp.where(step == 0, own, picks_ref[...]))
    top, acc = absorb(q, mine_ref, va_ref, None, None)
    sums = acc[:, :1]
    mean = acc / sums
    level = top + jnp.log2(sums)
    part0 = level.astype(BF16).astype(F32)
    part1 = (level - part0).astype(BF16).astype(F32)
    part2 = level - part0 - part1
    lane = lax.broadcasted_iota(jnp.int32, acc.shape, 1)
    low = jnp.where(lane == 0, part0, jnp.where(lane == 1, part1, part2))
    out = jnp.where(lane < HDIM, low, mean).astype(BF16).reshape(2, GROUP, CHUNK, LANES)
    side = me_ref[0] & 1
    side = jnp.where(step == 0, side, 1 - side)
    for half in range(2):
        o_ref[:, side, half * CHUNK : (half + 1) * CHUNK] = out[half]


VMEM = pl.BlockSpec(memory_space=pltpu.VMEM)
SMEM = pl.BlockSpec(memory_space=pltpu.SMEM)


def attend_settings(chunks):
    pairs = chunks * ROWS * GROUP * TOK
    return dict(
        grid=(chunks,),
        scratch_shapes=[pltpu.VMEM((GROUP, TOK, LANES), BF16)],
        compiler_params=pltpu.CompilerParams(vmem_limit_bytes=20 << 20),
        cost_estimate=pl.CostEstimate(
            flops=2 * pairs * LANES * 4, bytes_accessed=1 << 20, transcendentals=pairs
        ),
    )


HBM = pl.BlockSpec(memory_space=pltpu.HBM)
TICK = jax.ShapeDtypeStruct((8, LANES), F32)


def attend_own(mine, first, last, after=()):
    return pl.pallas_call(
        functools.partial(own_kernel, first),
        in_specs=[VMEM] * (1 + len(after)),
        out_specs=[pl.BlockSpec((ROWS, LANES), lambda i: (i, 0)), VMEM],
        out_shape=[jax.ShapeDtypeStruct(((last - first) * ROWS, LANES), F32), TICK],
        name=f"attend_own_{first}",
        **attend_settings(last - first),
    )(mine, *after)


def attend_picks(mine, picks, me, after):
    return pl.pallas_call(
        picks_kernel,
        in_specs=[VMEM, VMEM, SMEM] + [VMEM] * len(after),
        out_specs=[pl.BlockSpec((GROUP, 2, QMAX, LANES), lambda i: (0, 0, 0, 0)), VMEM],
        out_shape=[jax.ShapeDtypeStruct((GROUP, 2, QMAX, LANES), BF16), TICK],
        name="attend_picks",
        **attend_settings(2),
    )(mine, picks, me, *after)


def attend_other(mine, other, states, after=()):
    counts = [state.shape[0] // ROWS for state in states]
    chunks = sum(counts)
    starts = [CHUNKS - sum(counts[i:]) for i in range(len(counts))]

    def state_spec(start, count):
        shift = start - starts[0]
        return pl.BlockSpec((ROWS, LANES), lambda i: (jnp.clip(i - shift, 0, count - 1), 0))

    return pl.pallas_call(
        functools.partial(other_kernel, starts),
        in_specs=[VMEM, VMEM]
        + [state_spec(*pair) for pair in zip(starts, counts, strict=True)]
        + [VMEM] * len(after),
        out_specs=pl.BlockSpec((GROUP, CHUNK, LANES), lambda i: (0, i, 0)),
        out_shape=jax.ShapeDtypeStruct((GROUP, chunks * CHUNK, LANES), BF16),
        name="attend_other",
        **attend_settings(chunks),
    )(mine, other, *states, *after)


def join_heads(even_odd):
    top, bottom = [], []
    for even, odd in even_odd:
        low = low_half(even.shape[0])
        top.append(jnp.where(low, even, swap(odd)).astype(BF16))
        bottom.append(jnp.where(low, swap(even), odd).astype(BF16))
    return jnp.concatenate(top, axis=1), jnp.concatenate(bottom, axis=1)


def level_of(part):
    return part[:, 0:1] + part[:, 1:2] + part[:, 2:3]


def rows_kernel(part_ref, w_hbm, x_ref, place_ref, slots_ref, counts_ref, owner_ref, me_ref, *rest):
    send_hbm, att_ref, w_ref, rows_ref, sems = rest[-5:]
    load_w = pltpu.make_async_copy(w_hbm, w_ref, sems.at[0])
    load_w.start()
    heads = []
    for h in range(HEADS):
        a, b = part_ref[2 * h].astype(F32), part_ref[2 * h + 1].astype(F32)
        la, lb = level_of(a), level_of(b)
        most = jnp.maximum(la, lb)
        wa, wb = jnp.exp2(la - most), jnp.exp2(lb - most)
        heads.append((a * wa + b * wb) / (wa + wb))
    att = jnp.concatenate(
        [
            jnp.where(low_half(QMAX), swap(heads[2 * i]), heads[2 * i + 1]).astype(BF16)
            for i in range(HEADS // 2)
        ],
        axis=1,
    )
    att_ref[...] = att
    gap = jnp.zeros((TOK // 2 - CHUNK, D), BF16)
    placed = jnp.concatenate([att[:CHUNK], gap, att[CHUNK:], gap], axis=0)
    token_slot = jnp.where(slot_of_token(slots_ref[...]), 1.0, 0.0).astype(BF16)
    where = lax.dot_general(token_slot, place_ref[...], TN, preferred_element_type=F32).astype(BF16)
    chosen = jnp.dot(where, placed, preferred_element_type=F32).astype(BF16)
    x = lax.dot_general(token_slot, x_ref[...], TN, preferred_element_type=F32)
    load_w.wait()
    rows = (x + jnp.dot(chosen, w_ref[...], preferred_element_type=F32)).astype(BF16)
    me = me_ref[0]
    slot = lax.broadcasted_iota(jnp.int32, rows.shape, 0)
    rows_ref[...] = jnp.where(slot < counts_ref[me], rows, jnp.zeros_like(rows))
    put = pltpu.make_async_copy(rows_ref, send_hbm.at[owner_ref[me]], sems.at[1])
    put.start()
    put.wait()


def track_rows(parts, w_out, x, place, slots, counts, owner, me, after):
    return pl.pallas_call(
        rows_kernel,
        in_specs=[VMEM, HBM] + [VMEM] * 3 + [SMEM] * 3 + [HBM] * len(after),
        out_specs=[HBM, VMEM],
        scratch_shapes=[
            pltpu.VMEM((D, D), BF16),
            pltpu.VMEM((QMAX, D), BF16),
            pltpu.SemaphoreType.DMA((2,)),
        ],
        out_shape=[
            jax.ShapeDtypeStruct((FRAMES, QMAX, D), BF16),
            jax.ShapeDtypeStruct((QMAX, D), BF16),
        ],
        compiler_params=pltpu.CompilerParams(vmem_limit_bytes=58 << 20),
        cost_estimate=pl.CostEstimate(flops=2 << 30, bytes_accessed=4 << 20, transcendentals=0),
        name="track_rows",
    )(parts, w_out, x, place, slots, counts, owner, me, *after)


def finish_kernel(
    att1_ref, at2_ref, place_ref, owner_ref, me_ref, rows_hbm, x_hbm, w_hbm, mixed_ref, corr_ref, x_ref, w_ref, rows_ref, sems
):
    load_rows = pltpu.make_async_copy(rows_hbm, rows_ref, sems.at[2])

    @pl.when(pl.program_id(0) == 0)
    def _():
        load_w = pltpu.make_async_copy(w_hbm, w_ref, sems.at[0])
        load_x = pltpu.make_async_copy(x_hbm, x_ref, sems.at[1])
        load_w.start()
        load_x.start()
        load_rows.start()
        pairs = [
            (at2_ref[2 * i].astype(F32), at2_ref[2 * i + 1].astype(F32)) for i in range(HEADS // 2)
        ]
        top, bottom = join_heads(pairs)
        placed = jnp.concatenate([att1_ref[:CHUNK], top, att1_ref[CHUNK:], bottom], axis=0)
        att = jnp.dot(place_ref[...], placed, preferred_element_type=F32).astype(BF16)
        load_x.wait()
        load_w.wait()
        mixed_ref[...] = (
            x_ref[...].astype(F32) + jnp.dot(att, w_ref[...], preferred_element_type=F32)
        ).astype(BF16)
        load_rows.wait()

    step = corr_ref.shape[1]
    first = pl.program_id(0) * step
    rows = rows_ref[pl.ds(first, step)].reshape(-1, D)
    corr = lax.dot_general(rows, mixed_ref[...], NT, preferred_element_type=F32)
    corr = (corr * (1.0 / D**0.5)).reshape(step, QMAX, TOK)
    for i in range(step):
        owned = owner_ref[first + i] == me_ref[0]
        corr_ref[0, i] = jnp.where(owned, corr[i], jnp.zeros_like(corr[i]))


def finish(att1, att2, x, w_out, place, owner, me, arrived):
    step = 8
    return pl.pallas_call(
        finish_kernel,
        grid=(FRAMES // step,),
        in_specs=[
            pl.BlockSpec(att1.shape, lambda i: (0, 0)),
            pl.BlockSpec(att2.shape, lambda i: (0, 0, 0)),
            pl.BlockSpec(place.shape, lambda i: (0, 0)),
        ]
        + [SMEM] * 2
        + [HBM] * 3,
        out_specs=[
            pl.BlockSpec((TOK, D), lambda i: (0, 0)),
            pl.BlockSpec((1, step, QMAX, TOK), lambda i: (0, i, 0, 0)),
        ],
        out_shape=[
            jax.ShapeDtypeStruct((TOK, D), BF16),
            jax.ShapeDtypeStruct((1, FRAMES, QMAX, TOK), F32),
        ],
        scratch_shapes=[
            pltpu.VMEM((TOK, D), BF16),
            pltpu.VMEM((D, D), BF16),
            pltpu.VMEM((FRAMES, QMAX, D), BF16),
            pltpu.SemaphoreType.DMA((3,)),
        ],
        compiler_params=pltpu.CompilerParams(vmem_limit_bytes=58 << 20),
        name="finish",
    )(att1, att2, place, owner, me, arrived, x, w_out)


def per_device(features, norm_gain, w_qkv, w_out, counts, query_index, owner):
    groups = [[2 * i + side for i in range(GROUP)] for side in range(2)]
    swap_sides = [(d, d ^ 1) for d in range(FRAMES)]
    me = lax.axis_index("frame").astype(jnp.int32).reshape(1)
    packed, place = project(features, norm_gain, query_index, w_qkv)
    mine = lax.all_to_all(packed, "frame", 0, 0, tiled=True, axis_index_groups=groups)
    picks = lax.ppermute(mine[:, TOK : TOK + CHUNK], "frame", swap_sides)
    other = lax.ppermute(mine[:, :TOK], "frame", swap_sides)
    state1, tick = attend_own(mine, 1, 3)
    parts, tick = attend_picks(mine, picks, me, [tick])
    parts_here = lax.all_to_all(
        parts.reshape(FRAMES, QMAX, LANES), "frame", 0, 0, tiled=True
    )
    state2, _ = attend_own(mine, 3, SPLIT, [tick])
    send, att1 = track_rows(
        parts_here, w_out, features, place, query_index, counts, owner, me, [state2]
    )
    arrived = lax.all_to_all(send, "frame", 0, 0, tiled=True)
    state3, _ = attend_own(mine, SPLIT, CHUNKS, [att1])
    rest = attend_other(mine, other, [state1, state2, state3])
    rest, arrived = lax.optimization_barrier((rest, arrived))
    att2 = lax.all_to_all(rest, "frame", 0, 0, tiled=True, axis_index_groups=groups)
    return tuple(finish(att1, att2, features, w_out, place, owner, me, arrived))


def solution(mesh):
    rows = P(("scene", "frame"), None)
    in_specs = (rows, P(), P(), P(), P("scene"), rows, P("scene"))
    out_specs = (rows, P(("scene", "frame"), None, None, None))
    return jax.shard_map(
        per_device, mesh=mesh, in_specs=in_specs, out_specs=out_specs, check_vma=False
    )
```

```python
import functools

import jax
import jax.numpy as jnp
from jax import lax
from jax.experimental import pallas as pl
from jax.experimental.pallas import tpu as pltpu
from jax.sharding import PartitionSpec as P

D = 1024
HEADS = 16
HDIM = 64
TOK = 256
FRAMES = 32
QMAX = 32
LANES = 128
LOG2E = 1.4426950408889634
NT = (((1,), (1,)), ((), ()))
TN = (((0,), (0,)), ((), ()))
CHUNK = 16
F32 = jnp.float32
BF16 = jnp.bfloat16


def low_half(rows):
    return lax.broadcasted_iota(jnp.int32, (rows, LANES), 1) < HDIM


def swap(x):
    return pltpu.roll(x, HDIM, 1)


def slot_of_token(slots):
    return lax.broadcasted_iota(jnp.int32, (TOK, QMAX), 0) == slots


def arrange(slots):
    picked = jnp.max(jnp.where(slot_of_token(slots), 1.0, 0.0), axis=1, keepdims=True)
    row = lax.broadcasted_iota(jnp.int32, (TOK, TOK), 0)
    col = lax.broadcasted_iota(jnp.int32, (TOK, TOK), 1)
    wide = jnp.broadcast_to(picked, (TOK, LANES)).astype(BF16)
    before = jnp.dot(jnp.where(col < row, 1.0, 0.0).astype(BF16), wide, preferred_element_type=F32)
    before = before[:, :1].astype(jnp.int32)
    total = jnp.sum(picked).astype(jnp.int32)
    token = lax.broadcasted_iota(jnp.int32, (TOK, 1), 0)
    rank = jnp.where(picked > 0.5, before, total + token - before)
    within = rank & 31
    place = (rank >> 5) * CHUNK + (within & 15) + jnp.where(within >= CHUNK, TOK // 2, 0)
    return jnp.where(place == col, 1.0, 0.0).astype(BF16)


def project_kernel(x_ref, g_ref, slots_ref, wq_ref, wk_ref, wv_ref, o_ref, place_ref, n_ref):
    @pl.when(pl.program_id(0) == 0)
    def _():
        place = arrange(slots_ref[...])
        place_ref[...] = place
        xf = x_ref[...].astype(F32)
        mean = jnp.mean(xf, axis=-1, keepdims=True)
        cen = xf - mean
        var = jnp.mean(cen * cen, axis=-1, keepdims=True)
        normed = (cen * lax.rsqrt(var + 1e-05) * g_ref[...]).astype(BF16)
        n_ref[...] = lax.dot_general(place, normed, TN, preferred_element_type=F32).astype(BF16)

    n = n_ref[...]
    q = jnp.dot(n, wq_ref[...], preferred_element_type=F32) * (1.0 / HDIM**0.5)
    k = jnp.dot(n, wk_ref[...], preferred_element_type=F32)
    v = jnp.dot(n, wv_ref[...], preferred_element_type=F32)
    half = TOK // 2
    low = low_half(TOK)
    lowh = low_half(half)
    for c in range(wq_ref.shape[1] // LANES):
        cols = slice(c * LANES, (c + 1) * LANES)
        kp, vp = k[:, cols], v[:, cols]
        qa, qb = q[:half, cols], q[half:, cols]
        o_ref[2 * c, :TOK] = jnp.where(low, kp, swap(vp)).astype(BF16)
        o_ref[2 * c + 1, :TOK] = jnp.where(low, swap(kp), vp).astype(BF16)
        o_ref[2 * c, TOK:] = jnp.where(lowh, qa, swap(qb)).astype(BF16)
        o_ref[2 * c + 1, TOK:] = jnp.where(lowh, swap(qa), qb).astype(BF16)


def project(x, gain, slots, w_qkv):
    steps = 4
    width = D // steps
    return pl.pallas_call(
        project_kernel,
        grid=(steps,),
        in_specs=[
            pl.BlockSpec((TOK, D), lambda i: (0, 0)),
            pl.BlockSpec((1, D), lambda i: (0, 0)),
            pl.BlockSpec((1, QMAX), lambda i: (0, 0)),
            pl.BlockSpec((D, width), lambda i: (0, i)),
            pl.BlockSpec((D, width), lambda i: (0, i + steps)),
            pl.BlockSpec((D, width), lambda i: (0, i + 2 * steps)),
        ],
        out_specs=[
            pl.BlockSpec((HEADS // steps, TOK + TOK // 2, LANES), lambda i: (i, 0, 0)),
            pl.BlockSpec((TOK, TOK), lambda i: (0, 0)),
        ],
        out_shape=[
            jax.ShapeDtypeStruct((HEADS, TOK + TOK // 2, LANES), BF16),
            jax.ShapeDtypeStruct((TOK, TOK), BF16),
        ],
        scratch_shapes=[pltpu.VMEM((TOK, D), BF16)],
        compiler_params=pltpu.CompilerParams(vmem_limit_bytes=60 << 20),
        name="project",
    )(x, gain.reshape(1, D), slots, w_qkv, w_qkv, w_qkv)


BLOCK_FRAMES = 4
GROUP = FRAMES // 2
CHUNKS = TOK // (2 * CHUNK)
ROWS = GROUP * 2 * CHUNK
SPLIT = 6


def unpack_queries(packed):
    packed = packed.reshape(GROUP * CHUNK, LANES).astype(F32)
    low = low_half(packed.shape[0])
    zero = jnp.zeros_like(packed)
    both = [jnp.where(low, packed, zero), jnp.where(low, swap(packed), zero)]
    return jnp.concatenate(both, axis=0).astype(BF16)


def load_queries(mine_ref, chunk):
    start = pl.multiple_of(TOK + chunk * CHUNK, CHUNK)
    return unpack_queries(mine_ref[:, pl.ds(start, CHUNK), :])


def kv_block(kv_ref, j, count):
    return kv_ref[pl.ds(j * count, count), :TOK].reshape(count * TOK, LANES)


def fill_values(kv_ref, va_ref):
    @pl.when(pl.program_id(0) == 0)
    def _():
        for j in range(GROUP):
            kv = kv_ref[j, :TOK]
            va_ref[j] = jnp.where(low_half(TOK), jnp.ones_like(kv), kv)


def absorb(q, kv_ref, va_ref, top, acc):
    def scores(j):
        block = kv_block(kv_ref, j, BLOCK_FRAMES)
        return lax.dot_general(q, block, NT, preferred_element_type=F32)

    blocks = GROUP // BLOCK_FRAMES
    s = scores(0)
    for j in range(blocks):
        ahead = scores(j + 1) if j + 1 < blocks else None
        newtop = jnp.max(s, axis=-1, keepdims=True) * LOG2E
        if top is not None:
            newtop = jnp.maximum(top, newtop)
        p = jnp.exp2(s * LOG2E - newtop).astype(BF16)
        pv = jnp.dot(p, kv_block(va_ref, j, BLOCK_FRAMES), preferred_element_type=F32)
        acc = pv if top is None else acc * jnp.exp2(top - newtop) + pv
        top, s = newtop, ahead
    return top, acc


def own_kernel(first, mine_ref, *rest):
    state_ref, tick_ref, va_ref = rest[-3:]
    tick_ref[...] = jnp.zeros_like(tick_ref)
    fill_values(mine_ref, va_ref)
    q = load_queries(mine_ref, pl.program_id(0) + first)
    top, acc = absorb(q, mine_ref, va_ref, None, None)
    lane = lax.broadcasted_iota(jnp.int32, acc.shape, 1)
    state_ref[...] = jnp.where(lane == 1, top, acc)


def other_kernel(starts, mine_ref, other_ref, *rest):
    state_refs = rest[: len(starts)]
    o_ref, va_ref = rest[-2:]
    fill_values(other_ref, va_ref)
    chunk = pl.program_id(0) + starts[0]
    q = load_queries(mine_ref, chunk)
    state = state_refs[0][...]
    for start, ref in zip(starts[1:], state_refs[1:], strict=True):
        state = jnp.where(chunk >= start, ref[...], state)
    top, acc = absorb(q, other_ref, va_ref, state[:, 1:2], state)
    out = acc / acc[:, :1]
    packed = jnp.where(low_half(ROWS // 2), swap(out[: ROWS // 2]), out[ROWS // 2 :])
    o_ref[...] = packed.astype(BF16).reshape(o_ref.shape)


def picks_kernel(mine_ref, picks_ref, me_ref, *rest):
    o_ref, tick_ref, va_ref = rest[-3:]
    tick_ref[...] = jnp.zeros_like(tick_ref)
    fill_values(mine_ref, va_ref)
    step = pl.program_id(0)
    own = mine_ref[:, TOK : TOK + CHUNK, :]
    q = unpack_queries(jnp.where(step == 0, own, picks_ref[...]))
    top, acc = absorb(q, mine_ref, va_ref, None, None)
    sums = acc[:, :1]
    mean = acc / sums
    level = top + jnp.log2(sums)
    part0 = level.astype(BF16).astype(F32)
    part1 = (level - part0).astype(BF16).astype(F32)
    part2 = level - part0 - part1
    lane = lax.broadcasted_iota(jnp.int32, acc.shape, 1)
    low = jnp.where(lane == 0, part0, jnp.where(lane == 1, part1, part2))
    out = jnp.where(lane < HDIM, low, mean).astype(BF16).reshape(2, GROUP, CHUNK, LANES)
    side = me_ref[0] & 1
    side = jnp.where(step == 0, side, 1 - side)
    for half in range(2):
        o_ref[:, side, half * CHUNK : (half + 1) * CHUNK] = out[half]


VMEM = pl.BlockSpec(memory_space=pltpu.VMEM)
SMEM = pl.BlockSpec(memory_space=pltpu.SMEM)


def attend_settings(chunks):
    pairs = chunks * ROWS * GROUP * TOK
    return dict(
        grid=(chunks,),
        scratch_shapes=[pltpu.VMEM((GROUP, TOK, LANES), BF16)],
        compiler_params=pltpu.CompilerParams(vmem_limit_bytes=20 << 20),
        cost_estimate=pl.CostEstimate(
            flops=2 * pairs * LANES * 4, bytes_accessed=1 << 20, transcendentals=pairs
        ),
    )


HBM = pl.BlockSpec(memory_space=pltpu.HBM)
TICK = jax.ShapeDtypeStruct((8, LANES), F32)


def attend_own(mine, first, last, after=()):
    return pl.pallas_call(
        functools.partial(own_kernel, first),
        in_specs=[VMEM] * (1 + len(after)),
        out_specs=[pl.BlockSpec((ROWS, LANES), lambda i: (i, 0)), VMEM],
        out_shape=[jax.ShapeDtypeStruct(((last - first) * ROWS, LANES), F32), TICK],
        name=f"attend_own_{first}",
        **attend_settings(last - first),
    )(mine, *after)


def attend_picks(mine, picks, me, after):
    return pl.pallas_call(
        picks_kernel,
        in_specs=[VMEM, VMEM, SMEM] + [VMEM] * len(after),
        out_specs=[pl.BlockSpec((GROUP, 2, QMAX, LANES), lambda i: (0, 0, 0, 0)), VMEM],
        out_shape=[jax.ShapeDtypeStruct((GROUP, 2, QMAX, LANES), BF16), TICK],
        name="attend_picks",
        **attend_settings(2),
    )(mine, picks, me, *after)


def attend_other(mine, other, states, after=()):
    counts = [state.shape[0] // ROWS for state in states]
    chunks = sum(counts)
    starts = [CHUNKS - sum(counts[i:]) for i in range(len(counts))]

    def state_spec(start, count):
        shift = start - starts[0]
        return pl.BlockSpec((ROWS, LANES), lambda i: (jnp.clip(i - shift, 0, count - 1), 0))

    return pl.pallas_call(
        functools.partial(other_kernel, starts),
        in_specs=[VMEM, VMEM]
        + [state_spec(*pair) for pair in zip(starts, counts, strict=True)]
        + [VMEM] * len(after),
        out_specs=pl.BlockSpec((GROUP, CHUNK, LANES), lambda i: (0, i, 0)),
        out_shape=jax.ShapeDtypeStruct((GROUP, chunks * CHUNK, LANES), BF16),
        name="attend_other",
        **attend_settings(chunks),
    )(mine, other, *states, *after)


def join_heads(even_odd):
    top, bottom = [], []
    for even, odd in even_odd:
        low = low_half(even.shape[0])
        top.append(jnp.where(low, even, swap(odd)).astype(BF16))
        bottom.append(jnp.where(low, swap(even), odd).astype(BF16))
    return jnp.concatenate(top, axis=1), jnp.concatenate(bottom, axis=1)


def level_of(part):
    return part[:, 0:1] + part[:, 1:2] + part[:, 2:3]


def rows_kernel(part_ref, w_hbm, x_ref, place_ref, slots_ref, counts_ref, owner_ref, me_ref, *rest):
    send_hbm, att_ref, w_ref, rows_ref, sems = rest[-5:]
    load_w = pltpu.make_async_copy(w_hbm, w_ref, sems.at[0])
    load_w.start()
    heads = []
    for h in range(HEADS):
        a, b = part_ref[2 * h].astype(F32), part_ref[2 * h + 1].astype(F32)
        la, lb = level_of(a), level_of(b)
        most = jnp.maximum(la, lb)
        wa, wb = jnp.exp2(la - most), jnp.exp2(lb - most)
        heads.append((a * wa + b * wb) / (wa + wb))
    att = jnp.concatenate(
        [
            jnp.where(low_half(QMAX), swap(heads[2 * i]), heads[2 * i + 1]).astype(BF16)
            for i in range(HEADS // 2)
        ],
        axis=1,
    )
    att_ref[...] = att
    gap = jnp.zeros((TOK // 2 - CHUNK, D), BF16)
    placed = jnp.concatenate([att[:CHUNK], gap, att[CHUNK:], gap], axis=0)
    token_slot = jnp.where(slot_of_token(slots_ref[...]), 1.0, 0.0).astype(BF16)
    where = lax.dot_general(token_slot, place_ref[...], TN, preferred_element_type=F32).astype(BF16)
    chosen = jnp.dot(where, placed, preferred_element_type=F32).astype(BF16)
    x = lax.dot_general(token_slot, x_ref[...], TN, preferred_element_type=F32)
    load_w.wait()
    rows = (x + jnp.dot(chosen, w_ref[...], preferred_element_type=F32)).astype(BF16)
    me = me_ref[0]
    slot = lax.broadcasted_iota(jnp.int32, rows.shape, 0)
    rows_ref[...] = jnp.where(slot < counts_ref[me], rows, jnp.zeros_like(rows))
    put = pltpu.make_async_copy(rows_ref, send_hbm.at[owner_ref[me]], sems.at[1])
    put.start()
    put.wait()


def track_rows(parts, w_out, x, place, slots, counts, owner, me, after):
    return pl.pallas_call(
        rows_kernel,
        in_specs=[VMEM, HBM] + [VMEM] * 3 + [SMEM] * 3 + [HBM] * len(after),
        out_specs=[HBM, VMEM],
        scratch_shapes=[
            pltpu.VMEM((D, D), BF16),
            pltpu.VMEM((QMAX, D), BF16),
            pltpu.SemaphoreType.DMA((2,)),
        ],
        out_shape=[
            jax.ShapeDtypeStruct((FRAMES, QMAX, D), BF16),
            jax.ShapeDtypeStruct((QMAX, D), BF16),
        ],
        compiler_params=pltpu.CompilerParams(vmem_limit_bytes=52 << 20),
        cost_estimate=pl.CostEstimate(flops=2 << 30, bytes_accessed=4 << 20, transcendentals=0),
        name="track_rows",
    )(parts, w_out, x, place, slots, counts, owner, me, *after)


def finish_kernel(
    att1_ref, at2_ref, place_ref, owner_ref, me_ref, rows_hbm, x_hbm, w_hbm, mixed_ref, corr_ref, x_ref, w_ref, rows_ref, sems
):
    load_rows = pltpu.make_async_copy(rows_hbm, rows_ref, sems.at[2])

    @pl.when(pl.program_id(0) == 0)
    def _():
        load_w = pltpu.make_async_copy(w_hbm, w_ref, sems.at[0])
        load_x = pltpu.make_async_copy(x_hbm, x_ref, sems.at[1])
        load_w.start()
        load_x.start()
        load_rows.start()
        pairs = [
            (at2_ref[2 * i].astype(F32), at2_ref[2 * i + 1].astype(F32)) for i in range(HEADS // 2)
        ]
        top, bottom = join_heads(pairs)
        placed = jnp.concatenate([att1_ref[:CHUNK], top, att1_ref[CHUNK:], bottom], axis=0)
        att = jnp.dot(place_ref[...], placed, preferred_element_type=F32).astype(BF16)
        load_x.wait()
        load_w.wait()
        mixed_ref[...] = (
            x_ref[...].astype(F32) + jnp.dot(att, w_ref[...], preferred_element_type=F32)
        ).astype(BF16)
        load_rows.wait()

    step = corr_ref.shape[1]
    first = pl.program_id(0) * step
    rows = rows_ref[pl.ds(first, step)].reshape(-1, D)
    corr = lax.dot_general(rows, mixed_ref[...], NT, preferred_element_type=F32)
    corr = (corr * (1.0 / D**0.5)).reshape(step, QMAX, TOK)
    for i in range(step):
        owned = owner_ref[first + i] == me_ref[0]
        corr_ref[0, i] = jnp.where(owned, corr[i], jnp.zeros_like(corr[i]))


def finish(att1, att2, x, w_out, place, owner, me, arrived):
    step = 8
    return pl.pallas_call(
        finish_kernel,
        grid=(FRAMES // step,),
        in_specs=[
            pl.BlockSpec(att1.shape, lambda i: (0, 0)),
            pl.BlockSpec(att2.shape, lambda i: (0, 0, 0)),
            pl.BlockSpec(place.shape, lambda i: (0, 0)),
        ]
        + [SMEM] * 2
        + [HBM] * 3,
        out_specs=[
            pl.BlockSpec((TOK, D), lambda i: (0, 0)),
            pl.BlockSpec((1, step, QMAX, TOK), lambda i: (0, i, 0, 0)),
        ],
        out_shape=[
            jax.ShapeDtypeStruct((TOK, D), BF16),
            jax.ShapeDtypeStruct((1, FRAMES, QMAX, TOK), F32),
        ],
        scratch_shapes=[
            pltpu.VMEM((TOK, D), BF16),
            pltpu.VMEM((D, D), BF16),
            pltpu.VMEM((FRAMES, QMAX, D), BF16),
            pltpu.SemaphoreType.DMA((3,)),
        ],
        compiler_params=pltpu.CompilerParams(vmem_limit_bytes=58 << 20),
        name="finish",
    )(att1, att2, place, owner, me, arrived, x, w_out)


def per_device(features, norm_gain, w_qkv, w_out, counts, query_index, owner):
    groups = [[2 * i + side for i in range(GROUP)] for side in range(2)]
    swap_sides = [(d, d ^ 1) for d in range(FRAMES)]
    me = lax.axis_index("frame").astype(jnp.int32).reshape(1)
    packed, place = project(features, norm_gain, query_index, w_qkv)
    mine = lax.all_to_all(packed, "frame", 0, 0, tiled=True, axis_index_groups=groups)
    picks = lax.ppermute(mine[:, TOK : TOK + CHUNK], "frame", swap_sides)
    other = lax.ppermute(mine[:, :TOK], "frame", swap_sides)
    state1, tick = attend_own(mine, 1, 2)
    parts, tick = attend_picks(mine, picks, me, [tick])
    parts_here = lax.all_to_all(
        parts.reshape(FRAMES, QMAX, LANES), "frame", 0, 0, tiled=True
    )
    state2, _ = attend_own(mine, 2, SPLIT, [tick])
    send, att1 = track_rows(
        parts_here, w_out, features, place, query_index, counts, owner, me, [state2]
    )
    arrived = lax.all_to_all(send, "frame", 0, 0, tiled=True)
    state3, _ = attend_own(mine, SPLIT, CHUNKS, [att1])
    rest = attend_other(mine, other, [state1, state2, state3])
    rest, arrived = lax.optimization_barrier((rest, arrived))
    att2 = lax.all_to_all(rest, "frame", 0, 0, tiled=True, axis_index_groups=groups)
    return tuple(finish(att1, att2, features, w_out, place, owner, me, arrived))


def solution(mesh):
    rows = P(("scene", "frame"), None)
    in_specs = (rows, P(), P(), P(), P("scene"), rows, P("scene"))
    out_specs = (rows, P(("scene", "frame"), None, None, None))
    return jax.shard_map(
        per_device, mesh=mesh, in_specs=in_specs, out_specs=out_specs, check_vma=False
    )
```

```python
import functools

import jax
import jax.numpy as jnp
from jax import lax
from jax.experimental import pallas as pl
from jax.experimental.pallas import tpu as pltpu
from jax.sharding import PartitionSpec as P

D = 1024
HEADS = 16
HDIM = 64
TOK = 256
FRAMES = 32
QMAX = 32
LANES = 128
LOG2E = 1.4426950408889634
NT = (((1,), (1,)), ((), ()))
TN = (((0,), (0,)), ((), ()))
CHUNK = 16
F32 = jnp.float32
BF16 = jnp.bfloat16


def low_half(rows):
    return lax.broadcasted_iota(jnp.int32, (rows, LANES), 1) < HDIM


def swap(x):
    return pltpu.roll(x, HDIM, 1)


def slot_of_token(slots):
    return lax.broadcasted_iota(jnp.int32, (TOK, QMAX), 0) == slots


def arrange(slots):
    picked = jnp.max(jnp.where(slot_of_token(slots), 1.0, 0.0), axis=1, keepdims=True)
    row = lax.broadcasted_iota(jnp.int32, (TOK, TOK), 0)
    col = lax.broadcasted_iota(jnp.int32, (TOK, TOK), 1)
    wide = jnp.broadcast_to(picked, (TOK, LANES)).astype(BF16)
    before = jnp.dot(jnp.where(col < row, 1.0, 0.0).astype(BF16), wide, preferred_element_type=F32)
    before = before[:, :1].astype(jnp.int32)
    total = jnp.sum(picked).astype(jnp.int32)
    token = lax.broadcasted_iota(jnp.int32, (TOK, 1), 0)
    rank = jnp.where(picked > 0.5, before, total + token - before)
    within = rank & 31
    place = (rank >> 5) * CHUNK + (within & 15) + jnp.where(within >= CHUNK, TOK // 2, 0)
    return jnp.where(place == col, 1.0, 0.0).astype(BF16)


def project_kernel(x_ref, g_ref, slots_ref, wq_ref, wk_ref, wv_ref, o_ref, place_ref, n_ref):
    @pl.when(pl.program_id(0) == 0)
    def _():
        place = arrange(slots_ref[...])
        place_ref[...] = place
        xf = x_ref[...].astype(F32)
        mean = jnp.mean(xf, axis=-1, keepdims=True)
        cen = xf - mean
        var = jnp.mean(cen * cen, axis=-1, keepdims=True)
        normed = (cen * lax.rsqrt(var + 1e-05) * g_ref[...]).astype(BF16)
        n_ref[...] = lax.dot_general(place, normed, TN, preferred_element_type=F32).astype(BF16)

    n = n_ref[...]
    q = jnp.dot(n, wq_ref[...], preferred_element_type=F32) * (1.0 / HDIM**0.5)
    k = jnp.dot(n, wk_ref[...], preferred_element_type=F32)
    v = jnp.dot(n, wv_ref[...], preferred_element_type=F32)
    half = TOK // 2
    low = low_half(TOK)
    lowh = low_half(half)
    for c in range(wq_ref.shape[1] // LANES):
        cols = slice(c * LANES, (c + 1) * LANES)
        kp, vp = k[:, cols], v[:, cols]
        qa, qb = q[:half, cols], q[half:, cols]
        o_ref[2 * c, :TOK] = jnp.where(low, kp, swap(vp)).astype(BF16)
        o_ref[2 * c + 1, :TOK] = jnp.where(low, swap(kp), vp).astype(BF16)
        o_ref[2 * c, TOK:] = jnp.where(lowh, qa, swap(qb)).astype(BF16)
        o_ref[2 * c + 1, TOK:] = jnp.where(lowh, swap(qa), qb).astype(BF16)


def project(x, gain, slots, w_qkv):
    steps = 4
    width = D // steps
    return pl.pallas_call(
        project_kernel,
        grid=(steps,),
        in_specs=[
            pl.BlockSpec((TOK, D), lambda i: (0, 0)),
            pl.BlockSpec((1, D), lambda i: (0, 0)),
            pl.BlockSpec((1, QMAX), lambda i: (0, 0)),
            pl.BlockSpec((D, width), lambda i: (0, i)),
            pl.BlockSpec((D, width), lambda i: (0, i + steps)),
            pl.BlockSpec((D, width), lambda i: (0, i + 2 * steps)),
        ],
        out_specs=[
            pl.BlockSpec((HEADS // steps, TOK + TOK // 2, LANES), lambda i: (i, 0, 0)),
            pl.BlockSpec((TOK, TOK), lambda i: (0, 0)),
        ],
        out_shape=[
            jax.ShapeDtypeStruct((HEADS, TOK + TOK // 2, LANES), BF16),
            jax.ShapeDtypeStruct((TOK, TOK), BF16),
        ],
        scratch_shapes=[pltpu.VMEM((TOK, D), BF16)],
        compiler_params=pltpu.CompilerParams(vmem_limit_bytes=60 << 20),
        name="project",
    )(x, gain.reshape(1, D), slots, w_qkv, w_qkv, w_qkv)


BLOCK_FRAMES = 4
GROUP = FRAMES // 2
CHUNKS = TOK // (2 * CHUNK)
ROWS = GROUP * 2 * CHUNK
SPLIT = 6


def unpack_queries(packed):
    packed = packed.reshape(GROUP * CHUNK, LANES).astype(F32)
    low = low_half(packed.shape[0])
    zero = jnp.zeros_like(packed)
    both = [jnp.where(low, packed, zero), jnp.where(low, swap(packed), zero)]
    return jnp.concatenate(both, axis=0).astype(BF16)


def load_queries(mine_ref, chunk):
    start = pl.multiple_of(TOK + chunk * CHUNK, CHUNK)
    return unpack_queries(mine_ref[:, pl.ds(start, CHUNK), :])


def kv_block(kv_ref, j, count):
    return kv_ref[pl.ds(j * count, count), :TOK].reshape(count * TOK, LANES)


def fill_values(kv_ref, va_ref):
    @pl.when(pl.program_id(0) == 0)
    def _():
        for j in range(GROUP):
            kv = kv_ref[j, :TOK]
            va_ref[j] = jnp.where(low_half(TOK), jnp.ones_like(kv), kv)


def absorb(q, kv_ref, va_ref, top, acc):
    def scores(j):
        block = kv_block(kv_ref, j, BLOCK_FRAMES)
        return lax.dot_general(q, block, NT, preferred_element_type=F32)

    blocks = GROUP // BLOCK_FRAMES
    s = scores(0)
    for j in range(blocks):
        ahead = scores(j + 1) if j + 1 < blocks else None
        newtop = jnp.max(s, axis=-1, keepdims=True) * LOG2E
        if top is not None:
            newtop = jnp.maximum(top, newtop)
        p = jnp.exp2(s * LOG2E - newtop).astype(BF16)
        pv = jnp.dot(p, kv_block(va_ref, j, BLOCK_FRAMES), preferred_element_type=F32)
        acc = pv if top is None else acc * jnp.exp2(top - newtop) + pv
        top, s = newtop, ahead
    return top, acc


def own_kernel(first, mine_ref, *rest):
    state_ref, tick_ref, va_ref = rest[-3:]
    tick_ref[...] = jnp.zeros_like(tick_ref)
    fill_values(mine_ref, va_ref)
    q = load_queries(mine_ref, pl.program_id(0) + first)
    top, acc = absorb(q, mine_ref, va_ref, None, None)
    lane = lax.broadcasted_iota(jnp.int32, acc.shape, 1)
    state_ref[...] = jnp.where(lane == 1, top, acc)


def other_kernel(starts, mine_ref, other_ref, *rest):
    state_refs = rest[: len(starts)]
    o_ref, va_ref = rest[-2:]
    fill_values(other_ref, va_ref)
    chunk = pl.program_id(0) + starts[0]
    q = load_queries(mine_ref, chunk)
    state = state_refs[0][...]
    for start, ref in zip(starts[1:], state_refs[1:], strict=True):
        state = jnp.where(chunk >= start, ref[...], state)
    top, acc = absorb(q, other_ref, va_ref, state[:, 1:2], state)
    out = acc / acc[:, :1]
    packed = jnp.where(low_half(ROWS // 2), swap(out[: ROWS // 2]), out[ROWS // 2 :])
    o_ref[...] = packed.astype(BF16).reshape(o_ref.shape)


def picks_kernel(mine_ref, picks_ref, me_ref, *rest):
    o_ref, tick_ref, va_ref = rest[-3:]
    tick_ref[...] = jnp.zeros_like(tick_ref)
    fill_values(mine_ref, va_ref)
    step = pl.program_id(0)
    own = mine_ref[:, TOK : TOK + CHUNK, :]
    q = unpack_queries(jnp.where(step == 0, own, picks_ref[...]))
    top, acc = absorb(q, mine_ref, va_ref, None, None)
    sums = acc[:, :1]
    mean = acc / sums
    level = top + jnp.log2(sums)
    part0 = level.astype(BF16).astype(F32)
    part1 = (level - part0).astype(BF16).astype(F32)
    part2 = level - part0 - part1
    lane = lax.broadcasted_iota(jnp.int32, acc.shape, 1)
    low = jnp.where(lane == 0, part0, jnp.where(lane == 1, part1, part2))
    out = jnp.where(lane < HDIM, low, mean).astype(BF16).reshape(2, GROUP, CHUNK, LANES)
    side = me_ref[0] & 1
    side = jnp.where(step == 0, side, 1 - side)
    for half in range(2):
        o_ref[:, side, half * CHUNK : (half + 1) * CHUNK] = out[half]


VMEM = pl.BlockSpec(memory_space=pltpu.VMEM)
SMEM = pl.BlockSpec(memory_space=pltpu.SMEM)


def attend_settings(chunks):
    pairs = chunks * ROWS * GROUP * TOK
    return dict(
        grid=(chunks,),
        scratch_shapes=[pltpu.VMEM((GROUP, TOK, LANES), BF16)],
        compiler_params=pltpu.CompilerParams(vmem_limit_bytes=20 << 20),
        cost_estimate=pl.CostEstimate(
            flops=2 * pairs * LANES * 4, bytes_accessed=1 << 20, transcendentals=pairs
        ),
    )


HBM = pl.BlockSpec(memory_space=pltpu.HBM)
TICK = jax.ShapeDtypeStruct((8, LANES), F32)


def attend_own(mine, first, last, after=()):
    return pl.pallas_call(
        functools.partial(own_kernel, first),
        in_specs=[VMEM] * (1 + len(after)),
        out_specs=[pl.BlockSpec((ROWS, LANES), lambda i: (i, 0)), VMEM],
        out_shape=[jax.ShapeDtypeStruct(((last - first) * ROWS, LANES), F32), TICK],
        name=f"attend_own_{first}",
        **attend_settings(last - first),
    )(mine, *after)


def attend_picks(mine, picks, me, after):
    return pl.pallas_call(
        picks_kernel,
        in_specs=[VMEM, VMEM, SMEM] + [VMEM] * len(after),
        out_specs=[pl.BlockSpec((GROUP, 2, QMAX, LANES), lambda i: (0, 0, 0, 0)), VMEM],
        out_shape=[jax.ShapeDtypeStruct((GROUP, 2, QMAX, LANES), BF16), TICK],
        name="attend_picks",
        **attend_settings(2),
    )(mine, picks, me, *after)


def attend_other(mine, other, states, after=()):
    counts = [state.shape[0] // ROWS for state in states]
    chunks = sum(counts)
    starts = [CHUNKS - sum(counts[i:]) for i in range(len(counts))]

    def state_spec(start, count):
        shift = start - starts[0]
        return pl.BlockSpec((ROWS, LANES), lambda i: (jnp.clip(i - shift, 0, count - 1), 0))

    return pl.pallas_call(
        functools.partial(other_kernel, starts),
        in_specs=[VMEM, VMEM]
        + [state_spec(*pair) for pair in zip(starts, counts, strict=True)]
        + [VMEM] * len(after),
        out_specs=pl.BlockSpec((GROUP, CHUNK, LANES), lambda i: (0, i, 0)),
        out_shape=jax.ShapeDtypeStruct((GROUP, chunks * CHUNK, LANES), BF16),
        name="attend_other",
        **attend_settings(chunks),
    )(mine, other, *states, *after)


def join_heads(even_odd):
    top, bottom = [], []
    for even, odd in even_odd:
        low = low_half(even.shape[0])
        top.append(jnp.where(low, even, swap(odd)).astype(BF16))
        bottom.append(jnp.where(low, swap(even), odd).astype(BF16))
    return jnp.concatenate(top, axis=1), jnp.concatenate(bottom, axis=1)


def level_of(part):
    return part[:, 0:1] + part[:, 1:2] + part[:, 2:3]


def rows_kernel(part_ref, w_hbm, x_ref, place_ref, slots_ref, counts_ref, owner_ref, me_ref, *rest):
    send_hbm, att_ref, w_ref, rows_ref, sems = rest[-5:]
    load_w = pltpu.make_async_copy(w_hbm, w_ref, sems.at[0])
    load_w.start()
    heads = []
    for h in range(HEADS):
        a, b = part_ref[2 * h].astype(F32), part_ref[2 * h + 1].astype(F32)
        la, lb = level_of(a), level_of(b)
        most = jnp.maximum(la, lb)
        wa, wb = jnp.exp2(la - most), jnp.exp2(lb - most)
        heads.append((a * wa + b * wb) / (wa + wb))
    att = jnp.concatenate(
        [
            jnp.where(low_half(QMAX), swap(heads[2 * i]), heads[2 * i + 1]).astype(BF16)
            for i in range(HEADS // 2)
        ],
        axis=1,
    )
    att_ref[...] = att
    gap = jnp.zeros((TOK // 2 - CHUNK, D), BF16)
    placed = jnp.concatenate([att[:CHUNK], gap, att[CHUNK:], gap], axis=0)
    token_slot = jnp.where(slot_of_token(slots_ref[...]), 1.0, 0.0).astype(BF16)
    where = lax.dot_general(token_slot, place_ref[...], TN, preferred_element_type=F32).astype(BF16)
    chosen = jnp.dot(where, placed, preferred_element_type=F32).astype(BF16)
    x = lax.dot_general(token_slot, x_ref[...], TN, preferred_element_type=F32)
    load_w.wait()
    rows = (x + jnp.dot(chosen, w_ref[...], preferred_element_type=F32)).astype(BF16)
    me = me_ref[0]
    slot = lax.broadcasted_iota(jnp.int32, rows.shape, 0)
    rows_ref[...] = jnp.where(slot < counts_ref[me], rows, jnp.zeros_like(rows))
    put = pltpu.make_async_copy(rows_ref, send_hbm.at[owner_ref[me]], sems.at[1])
    put.start()
    put.wait()


def track_rows(parts, w_out, x, place, slots, counts, owner, me, after):
    return pl.pallas_call(
        rows_kernel,
        in_specs=[VMEM, HBM] + [VMEM] * 3 + [SMEM] * 3 + [HBM] * len(after),
        out_specs=[HBM, VMEM],
        scratch_shapes=[
            pltpu.VMEM((D, D), BF16),
            pltpu.VMEM((QMAX, D), BF16),
            pltpu.SemaphoreType.DMA((2,)),
        ],
        out_shape=[
            jax.ShapeDtypeStruct((FRAMES, QMAX, D), BF16),
            jax.ShapeDtypeStruct((QMAX, D), BF16),
        ],
        compiler_params=pltpu.CompilerParams(vmem_limit_bytes=52 << 20),
        cost_estimate=pl.CostEstimate(flops=2 << 30, bytes_accessed=4 << 20, transcendentals=0),
        name="track_rows",
    )(parts, w_out, x, place, slots, counts, owner, me, *after)


def finish_kernel(
    owner_ref, me_ref, att1_hbm, at2_hbm, place_hbm, w_hbm, x_hbm, rows_hbm, mixed_ref, corr_ref, *scratch
):
    att1_ref, at2_ref, place_ref, w_ref, x_ref, rows_ref, sems = scratch

    @pl.when(pl.program_id(0) == 0)
    def _():
        sources = (at2_hbm, att1_hbm, place_hbm, w_hbm, x_hbm, rows_hbm)
        targets = (at2_ref, att1_ref, place_ref, w_ref, x_ref, rows_ref)
        loads = [
            pltpu.make_async_copy(source, target, sems.at[n])
            for n, (source, target) in enumerate(zip(sources, targets, strict=True))
        ]
        for load in loads:
            load.start()
        loads[0].wait()
        pairs = [
            (at2_ref[2 * i].astype(F32), at2_ref[2 * i + 1].astype(F32)) for i in range(HEADS // 2)
        ]
        top, bottom = join_heads(pairs)
        loads[1].wait()
        loads[2].wait()
        placed = jnp.concatenate([att1_ref[:CHUNK], top, att1_ref[CHUNK:], bottom], axis=0)
        att = jnp.dot(place_ref[...], placed, preferred_element_type=F32).astype(BF16)
        loads[3].wait()
        loads[4].wait()
        mixed_ref[...] = (
            x_ref[...].astype(F32) + jnp.dot(att, w_ref[...], preferred_element_type=F32)
        ).astype(BF16)
        loads[5].wait()

    step = corr_ref.shape[1]
    first = pl.program_id(0) * step
    rows = rows_ref[pl.ds(first, step)].reshape(-1, D)
    corr = lax.dot_general(rows, mixed_ref[...], NT, preferred_element_type=F32)
    corr = (corr * (1.0 / D**0.5)).reshape(step, QMAX, TOK)
    for i in range(step):
        owned = owner_ref[first + i] == me_ref[0]
        corr_ref[0, i] = jnp.where(owned, corr[i], jnp.zeros_like(corr[i]))


def finish(att1, att2, x, w_out, place, owner, me, arrived):
    step = 16
    return pl.pallas_call(
        finish_kernel,
        grid=(FRAMES // step,),
        in_specs=[SMEM] * 2 + [HBM] * 6,
        out_specs=[
            pl.BlockSpec((TOK, D), lambda i: (0, 0)),
            pl.BlockSpec((1, step, QMAX, TOK), lambda i: (0, i, 0, 0)),
        ],
        out_shape=[
            jax.ShapeDtypeStruct((TOK, D), BF16),
            jax.ShapeDtypeStruct((1, FRAMES, QMAX, TOK), F32),
        ],
        scratch_shapes=[
            pltpu.VMEM(array.shape, array.dtype) for array in (att1, att2, place, w_out, x, arrived)
        ]
        + [pltpu.SemaphoreType.DMA((6,))],
        compiler_params=pltpu.CompilerParams(vmem_limit_bytes=58 << 20),
        name="finish",
    )(owner, me, att1, att2, place, w_out, x, arrived)


def per_device(features, norm_gain, w_qkv, w_out, counts, query_index, owner):
    groups = [[2 * i + side for i in range(GROUP)] for side in range(2)]
    swap_sides = [(d, d ^ 1) for d in range(FRAMES)]
    me = lax.axis_index("frame").astype(jnp.int32).reshape(1)
    packed, place = project(features, norm_gain, query_index, w_qkv)
    mine = lax.all_to_all(packed, "frame", 0, 0, tiled=True, axis_index_groups=groups)
    picks = lax.ppermute(mine[:, TOK : TOK + CHUNK], "frame", swap_sides)
    other = lax.ppermute(mine[:, :TOK], "frame", swap_sides)
    state1, tick = attend_own(mine, 1, 2)
    parts, tick = attend_picks(mine, picks, me, [tick])
    parts_here = lax.all_to_all(
        parts.reshape(FRAMES, QMAX, LANES), "frame", 0, 0, tiled=True
    )
    state2, _ = attend_own(mine, 2, SPLIT, [tick])
    send, att1 = track_rows(
        parts_here, w_out, features, place, query_index, counts, owner, me, [state2]
    )
    arrived = lax.all_to_all(send, "frame", 0, 0, tiled=True)
    state3, _ = attend_own(mine, SPLIT, CHUNKS, [att1])
    rest = attend_other(mine, other, [state1, state2, state3])
    rest, arrived = lax.optimization_barrier((rest, arrived))
    att2 = lax.all_to_all(rest, "frame", 0, 0, tiled=True, axis_index_groups=groups)
    return tuple(finish(att1, att2, features, w_out, place, owner, me, arrived))


def solution(mesh):
    rows = P(("scene", "frame"), None)
    in_specs = (rows, P(), P(), P(), P("scene"), rows, P("scene"))
    out_specs = (rows, P(("scene", "frame"), None, None, None))
    return jax.shard_map(
        per_device, mesh=mesh, in_specs=in_specs, out_specs=out_specs, check_vma=False
    )
```

```python
import functools

import jax
import jax.numpy as jnp
from jax import lax
from jax.experimental import pallas as pl
from jax.experimental.pallas import tpu as pltpu
from jax.sharding import PartitionSpec as P

D = 1024
HEADS = 16
HDIM = 64
TOK = 256
FRAMES = 32
QMAX = 32
LANES = 128
LOG2E = 1.4426950408889634
NT = (((1,), (1,)), ((), ()))
TN = (((0,), (0,)), ((), ()))
CHUNK = 16
F32 = jnp.float32
BF16 = jnp.bfloat16


def low_half(rows):
    return lax.broadcasted_iota(jnp.int32, (rows, LANES), 1) < HDIM


def swap(x):
    return pltpu.roll(x, HDIM, 1)


def slot_of_token(slots):
    return lax.broadcasted_iota(jnp.int32, (TOK, QMAX), 0) == slots


def arrange(slots):
    picked = jnp.max(jnp.where(slot_of_token(slots), 1.0, 0.0), axis=1, keepdims=True)
    row = lax.broadcasted_iota(jnp.int32, (TOK, TOK), 0)
    col = lax.broadcasted_iota(jnp.int32, (TOK, TOK), 1)
    wide = jnp.broadcast_to(picked, (TOK, LANES)).astype(BF16)
    before = jnp.dot(jnp.where(col < row, 1.0, 0.0).astype(BF16), wide, preferred_element_type=F32)
    before = before[:, :1].astype(jnp.int32)
    total = jnp.sum(picked).astype(jnp.int32)
    token = lax.broadcasted_iota(jnp.int32, (TOK, 1), 0)
    rank = jnp.where(picked > 0.5, before, total + token - before)
    within = rank & 31
    place = (rank >> 5) * CHUNK + (within & 15) + jnp.where(within >= CHUNK, TOK // 2, 0)
    return jnp.where(place == col, 1.0, 0.0).astype(BF16)


def project_kernel(x_ref, g_ref, slots_ref, wq_ref, wk_ref, wv_ref, o_ref, place_ref, n_ref):
    @pl.when(pl.program_id(0) == 0)
    def _():
        place = arrange(slots_ref[...])
        place_ref[...] = place
        xf = x_ref[...].astype(F32)
        mean = jnp.mean(xf, axis=-1, keepdims=True)
        cen = xf - mean
        var = jnp.mean(cen * cen, axis=-1, keepdims=True)
        normed = (cen * lax.rsqrt(var + 1e-05) * g_ref[...]).astype(BF16)
        n_ref[...] = lax.dot_general(place, normed, TN, preferred_element_type=F32).astype(BF16)

    n = n_ref[...]
    q = jnp.dot(n, wq_ref[...], preferred_element_type=F32) * (1.0 / HDIM**0.5)
    k = jnp.dot(n, wk_ref[...], preferred_element_type=F32)
    v = jnp.dot(n, wv_ref[...], preferred_element_type=F32)
    half = TOK // 2
    low = low_half(TOK)
    lowh = low_half(half)
    for c in range(wq_ref.shape[1] // LANES):
        cols = slice(c * LANES, (c + 1) * LANES)
        kp, vp = k[:, cols], v[:, cols]
        qa, qb = q[:half, cols], q[half:, cols]
        o_ref[2 * c, :TOK] = jnp.where(low, kp, swap(vp)).astype(BF16)
        o_ref[2 * c + 1, :TOK] = jnp.where(low, swap(kp), vp).astype(BF16)
        o_ref[2 * c, TOK:] = jnp.where(lowh, qa, swap(qb)).astype(BF16)
        o_ref[2 * c + 1, TOK:] = jnp.where(lowh, swap(qa), qb).astype(BF16)


def project(x, gain, slots, w_qkv):
    steps = 4
    width = D // steps
    return pl.pallas_call(
        project_kernel,
        grid=(steps,),
        in_specs=[
            pl.BlockSpec((TOK, D), lambda i: (0, 0)),
            pl.BlockSpec((1, D), lambda i: (0, 0)),
            pl.BlockSpec((1, QMAX), lambda i: (0, 0)),
            pl.BlockSpec((D, width), lambda i: (0, i)),
            pl.BlockSpec((D, width), lambda i: (0, i + steps)),
            pl.BlockSpec((D, width), lambda i: (0, i + 2 * steps)),
        ],
        out_specs=[
            pl.BlockSpec((HEADS // steps, TOK + TOK // 2, LANES), lambda i: (i, 0, 0)),
            pl.BlockSpec((TOK, TOK), lambda i: (0, 0)),
        ],
        out_shape=[
            jax.ShapeDtypeStruct((HEADS, TOK + TOK // 2, LANES), BF16),
            jax.ShapeDtypeStruct((TOK, TOK), BF16),
        ],
        scratch_shapes=[pltpu.VMEM((TOK, D), BF16)],
        compiler_params=pltpu.CompilerParams(vmem_limit_bytes=60 << 20),
        name="project",
    )(x, gain.reshape(1, D), slots, w_qkv, w_qkv, w_qkv)


BLOCK_FRAMES = 4
GROUP = FRAMES // 2
CHUNKS = TOK // (2 * CHUNK)
ROWS = GROUP * 2 * CHUNK
SPLIT = 6


def unpack_queries(packed):
    packed = packed.reshape(GROUP * CHUNK, LANES).astype(F32)
    low = low_half(packed.shape[0])
    zero = jnp.zeros_like(packed)
    both = [jnp.where(low, packed, zero), jnp.where(low, swap(packed), zero)]
    return jnp.concatenate(both, axis=0).astype(BF16)


def load_queries(mine_ref, chunk):
    start = pl.multiple_of(TOK + chunk * CHUNK, CHUNK)
    return unpack_queries(mine_ref[:, pl.ds(start, CHUNK), :])


def kv_block(kv_ref, j, count):
    return kv_ref[pl.ds(j * count, count), :TOK].reshape(count * TOK, LANES)


def fill_values(kv_ref, va_ref):
    @pl.when(pl.program_id(0) == 0)
    def _():
        for j in range(GROUP):
            kv = kv_ref[j, :TOK]
            va_ref[j] = jnp.where(low_half(TOK), jnp.ones_like(kv), kv)


def absorb(q, kv_ref, va_ref, top, acc):
    def scores(j):
        block = kv_block(kv_ref, j, BLOCK_FRAMES)
        return lax.dot_general(q, block, NT, preferred_element_type=F32)

    blocks = GROUP // BLOCK_FRAMES
    s = scores(0)
    for j in range(blocks):
        ahead = scores(j + 1) if j + 1 < blocks else None
        newtop = jnp.max(s, axis=-1, keepdims=True) * LOG2E
        if top is not None:
            newtop = jnp.maximum(top, newtop)
        p = jnp.exp2(s * LOG2E - newtop).astype(BF16)
        pv = jnp.dot(p, kv_block(va_ref, j, BLOCK_FRAMES), preferred_element_type=F32)
        acc = pv if top is None else acc * jnp.exp2(top - newtop) + pv
        top, s = newtop, ahead
    return top, acc


def own_kernel(first, mine_ref, *rest):
    state_ref, tick_ref, va_ref = rest[-3:]
    tick_ref[...] = jnp.zeros_like(tick_ref)
    fill_values(mine_ref, va_ref)
    q = load_queries(mine_ref, pl.program_id(0) + first)
    top, acc = absorb(q, mine_ref, va_ref, None, None)
    lane = lax.broadcasted_iota(jnp.int32, acc.shape, 1)
    state_ref[...] = jnp.where(lane == 1, top, acc)


def other_kernel(starts, mine_ref, other_ref, *rest):
    state_refs = rest[: len(starts)]
    o_ref, va_ref = rest[-2:]
    fill_values(other_ref, va_ref)
    chunk = pl.program_id(0) + starts[0]
    q = load_queries(mine_ref, chunk)
    state = state_refs[0][...]
    for start, ref in zip(starts[1:], state_refs[1:], strict=True):
        state = jnp.where(chunk >= start, ref[...], state)
    top, acc = absorb(q, other_ref, va_ref, state[:, 1:2], state)
    out = acc / acc[:, :1]
    packed = jnp.where(low_half(ROWS // 2), swap(out[: ROWS // 2]), out[ROWS // 2 :])
    o_ref[...] = packed.astype(BF16).reshape(o_ref.shape)


def picks_kernel(mine_ref, picks_ref, me_ref, *rest):
    o_ref, tick_ref, va_ref = rest[-3:]
    tick_ref[...] = jnp.zeros_like(tick_ref)
    fill_values(mine_ref, va_ref)
    step = pl.program_id(0)
    own = mine_ref[:, TOK : TOK + CHUNK, :]
    q = unpack_queries(jnp.where(step == 0, own, picks_ref[...]))
    top, acc = absorb(q, mine_ref, va_ref, None, None)
    sums = acc[:, :1]
    mean = acc / sums
    level = top + jnp.log2(sums)
    part0 = level.astype(BF16).astype(F32)
    part1 = (level - part0).astype(BF16).astype(F32)
    part2 = level - part0 - part1
    lane = lax.broadcasted_iota(jnp.int32, acc.shape, 1)
    low = jnp.where(lane == 0, part0, jnp.where(lane == 1, part1, part2))
    out = jnp.where(lane < HDIM, low, mean).astype(BF16).reshape(2, GROUP, CHUNK, LANES)
    side = me_ref[0] & 1
    side = jnp.where(step == 0, side, 1 - side)
    for half in range(2):
        o_ref[:, side, half * CHUNK : (half + 1) * CHUNK] = out[half]


VMEM = pl.BlockSpec(memory_space=pltpu.VMEM)
SMEM = pl.BlockSpec(memory_space=pltpu.SMEM)


def attend_settings(chunks):
    pairs = chunks * ROWS * GROUP * TOK
    return dict(
        grid=(chunks,),
        scratch_shapes=[pltpu.VMEM((GROUP, TOK, LANES), BF16)],
        compiler_params=pltpu.CompilerParams(vmem_limit_bytes=20 << 20),
        cost_estimate=pl.CostEstimate(
            flops=2 * pairs * LANES * 4, bytes_accessed=1 << 20, transcendentals=pairs
        ),
    )


HBM = pl.BlockSpec(memory_space=pltpu.HBM)
TICK = jax.ShapeDtypeStruct((8, LANES), F32)
STATE_ROWS = 160 * ROWS


def attend_own(mine, first, last, after=()):
    return pl.pallas_call(
        functools.partial(own_kernel, first),
        in_specs=[VMEM] * (1 + len(after)),
        out_specs=[pl.BlockSpec((ROWS, LANES), lambda i: (i, 0)), VMEM],
        out_shape=[jax.ShapeDtypeStruct((STATE_ROWS, LANES), F32), TICK],
        name=f"attend_own_{first}",
        **attend_settings(last - first),
    )(mine, *after)


def attend_picks(mine, picks, me, after):
    return pl.pallas_call(
        picks_kernel,
        in_specs=[VMEM, VMEM, SMEM] + [VMEM] * len(after),
        out_specs=[pl.BlockSpec((GROUP, 2, QMAX, LANES), lambda i: (0, 0, 0, 0)), VMEM],
        out_shape=[jax.ShapeDtypeStruct((GROUP, 2, QMAX, LANES), BF16), TICK],
        name="attend_picks",
        **attend_settings(2),
    )(mine, picks, me, *after)


def attend_other(mine, other, states, counts, after=()):
    chunks = sum(counts)
    starts = [CHUNKS - sum(counts[i:]) for i in range(len(counts))]

    def state_spec(start, count):
        shift = start - starts[0]
        return pl.BlockSpec((ROWS, LANES), lambda i: (jnp.clip(i - shift, 0, count - 1), 0))

    return pl.pallas_call(
        functools.partial(other_kernel, starts),
        in_specs=[VMEM, VMEM]
        + [state_spec(*pair) for pair in zip(starts, counts, strict=True)]
        + [VMEM] * len(after),
        out_specs=pl.BlockSpec((GROUP, CHUNK, LANES), lambda i: (0, i, 0)),
        out_shape=jax.ShapeDtypeStruct((GROUP, chunks * CHUNK, LANES), BF16),
        name="attend_other",
        **attend_settings(chunks),
    )(mine, other, *states, *after)


def join_heads(even_odd):
    top, bottom = [], []
    for even, odd in even_odd:
        low = low_half(even.shape[0])
        top.append(jnp.where(low, even, swap(odd)).astype(BF16))
        bottom.append(jnp.where(low, swap(even), odd).astype(BF16))
    return jnp.concatenate(top, axis=1), jnp.concatenate(bottom, axis=1)


def level_of(part):
    return part[:, 0:1] + part[:, 1:2] + part[:, 2:3]


def rows_kernel(part_ref, w_hbm, x_ref, place_ref, slots_ref, counts_ref, owner_ref, me_ref, *rest):
    send_hbm, att_ref, w_ref, rows_ref, sems = rest[-5:]
    load_w = pltpu.make_async_copy(w_hbm, w_ref, sems.at[0])
    load_w.start()
    heads = []
    for h in range(HEADS):
        a, b = part_ref[2 * h].astype(F32), part_ref[2 * h + 1].astype(F32)
        la, lb = level_of(a), level_of(b)
        most = jnp.maximum(la, lb)
        wa, wb = jnp.exp2(la - most), jnp.exp2(lb - most)
        heads.append((a * wa + b * wb) / (wa + wb))
    att = jnp.concatenate(
        [
            jnp.where(low_half(QMAX), swap(heads[2 * i]), heads[2 * i + 1]).astype(BF16)
            for i in range(HEADS // 2)
        ],
        axis=1,
    )
    att_ref[...] = att
    gap = jnp.zeros((TOK // 2 - CHUNK, D), BF16)
    placed = jnp.concatenate([att[:CHUNK], gap, att[CHUNK:], gap], axis=0)
    token_slot = jnp.where(slot_of_token(slots_ref[...]), 1.0, 0.0).astype(BF16)
    where = lax.dot_general(token_slot, place_ref[...], TN, preferred_element_type=F32).astype(BF16)
    chosen = jnp.dot(where, placed, preferred_element_type=F32).astype(BF16)
    x = lax.dot_general(token_slot, x_ref[...], TN, preferred_element_type=F32)
    load_w.wait()
    rows = (x + jnp.dot(chosen, w_ref[...], preferred_element_type=F32)).astype(BF16)
    me = me_ref[0]
    slot = lax.broadcasted_iota(jnp.int32, rows.shape, 0)
    rows_ref[...] = jnp.where(slot < counts_ref[me], rows, jnp.zeros_like(rows))
    put = pltpu.make_async_copy(rows_ref, send_hbm.at[owner_ref[me]], sems.at[1])
    put.start()
    put.wait()


def track_rows(parts, w_out, x, place, slots, counts, owner, me, after):
    return pl.pallas_call(
        rows_kernel,
        in_specs=[VMEM, HBM] + [VMEM] * 3 + [SMEM] * 3 + [HBM] * len(after),
        out_specs=[HBM, VMEM],
        scratch_shapes=[
            pltpu.VMEM((D, D), BF16),
            pltpu.VMEM((QMAX, D), BF16),
            pltpu.SemaphoreType.DMA((2,)),
        ],
        out_shape=[
            jax.ShapeDtypeStruct((FRAMES, QMAX, D), BF16),
            jax.ShapeDtypeStruct((QMAX, D), BF16),
        ],
        compiler_params=pltpu.CompilerParams(vmem_limit_bytes=52 << 20),
        cost_estimate=pl.CostEstimate(flops=2 << 30, bytes_accessed=4 << 20, transcendentals=0),
        name="track_rows",
    )(parts, w_out, x, place, slots, counts, owner, me, *after)


def finish_kernel(
    owner_ref, me_ref, att1_hbm, at2_hbm, place_hbm, w_hbm, x_hbm, rows_hbm, mixed_ref, corr_ref, *scratch
):
    att1_ref, at2_ref, place_ref, w_ref, x_ref, rows_ref, sems = scratch

    @pl.when(pl.program_id(0) == 0)
    def _():
        sources = (at2_hbm, att1_hbm, place_hbm, w_hbm, x_hbm, rows_hbm)
        targets = (at2_ref, att1_ref, place_ref, w_ref, x_ref, rows_ref)
        loads = [
            pltpu.make_async_copy(source, target, sems.at[n])
            for n, (source, target) in enumerate(zip(sources, targets, strict=True))
        ]
        for load in loads:
            load.start()
        loads[0].wait()
        pairs = [
            (at2_ref[2 * i].astype(F32), at2_ref[2 * i + 1].astype(F32)) for i in range(HEADS // 2)
        ]
        top, bottom = join_heads(pairs)
        loads[1].wait()
        loads[2].wait()
        placed = jnp.concatenate([att1_ref[:CHUNK], top, att1_ref[CHUNK:], bottom], axis=0)
        att = jnp.dot(place_ref[...], placed, preferred_element_type=F32).astype(BF16)
        loads[3].wait()
        loads[4].wait()
        mixed_ref[...] = (
            x_ref[...].astype(F32) + jnp.dot(att, w_ref[...], preferred_element_type=F32)
        ).astype(BF16)
        loads[5].wait()

    step = corr_ref.shape[1]
    first = pl.program_id(0) * step
    rows = rows_ref[pl.ds(first, step)].reshape(-1, D)
    corr = lax.dot_general(rows, mixed_ref[...], NT, preferred_element_type=F32)
    corr = (corr * (1.0 / D**0.5)).reshape(step, QMAX, TOK)
    for i in range(step):
        owned = owner_ref[first + i] == me_ref[0]
        corr_ref[0, i] = jnp.where(owned, corr[i], jnp.zeros_like(corr[i]))


def finish(att1, att2, x, w_out, place, owner, me, arrived):
    step = 16
    return pl.pallas_call(
        finish_kernel,
        grid=(FRAMES // step,),
        in_specs=[SMEM] * 2 + [HBM] * 6,
        out_specs=[
            pl.BlockSpec((TOK, D), lambda i: (0, 0)),
            pl.BlockSpec((1, step, QMAX, TOK), lambda i: (0, i, 0, 0)),
        ],
        out_shape=[
            jax.ShapeDtypeStruct((TOK, D), BF16),
            jax.ShapeDtypeStruct((1, FRAMES, QMAX, TOK), F32),
        ],
        scratch_shapes=[
            pltpu.VMEM(array.shape, array.dtype) for array in (att1, att2, place, w_out, x, arrived)
        ]
        + [pltpu.SemaphoreType.DMA((6,))],
        compiler_params=pltpu.CompilerParams(vmem_limit_bytes=58 << 20),
        name="finish",
    )(owner, me, att1, att2, place, w_out, x, arrived)


def per_device(features, norm_gain, w_qkv, w_out, counts, query_index, owner):
    groups = [[2 * i + side for i in range(GROUP)] for side in range(2)]
    swap_sides = [(d, d ^ 1) for d in range(FRAMES)]
    me = lax.axis_index("frame").astype(jnp.int32).reshape(1)
    packed, place = project(features, norm_gain, query_index, w_qkv)
    mine = lax.all_to_all(packed, "frame", 0, 0, tiled=True, axis_index_groups=groups)
    picks = lax.ppermute(mine[:, TOK : TOK + CHUNK], "frame", swap_sides)
    other = lax.ppermute(mine[:, :TOK], "frame", swap_sides)
    state1, tick = attend_own(mine, 1, 2)
    parts, tick = attend_picks(mine, picks, me, [tick])
    parts_here = lax.all_to_all(
        parts.reshape(FRAMES, QMAX, LANES), "frame", 0, 0, tiled=True
    )
    state2, _ = attend_own(mine, 2, SPLIT, [tick])
    send, att1 = track_rows(
        parts_here, w_out, features, place, query_index, counts, owner, me, [state2]
    )
    arrived = lax.all_to_all(send, "frame", 0, 0, tiled=True)
    state3, _ = attend_own(mine, SPLIT, CHUNKS, [att1])
    rest = attend_other(
        mine, other, [state1, state2, state3], [1, SPLIT - 2, CHUNKS - SPLIT]
    )
    rest, arrived = lax.optimization_barrier((rest, arrived))
    att2 = lax.all_to_all(rest, "frame", 0, 0, tiled=True, axis_index_groups=groups)
    return tuple(finish(att1, att2, features, w_out, place, owner, me, arrived))


def solution(mesh):
    rows = P(("scene", "frame"), None)
    in_specs = (rows, P(), P(), P(), P("scene"), rows, P("scene"))
    out_specs = (rows, P(("scene", "frame"), None, None, None))
    return jax.shard_map(
        per_device, mesh=mesh, in_specs=in_specs, out_specs=out_specs, check_vma=False
    )
```

```python
import functools

import jax
import jax.numpy as jnp
from jax import lax
from jax.experimental import pallas as pl
from jax.experimental.pallas import tpu as pltpu
from jax.sharding import PartitionSpec as P

D = 1024
HEADS = 16
HDIM = 64
TOK = 256
FRAMES = 32
QMAX = 32
LANES = 128
LOG2E = 1.4426950408889634
NT = (((1,), (1,)), ((), ()))
TN = (((0,), (0,)), ((), ()))
CHUNK = 16
F32 = jnp.float32
BF16 = jnp.bfloat16


def low_half(rows):
    return lax.broadcasted_iota(jnp.int32, (rows, LANES), 1) < HDIM


def swap(x):
    return pltpu.roll(x, HDIM, 1)


def slot_of_token(slots):
    return lax.broadcasted_iota(jnp.int32, (TOK, QMAX), 0) == slots


def arrange(slots):
    picked = jnp.max(jnp.where(slot_of_token(slots), 1.0, 0.0), axis=1, keepdims=True)
    row = lax.broadcasted_iota(jnp.int32, (TOK, TOK), 0)
    col = lax.broadcasted_iota(jnp.int32, (TOK, TOK), 1)
    wide = jnp.broadcast_to(picked, (TOK, LANES)).astype(BF16)
    before = jnp.dot(jnp.where(col < row, 1.0, 0.0).astype(BF16), wide, preferred_element_type=F32)
    before = before[:, :1].astype(jnp.int32)
    total = jnp.sum(picked).astype(jnp.int32)
    token = lax.broadcasted_iota(jnp.int32, (TOK, 1), 0)
    rank = jnp.where(picked > 0.5, before, total + token - before)
    within = rank & 31
    place = (rank >> 5) * CHUNK + (within & 15) + jnp.where(within >= CHUNK, TOK // 2, 0)
    return jnp.where(place == col, 1.0, 0.0).astype(BF16)


def project_kernel(x_ref, g_ref, slots_ref, wq_ref, wk_ref, wv_ref, o_ref, place_ref, n_ref):
    @pl.when(pl.program_id(0) == 0)
    def _():
        place = arrange(slots_ref[...])
        place_ref[...] = place
        xf = x_ref[...].astype(F32)
        mean = jnp.mean(xf, axis=-1, keepdims=True)
        cen = xf - mean
        var = jnp.mean(cen * cen, axis=-1, keepdims=True)
        normed = (cen * lax.rsqrt(var + 1e-05) * g_ref[...]).astype(BF16)
        n_ref[...] = lax.dot_general(place, normed, TN, preferred_element_type=F32).astype(BF16)

    n = n_ref[...]
    q = jnp.dot(n, wq_ref[...], preferred_element_type=F32) * (1.0 / HDIM**0.5)
    k = jnp.dot(n, wk_ref[...], preferred_element_type=F32)
    v = jnp.dot(n, wv_ref[...], preferred_element_type=F32)
    half = TOK // 2
    low = low_half(TOK)
    lowh = low_half(half)
    for c in range(wq_ref.shape[1] // LANES):
        cols = slice(c * LANES, (c + 1) * LANES)
        kp, vp = k[:, cols], v[:, cols]
        qa, qb = q[:half, cols], q[half:, cols]
        o_ref[2 * c, :TOK] = jnp.where(low, kp, swap(vp)).astype(BF16)
        o_ref[2 * c + 1, :TOK] = jnp.where(low, swap(kp), vp).astype(BF16)
        o_ref[2 * c, TOK:] = jnp.where(lowh, qa, swap(qb)).astype(BF16)
        o_ref[2 * c + 1, TOK:] = jnp.where(lowh, swap(qa), qb).astype(BF16)


def project(x, gain, slots, w_qkv):
    steps = 4
    width = D // steps
    return pl.pallas_call(
        project_kernel,
        grid=(steps,),
        in_specs=[
            pl.BlockSpec((TOK, D), lambda i: (0, 0)),
            pl.BlockSpec((1, D), lambda i: (0, 0)),
            pl.BlockSpec((1, QMAX), lambda i: (0, 0)),
            pl.BlockSpec((D, width), lambda i: (0, i)),
            pl.BlockSpec((D, width), lambda i: (0, i + steps)),
            pl.BlockSpec((D, width), lambda i: (0, i + 2 * steps)),
        ],
        out_specs=[
            pl.BlockSpec((HEADS // steps, TOK + TOK // 2, LANES), lambda i: (i, 0, 0)),
            pl.BlockSpec((TOK, TOK), lambda i: (0, 0)),
        ],
        out_shape=[
            jax.ShapeDtypeStruct((HEADS, TOK + TOK // 2, LANES), BF16),
            jax.ShapeDtypeStruct((TOK, TOK), BF16),
        ],
        scratch_shapes=[pltpu.VMEM((TOK, D), BF16)],
        compiler_params=pltpu.CompilerParams(vmem_limit_bytes=60 << 20),
        name="project",
    )(x, gain.reshape(1, D), slots, w_qkv, w_qkv, w_qkv)


BLOCK_FRAMES = 4
GROUP = FRAMES // 2
CHUNKS = TOK // (2 * CHUNK)
ROWS = GROUP * 2 * CHUNK
SPLIT = 6


def unpack_queries(packed):
    packed = packed.reshape(GROUP * CHUNK, LANES).astype(F32)
    low = low_half(packed.shape[0])
    zero = jnp.zeros_like(packed)
    both = [jnp.where(low, packed, zero), jnp.where(low, swap(packed), zero)]
    return jnp.concatenate(both, axis=0).astype(BF16)


def load_queries(mine_ref, chunk):
    start = pl.multiple_of(TOK + chunk * CHUNK, CHUNK)
    return unpack_queries(mine_ref[:, pl.ds(start, CHUNK), :])


def kv_block(kv_ref, j, count):
    return kv_ref[pl.ds(j * count, count), :TOK].reshape(count * TOK, LANES)


def fill_values(kv_ref, va_ref, step=0):
    @pl.when(pl.program_id(0) == step)
    def _():
        for j in range(GROUP):
            kv = kv_ref[j, :TOK]
            va_ref[j] = jnp.where(low_half(TOK), jnp.ones_like(kv), kv)


def absorb(q, kv_ref, va_ref, top, acc):
    def scores(j):
        block = kv_block(kv_ref, j, BLOCK_FRAMES)
        return lax.dot_general(q, block, NT, preferred_element_type=F32)

    blocks = GROUP // BLOCK_FRAMES
    s = scores(0)
    for j in range(blocks):
        ahead = scores(j + 1) if j + 1 < blocks else None
        newtop = jnp.max(s, axis=-1, keepdims=True) * LOG2E
        if top is not None:
            newtop = jnp.maximum(top, newtop)
        p = jnp.exp2(s * LOG2E - newtop).astype(BF16)
        pv = jnp.dot(p, kv_block(va_ref, j, BLOCK_FRAMES), preferred_element_type=F32)
        acc = pv if top is None else acc * jnp.exp2(top - newtop) + pv
        top, s = newtop, ahead
    return top, acc


def own_kernel(first, mine_ref, *rest):
    state_ref, tick_ref, va_ref = rest[-3:]
    tick_ref[...] = jnp.zeros_like(tick_ref)
    fill_values(mine_ref, va_ref)
    q = load_queries(mine_ref, pl.program_id(0) + first)
    top, acc = absorb(q, mine_ref, va_ref, None, None)
    lane = lax.broadcasted_iota(jnp.int32, acc.shape, 1)
    state_ref[...] = jnp.where(lane == 1, top, acc)


def last_kernel(starts, mine_ref, other_ref, *rest):
    o_ref, va_ref, keep_ref = rest[-3:]
    late = keep_ref.shape[0]
    step = pl.program_id(0)
    fill_values(mine_ref, va_ref)
    fill_values(other_ref, va_ref, late)

    @pl.when(step < late)
    def _():
        q = load_queries(mine_ref, step + CHUNKS - late)
        top, acc = absorb(q, mine_ref, va_ref, None, None)
        lane = lax.broadcasted_iota(jnp.int32, acc.shape, 1)
        keep_ref[step] = jnp.where(lane == 1, top, acc)

    @pl.when(step >= late)
    def _():
        chunk = step - late + starts[0]
        q = load_queries(mine_ref, chunk)
        state = rest[0][...]
        for n in range(1, len(starts)):
            state = jnp.where(chunk >= starts[n], rest[n][...], state)
        kept = keep_ref[jnp.maximum(chunk - (CHUNKS - late), 0)]
        state = jnp.where(chunk >= CHUNKS - late, kept, state)
        top, acc = absorb(q, other_ref, va_ref, state[:, 1:2], state)
        out = acc / acc[:, :1]
        packed = jnp.where(low_half(ROWS // 2), swap(out[: ROWS // 2]), out[ROWS // 2 :])
        o_ref[...] = packed.astype(BF16).reshape(o_ref.shape)


def picks_kernel(mine_ref, picks_ref, me_ref, *rest):
    o_ref, tick_ref, va_ref = rest[-3:]
    tick_ref[...] = jnp.zeros_like(tick_ref)
    fill_values(mine_ref, va_ref)
    step = pl.program_id(0)
    own = mine_ref[:, TOK : TOK + CHUNK, :]
    q = unpack_queries(jnp.where(step == 0, own, picks_ref[...]))
    top, acc = absorb(q, mine_ref, va_ref, None, None)
    sums = acc[:, :1]
    mean = acc / sums
    level = top + jnp.log2(sums)
    part0 = level.astype(BF16).astype(F32)
    part1 = (level - part0).astype(BF16).astype(F32)
    part2 = level - part0 - part1
    lane = lax.broadcasted_iota(jnp.int32, acc.shape, 1)
    low = jnp.where(lane == 0, part0, jnp.where(lane == 1, part1, part2))
    out = jnp.where(lane < HDIM, low, mean).astype(BF16).reshape(2, GROUP, CHUNK, LANES)
    side = me_ref[0] & 1
    side = jnp.where(step == 0, side, 1 - side)
    for half in range(2):
        o_ref[:, side, half * CHUNK : (half + 1) * CHUNK] = out[half]


VMEM = pl.BlockSpec(memory_space=pltpu.VMEM)
SMEM = pl.BlockSpec(memory_space=pltpu.SMEM)


def attend_settings(chunks):
    pairs = chunks * ROWS * GROUP * TOK
    return dict(
        grid=(chunks,),
        scratch_shapes=[pltpu.VMEM((GROUP, TOK, LANES), BF16)],
        compiler_params=pltpu.CompilerParams(vmem_limit_bytes=20 << 20),
        cost_estimate=pl.CostEstimate(
            flops=2 * pairs * LANES * 4, bytes_accessed=1 << 20, transcendentals=pairs
        ),
    )


HBM = pl.BlockSpec(memory_space=pltpu.HBM)
TICK = jax.ShapeDtypeStruct((8, LANES), F32)


def attend_own(mine, first, last, after=(), in_hbm=False):
    return pl.pallas_call(
        functools.partial(own_kernel, first),
        in_specs=[VMEM] * (1 + len(after)),
        out_specs=[pl.BlockSpec((ROWS, LANES), lambda i: (i, 0)), VMEM],
        out_shape=[jax.ShapeDtypeStruct(((160 if in_hbm else last - first) * ROWS, LANES), F32), TICK],
        name=f"attend_own_{first}",
        **attend_settings(last - first),
    )(mine, *after)


def attend_picks(mine, picks, me, after):
    return pl.pallas_call(
        picks_kernel,
        in_specs=[VMEM, VMEM, SMEM] + [VMEM] * len(after),
        out_specs=[pl.BlockSpec((GROUP, 2, QMAX, LANES), lambda i: (0, 0, 0, 0)), VMEM],
        out_shape=[jax.ShapeDtypeStruct((GROUP, 2, QMAX, LANES), BF16), TICK],
        name="attend_picks",
        **attend_settings(2),
    )(mine, picks, me, *after)


def attend_last(mine, other, states, counts, after):
    starts = [1 + sum(counts[:i]) for i in range(len(counts))]
    late = CHUNKS - 1 - sum(counts)
    settings = attend_settings(CHUNKS - 1 + late)
    settings["scratch_shapes"] += [pltpu.VMEM((late, ROWS, LANES), F32)]

    def state_spec(start, count):
        shift = late + start - starts[0]
        return pl.BlockSpec((ROWS, LANES), lambda i: (jnp.clip(i - shift, 0, count - 1), 0))

    return pl.pallas_call(
        functools.partial(last_kernel, starts),
        in_specs=[VMEM, VMEM]
        + [state_spec(*pair) for pair in zip(starts, counts, strict=True)]
        + [VMEM] * len(after),
        out_specs=pl.BlockSpec((GROUP, CHUNK, LANES), lambda i: (0, jnp.maximum(i - late, 0), 0)),
        out_shape=jax.ShapeDtypeStruct((GROUP, (CHUNKS - 1) * CHUNK, LANES), BF16),
        name="attend_last",
        **settings,
    )(mine, other, *states, *after)


def join_heads(even_odd):
    top, bottom = [], []
    for even, odd in even_odd:
        low = low_half(even.shape[0])
        top.append(jnp.where(low, even, swap(odd)).astype(BF16))
        bottom.append(jnp.where(low, swap(even), odd).astype(BF16))
    return jnp.concatenate(top, axis=1), jnp.concatenate(bottom, axis=1)


def level_of(part):
    return part[:, 0:1] + part[:, 1:2] + part[:, 2:3]


def rows_kernel(part_ref, w_hbm, x_ref, place_ref, slots_ref, counts_ref, owner_ref, me_ref, *rest):
    send_hbm, att_ref, w_ref, rows_ref, sems = rest[-5:]
    load_w = pltpu.make_async_copy(w_hbm, w_ref, sems.at[0])
    load_w.start()
    heads = []
    for h in range(HEADS):
        a, b = part_ref[2 * h].astype(F32), part_ref[2 * h + 1].astype(F32)
        la, lb = level_of(a), level_of(b)
        most = jnp.maximum(la, lb)
        wa, wb = jnp.exp2(la - most), jnp.exp2(lb - most)
        heads.append((a * wa + b * wb) / (wa + wb))
    att = jnp.concatenate(
        [
            jnp.where(low_half(QMAX), swap(heads[2 * i]), heads[2 * i + 1]).astype(BF16)
            for i in range(HEADS // 2)
        ],
        axis=1,
    )
    att_ref[...] = att
    gap = jnp.zeros((TOK // 2 - CHUNK, D), BF16)
    placed = jnp.concatenate([att[:CHUNK], gap, att[CHUNK:], gap], axis=0)
    token_slot = jnp.where(slot_of_token(slots_ref[...]), 1.0, 0.0).astype(BF16)
    where = lax.dot_general(token_slot, place_ref[...], TN, preferred_element_type=F32).astype(BF16)
    chosen = jnp.dot(where, placed, preferred_element_type=F32).astype(BF16)
    x = lax.dot_general(token_slot, x_ref[...], TN, preferred_element_type=F32)
    load_w.wait()
    rows = (x + jnp.dot(chosen, w_ref[...], preferred_element_type=F32)).astype(BF16)
    me = me_ref[0]
    slot = lax.broadcasted_iota(jnp.int32, rows.shape, 0)
    rows_ref[...] = jnp.where(slot < counts_ref[me], rows, jnp.zeros_like(rows))
    put = pltpu.make_async_copy(rows_ref, send_hbm.at[owner_ref[me]], sems.at[1])
    put.start()
    put.wait()


def track_rows(parts, w_out, x, place, slots, counts, owner, me, after):
    return pl.pallas_call(
        rows_kernel,
        in_specs=[VMEM, HBM] + [VMEM] * 3 + [SMEM] * 3 + [HBM] * len(after),
        out_specs=[HBM, VMEM],
        scratch_shapes=[
            pltpu.VMEM((D, D), BF16),
            pltpu.VMEM((QMAX, D), BF16),
            pltpu.SemaphoreType.DMA((2,)),
        ],
        out_shape=[
            jax.ShapeDtypeStruct((FRAMES, QMAX, D), BF16),
            jax.ShapeDtypeStruct((QMAX, D), BF16),
        ],
        compiler_params=pltpu.CompilerParams(vmem_limit_bytes=52 << 20),
        cost_estimate=pl.CostEstimate(flops=2 << 30, bytes_accessed=4 << 20, transcendentals=0),
        name="track_rows",
    )(parts, w_out, x, place, slots, counts, owner, me, *after)


def finish_kernel(
    owner_ref, me_ref, att1_hbm, at2_hbm, place_hbm, w_hbm, x_hbm, rows_hbm, mixed_ref, corr_ref, *scratch
):
    att1_ref, at2_ref, place_ref, w_ref, x_ref, rows_ref, sems = scratch

    @pl.when(pl.program_id(0) == 0)
    def _():
        sources = (at2_hbm, att1_hbm, place_hbm, w_hbm, x_hbm, rows_hbm)
        targets = (at2_ref, att1_ref, place_ref, w_ref, x_ref, rows_ref)
        loads = [
            pltpu.make_async_copy(source, target, sems.at[n])
            for n, (source, target) in enumerate(zip(sources, targets, strict=True))
        ]
        for load in loads:
            load.start()
        loads[0].wait()
        pairs = [
            (at2_ref[2 * i].astype(F32), at2_ref[2 * i + 1].astype(F32)) for i in range(HEADS // 2)
        ]
        top, bottom = join_heads(pairs)
        loads[1].wait()
        loads[2].wait()
        placed = jnp.concatenate([att1_ref[:CHUNK], top, att1_ref[CHUNK:], bottom], axis=0)
        att = jnp.dot(place_ref[...], placed, preferred_element_type=F32).astype(BF16)
        loads[3].wait()
        loads[4].wait()
        mixed_ref[...] = (
            x_ref[...].astype(F32) + jnp.dot(att, w_ref[...], preferred_element_type=F32)
        ).astype(BF16)
        loads[5].wait()

    step = corr_ref.shape[1]
    first = pl.program_id(0) * step
    rows = rows_ref[pl.ds(first, step)].reshape(-1, D)
    corr = lax.dot_general(rows, mixed_ref[...], NT, preferred_element_type=F32)
    corr = (corr * (1.0 / D**0.5)).reshape(step, QMAX, TOK)
    for i in range(step):
        owned = owner_ref[first + i] == me_ref[0]
        corr_ref[0, i] = jnp.where(owned, corr[i], jnp.zeros_like(corr[i]))


def finish(att1, att2, x, w_out, place, owner, me, arrived):
    step = 16
    return pl.pallas_call(
        finish_kernel,
        grid=(FRAMES // step,),
        in_specs=[SMEM] * 2 + [HBM] * 6,
        out_specs=[
            pl.BlockSpec((TOK, D), lambda i: (0, 0)),
            pl.BlockSpec((1, step, QMAX, TOK), lambda i: (0, i, 0, 0)),
        ],
        out_shape=[
            jax.ShapeDtypeStruct((TOK, D), BF16),
            jax.ShapeDtypeStruct((1, FRAMES, QMAX, TOK), F32),
        ],
        scratch_shapes=[
            pltpu.VMEM(array.shape, array.dtype) for array in (att1, att2, place, w_out, x, arrived)
        ]
        + [pltpu.SemaphoreType.DMA((6,))],
        compiler_params=pltpu.CompilerParams(vmem_limit_bytes=58 << 20),
        name="finish",
    )(owner, me, att1, att2, place, w_out, x, arrived)


def per_device(features, norm_gain, w_qkv, w_out, counts, query_index, owner):
    groups = [[2 * i + side for i in range(GROUP)] for side in range(2)]
    swap_sides = [(d, d ^ 1) for d in range(FRAMES)]
    me = lax.axis_index("frame").astype(jnp.int32).reshape(1)
    packed, place = project(features, norm_gain, query_index, w_qkv)
    mine = lax.all_to_all(packed, "frame", 0, 0, tiled=True, axis_index_groups=groups)
    picks = lax.ppermute(mine[:, TOK : TOK + CHUNK], "frame", swap_sides)
    other = lax.ppermute(mine[:, :TOK], "frame", swap_sides)
    state1, tick = attend_own(mine, 1, 2)
    parts, tick = attend_picks(mine, picks, me, [tick])
    parts_here = lax.all_to_all(
        parts.reshape(FRAMES, QMAX, LANES), "frame", 0, 0, tiled=True
    )
    state2, _ = attend_own(mine, 2, SPLIT, [tick], in_hbm=True)
    send, att1 = track_rows(
        parts_here, w_out, features, place, query_index, counts, owner, me, [state2]
    )
    arrived = lax.all_to_all(send, "frame", 0, 0, tiled=True)
    rest = attend_last(mine, other, [state1, state2], [1, SPLIT - 2], [att1])
    rest, arrived = lax.optimization_barrier((rest, arrived))
    att2 = lax.all_to_all(rest, "frame", 0, 0, tiled=True, axis_index_groups=groups)
    return tuple(finish(att1, att2, features, w_out, place, owner, me, arrived))


def solution(mesh):
    rows = P(("scene", "frame"), None)
    in_specs = (rows, P(), P(), P(), P("scene"), rows, P("scene"))
    out_specs = (rows, P(("scene", "frame"), None, None, None))
    return jax.shard_map(
        per_device, mesh=mesh, in_specs=in_specs, out_specs=out_specs, check_vma=False
    )
```

```python
import functools

import jax
import jax.numpy as jnp
from jax import lax
from jax.experimental import pallas as pl
from jax.experimental.pallas import tpu as pltpu
from jax.sharding import PartitionSpec as P

D = 1024
HEADS = 16
HDIM = 64
TOK = 256
FRAMES = 32
QMAX = 32
LANES = 128
LOG2E = 1.4426950408889634
NT = (((1,), (1,)), ((), ()))
TN = (((0,), (0,)), ((), ()))
CHUNK = 16
F32 = jnp.float32
BF16 = jnp.bfloat16


def low_half(rows):
    return lax.broadcasted_iota(jnp.int32, (rows, LANES), 1) < HDIM


def swap(x):
    return pltpu.roll(x, HDIM, 1)


def slot_of_token(slots):
    return lax.broadcasted_iota(jnp.int32, (TOK, QMAX), 0) == slots


def arrange(slots):
    picked = jnp.max(jnp.where(slot_of_token(slots), 1.0, 0.0), axis=1, keepdims=True)
    row = lax.broadcasted_iota(jnp.int32, (TOK, TOK), 0)
    col = lax.broadcasted_iota(jnp.int32, (TOK, TOK), 1)
    wide = jnp.broadcast_to(picked, (TOK, LANES)).astype(BF16)
    before = jnp.dot(jnp.where(col < row, 1.0, 0.0).astype(BF16), wide, preferred_element_type=F32)
    before = before[:, :1].astype(jnp.int32)
    total = jnp.sum(picked).astype(jnp.int32)
    token = lax.broadcasted_iota(jnp.int32, (TOK, 1), 0)
    rank = jnp.where(picked > 0.5, before, total + token - before)
    within = rank & 31
    place = (rank >> 5) * CHUNK + (within & 15) + jnp.where(within >= CHUNK, TOK // 2, 0)
    return jnp.where(place == col, 1.0, 0.0).astype(BF16)


def project_kernel(x_ref, g_ref, slots_ref, wq_ref, wk_ref, wv_ref, o_ref, place_ref, n_ref):
    @pl.when(pl.program_id(0) == 0)
    def _():
        place = arrange(slots_ref[...])
        place_ref[...] = place
        xf = x_ref[...].astype(F32)
        mean = jnp.mean(xf, axis=-1, keepdims=True)
        cen = xf - mean
        var = jnp.mean(cen * cen, axis=-1, keepdims=True)
        normed = (cen * lax.rsqrt(var + 1e-05) * g_ref[...]).astype(BF16)
        n_ref[...] = lax.dot_general(place, normed, TN, preferred_element_type=F32).astype(BF16)

    n = n_ref[...]
    q = jnp.dot(n, wq_ref[...], preferred_element_type=F32) * (1.0 / HDIM**0.5)
    k = jnp.dot(n, wk_ref[...], preferred_element_type=F32)
    v = jnp.dot(n, wv_ref[...], preferred_element_type=F32)
    half = TOK // 2
    low = low_half(TOK)
    lowh = low_half(half)
    for c in range(wq_ref.shape[1] // LANES):
        cols = slice(c * LANES, (c + 1) * LANES)
        kp, vp = k[:, cols], v[:, cols]
        qa, qb = q[:half, cols], q[half:, cols]
        o_ref[2 * c, :TOK] = jnp.where(low, kp, swap(vp)).astype(BF16)
        o_ref[2 * c + 1, :TOK] = jnp.where(low, swap(kp), vp).astype(BF16)
        o_ref[2 * c, TOK:] = jnp.where(lowh, qa, swap(qb)).astype(BF16)
        o_ref[2 * c + 1, TOK:] = jnp.where(lowh, swap(qa), qb).astype(BF16)


def project(x, gain, slots, w_qkv):
    steps = 4
    width = D // steps
    return pl.pallas_call(
        project_kernel,
        grid=(steps,),
        in_specs=[
            pl.BlockSpec((TOK, D), lambda i: (0, 0)),
            pl.BlockSpec((1, D), lambda i: (0, 0)),
            pl.BlockSpec((1, QMAX), lambda i: (0, 0)),
            pl.BlockSpec((D, width), lambda i: (0, i)),
            pl.BlockSpec((D, width), lambda i: (0, i + steps)),
            pl.BlockSpec((D, width), lambda i: (0, i + 2 * steps)),
        ],
        out_specs=[
            pl.BlockSpec((HEADS // steps, TOK + TOK // 2, LANES), lambda i: (i, 0, 0)),
            pl.BlockSpec((TOK, TOK), lambda i: (0, 0)),
        ],
        out_shape=[
            jax.ShapeDtypeStruct((HEADS, TOK + TOK // 2, LANES), BF16),
            jax.ShapeDtypeStruct((TOK, TOK), BF16),
        ],
        scratch_shapes=[pltpu.VMEM((TOK, D), BF16)],
        compiler_params=pltpu.CompilerParams(vmem_limit_bytes=60 << 20),
        name="project",
    )(x, gain.reshape(1, D), slots, w_qkv, w_qkv, w_qkv)


BLOCK_FRAMES = 4
GROUP = FRAMES // 2
CHUNKS = TOK // (2 * CHUNK)
ROWS = GROUP * 2 * CHUNK
SPLIT = 6


def unpack_queries(packed):
    packed = packed.reshape(GROUP * CHUNK, LANES).astype(F32)
    low = low_half(packed.shape[0])
    zero = jnp.zeros_like(packed)
    both = [jnp.where(low, packed, zero), jnp.where(low, swap(packed), zero)]
    return jnp.concatenate(both, axis=0).astype(BF16)


def load_queries(mine_ref, chunk):
    start = pl.multiple_of(TOK + chunk * CHUNK, CHUNK)
    return unpack_queries(mine_ref[:, pl.ds(start, CHUNK), :])


def kv_block(kv_ref, j, count):
    return kv_ref[pl.ds(j * count, count), :TOK].reshape(count * TOK, LANES)


def fill_values(kv_ref, va_ref):
    @pl.when(pl.program_id(0) == 0)
    def _():
        for j in range(GROUP):
            kv = kv_ref[j, :TOK]
            va_ref[j] = jnp.where(low_half(TOK), jnp.ones_like(kv), kv)


def absorb(q, kv_ref, va_ref, top, acc):
    def scores(j):
        block = kv_block(kv_ref, j, BLOCK_FRAMES)
        return lax.dot_general(q, block, NT, preferred_element_type=F32)

    blocks = GROUP // BLOCK_FRAMES
    s = scores(0)
    for j in range(blocks):
        ahead = scores(j + 1) if j + 1 < blocks else None
        newtop = jnp.max(s, axis=-1, keepdims=True) * LOG2E
        if top is not None:
            newtop = jnp.maximum(top, newtop)
        p = jnp.exp2(s * LOG2E - newtop).astype(BF16)
        pv = jnp.dot(p, kv_block(va_ref, j, BLOCK_FRAMES), preferred_element_type=F32)
        acc = pv if top is None else acc * jnp.exp2(top - newtop) + pv
        top, s = newtop, ahead
    return top, acc


def own_kernel(first, mine_ref, *rest):
    state_ref, tick_ref, va_ref = rest[-3:]
    tick_ref[...] = jnp.zeros_like(tick_ref)
    fill_values(mine_ref, va_ref)
    q = load_queries(mine_ref, pl.program_id(0) + first)
    top, acc = absorb(q, mine_ref, va_ref, None, None)
    lane = lax.broadcasted_iota(jnp.int32, acc.shape, 1)
    state_ref[...] = jnp.where(lane == 1, top, acc)


def other_kernel(starts, mine_ref, other_ref, *rest):
    state_refs = rest[: len(starts)]
    o_ref, va_ref = rest[-2:]
    fill_values(other_ref, va_ref)
    chunk = pl.program_id(0) + starts[0]
    q = load_queries(mine_ref, chunk)
    state = state_refs[0][...]
    for start, ref in zip(starts[1:], state_refs[1:], strict=True):
        state = jnp.where(chunk >= start, ref[...], state)
    top, acc = absorb(q, other_ref, va_ref, state[:, 1:2], state)
    out = acc / acc[:, :1]
    packed = jnp.where(low_half(ROWS // 2), swap(out[: ROWS // 2]), out[ROWS // 2 :])
    o_ref[...] = packed.astype(BF16).reshape(o_ref.shape)


def picks_kernel(mine_ref, picks_ref, me_ref, *rest):
    o_ref, tick_ref, va_ref = rest[-3:]
    tick_ref[...] = jnp.zeros_like(tick_ref)
    fill_values(mine_ref, va_ref)
    step = pl.program_id(0)
    own = mine_ref[:, TOK : TOK + CHUNK, :]
    q = unpack_queries(jnp.where(step == 0, own, picks_ref[...]))
    top, acc = absorb(q, mine_ref, va_ref, None, None)
    sums = acc[:, :1]
    mean = acc / sums
    level = top + jnp.log2(sums)
    part0 = level.astype(BF16).astype(F32)
    part1 = (level - part0).astype(BF16).astype(F32)
    part2 = level - part0 - part1
    lane = lax.broadcasted_iota(jnp.int32, acc.shape, 1)
    low = jnp.where(lane == 0, part0, jnp.where(lane == 1, part1, part2))
    out = jnp.where(lane < HDIM, low, mean).astype(BF16).reshape(2, GROUP, CHUNK, LANES)
    side = me_ref[0] & 1
    side = jnp.where(step == 0, side, 1 - side)
    for half in range(2):
        o_ref[:, side, half * CHUNK : (half + 1) * CHUNK] = out[half]


VMEM = pl.BlockSpec(memory_space=pltpu.VMEM)
SMEM = pl.BlockSpec(memory_space=pltpu.SMEM)


def attend_settings(chunks):
    pairs = chunks * ROWS * GROUP * TOK
    return dict(
        grid=(chunks,),
        scratch_shapes=[pltpu.VMEM((GROUP, TOK, LANES), BF16)],
        compiler_params=pltpu.CompilerParams(vmem_limit_bytes=20 << 20),
        cost_estimate=pl.CostEstimate(
            flops=2 * pairs * LANES * 4, bytes_accessed=1 << 20, transcendentals=pairs
        ),
    )


HBM = pl.BlockSpec(memory_space=pltpu.HBM)
TICK = jax.ShapeDtypeStruct((8, LANES), F32)


def attend_own(mine, first, last, after=()):
    return pl.pallas_call(
        functools.partial(own_kernel, first),
        in_specs=[VMEM] * (1 + len(after)),
        out_specs=[pl.BlockSpec((ROWS, LANES), lambda i: (i, 0)), VMEM],
        out_shape=[jax.ShapeDtypeStruct(((last - first) * ROWS, LANES), F32), TICK],
        name=f"attend_own_{first}",
        **attend_settings(last - first),
    )(mine, *after)


def attend_picks(mine, picks, me, after):
    return pl.pallas_call(
        picks_kernel,
        in_specs=[VMEM, VMEM, SMEM] + [VMEM] * len(after),
        out_specs=[pl.BlockSpec((GROUP, 2, QMAX, LANES), lambda i: (0, 0, 0, 0)), VMEM],
        out_shape=[jax.ShapeDtypeStruct((GROUP, 2, QMAX, LANES), BF16), TICK],
        name="attend_picks",
        **attend_settings(2),
    )(mine, picks, me, *after)


def attend_other(mine, other, states, after=()):
    counts = [state.shape[0] // ROWS for state in states]
    chunks = sum(counts)
    starts = [CHUNKS - sum(counts[i:]) for i in range(len(counts))]

    def state_spec(start, count):
        shift = start - starts[0]
        return pl.BlockSpec((ROWS, LANES), lambda i: (jnp.clip(i - shift, 0, count - 1), 0))

    return pl.pallas_call(
        functools.partial(other_kernel, starts),
        in_specs=[VMEM, VMEM]
        + [state_spec(*pair) for pair in zip(starts, counts, strict=True)]
        + [VMEM] * len(after),
        out_specs=pl.BlockSpec((GROUP, CHUNK, LANES), lambda i: (0, i, 0)),
        out_shape=jax.ShapeDtypeStruct((GROUP, chunks * CHUNK, LANES), BF16),
        name="attend_other",
        **attend_settings(chunks),
    )(mine, other, *states, *after)


def join_heads(even_odd):
    top, bottom = [], []
    for even, odd in even_odd:
        low = low_half(even.shape[0])
        top.append(jnp.where(low, even, swap(odd)).astype(BF16))
        bottom.append(jnp.where(low, swap(even), odd).astype(BF16))
    return jnp.concatenate(top, axis=1), jnp.concatenate(bottom, axis=1)


def level_of(part):
    return part[:, 0:1] + part[:, 1:2] + part[:, 2:3]


def rows_kernel(part_ref, w_hbm, x_ref, place_ref, slots_ref, counts_ref, owner_ref, me_ref, *rest):
    send_hbm, att_ref, w_ref, rows_ref, sems = rest[-5:]
    load_w = pltpu.make_async_copy(w_hbm, w_ref, sems.at[0])
    load_w.start()
    heads = []
    for h in range(HEADS):
        a, b = part_ref[2 * h].astype(F32), part_ref[2 * h + 1].astype(F32)
        la, lb = level_of(a), level_of(b)
        most = jnp.maximum(la, lb)
        wa, wb = jnp.exp2(la - most), jnp.exp2(lb - most)
        heads.append((a * wa + b * wb) / (wa + wb))
    att = jnp.concatenate(
        [
            jnp.where(low_half(QMAX), swap(heads[2 * i]), heads[2 * i + 1]).astype(BF16)
            for i in range(HEADS // 2)
        ],
        axis=1,
    )
    att_ref[...] = att
    gap = jnp.zeros((TOK // 2 - CHUNK, D), BF16)
    placed = jnp.concatenate([att[:CHUNK], gap, att[CHUNK:], gap], axis=0)
    token_slot = jnp.where(slot_of_token(slots_ref[...]), 1.0, 0.0).astype(BF16)
    where = lax.dot_general(token_slot, place_ref[...], TN, preferred_element_type=F32).astype(BF16)
    chosen = jnp.dot(where, placed, preferred_element_type=F32).astype(BF16)
    x = lax.dot_general(token_slot, x_ref[...], TN, preferred_element_type=F32)
    load_w.wait()
    rows = (x + jnp.dot(chosen, w_ref[...], preferred_element_type=F32)).astype(BF16)
    me = me_ref[0]
    slot = lax.broadcasted_iota(jnp.int32, rows.shape, 0)
    rows_ref[...] = jnp.where(slot < counts_ref[me], rows, jnp.zeros_like(rows))
    put = pltpu.make_async_copy(rows_ref, send_hbm.at[owner_ref[me]], sems.at[1])
    put.start()
    put.wait()


def track_rows(parts, w_out, x, place, slots, counts, owner, me, after):
    return pl.pallas_call(
        rows_kernel,
        in_specs=[VMEM, HBM] + [VMEM] * 3 + [SMEM] * 3 + [HBM] * len(after),
        out_specs=[HBM, VMEM],
        scratch_shapes=[
            pltpu.VMEM((D, D), BF16),
            pltpu.VMEM((QMAX, D), BF16),
            pltpu.SemaphoreType.DMA((2,)),
        ],
        out_shape=[
            jax.ShapeDtypeStruct((FRAMES, QMAX, D), BF16),
            jax.ShapeDtypeStruct((QMAX, D), BF16),
        ],
        compiler_params=pltpu.CompilerParams(vmem_limit_bytes=52 << 20),
        cost_estimate=pl.CostEstimate(flops=2 << 30, bytes_accessed=4 << 20, transcendentals=0),
        name="track_rows",
    )(parts, w_out, x, place, slots, counts, owner, me, *after)


def finish_kernel(
    owner_ref, me_ref, att1_hbm, at2_hbm, place_hbm, w_hbm, x_hbm, rows_hbm, mixed_ref, corr_ref, *scratch
):
    att1_ref, at2_ref, place_ref, w_ref, x_ref, rows_ref, sems = scratch

    @pl.when(pl.program_id(0) == 0)
    def _():
        sources = (at2_hbm, att1_hbm, place_hbm, w_hbm, x_hbm, rows_hbm)
        targets = (at2_ref, att1_ref, place_ref, w_ref, x_ref, rows_ref)
        loads = [
            pltpu.make_async_copy(source, target, sems.at[n])
            for n, (source, target) in enumerate(zip(sources, targets, strict=True))
        ]
        for load in loads:
            load.start()
        loads[0].wait()
        pairs = [
            (at2_ref[2 * i].astype(F32), at2_ref[2 * i + 1].astype(F32)) for i in range(HEADS // 2)
        ]
        top, bottom = join_heads(pairs)
        loads[1].wait()
        loads[2].wait()
        placed = jnp.concatenate([att1_ref[:CHUNK], top, att1_ref[CHUNK:], bottom], axis=0)
        att = jnp.dot(place_ref[...], placed, preferred_element_type=F32).astype(BF16)
        loads[3].wait()
        loads[4].wait()
        mixed_ref[...] = (
            x_ref[...].astype(F32) + jnp.dot(att, w_ref[...], preferred_element_type=F32)
        ).astype(BF16)
        loads[5].wait()

    step = corr_ref.shape[1]
    first = pl.program_id(0) * step
    rows = rows_ref[pl.ds(first, step)].reshape(-1, D)
    corr = lax.dot_general(rows, mixed_ref[...], NT, preferred_element_type=F32)
    corr = (corr * (1.0 / D**0.5)).reshape(step, QMAX, TOK)
    for i in range(step):
        owned = owner_ref[first + i] == me_ref[0]
        corr_ref[0, i] = jnp.where(owned, corr[i], jnp.zeros_like(corr[i]))


def finish(att1, att2, x, w_out, place, owner, me, arrived):
    step = 16
    return pl.pallas_call(
        finish_kernel,
        grid=(FRAMES // step,),
        in_specs=[SMEM] * 2 + [HBM] * 6,
        out_specs=[
            pl.BlockSpec((TOK, D), lambda i: (0, 0)),
            pl.BlockSpec((1, step, QMAX, TOK), lambda i: (0, i, 0, 0)),
        ],
        out_shape=[
            jax.ShapeDtypeStruct((TOK, D), BF16),
            jax.ShapeDtypeStruct((1, FRAMES, QMAX, TOK), F32),
        ],
        scratch_shapes=[
            pltpu.VMEM(array.shape, array.dtype) for array in (att1, att2, place, w_out, x, arrived)
        ]
        + [pltpu.SemaphoreType.DMA((6,))],
        compiler_params=pltpu.CompilerParams(vmem_limit_bytes=58 << 20),
        name="finish",
    )(owner, me, att1, att2, place, w_out, x, arrived)


def per_device(features, norm_gain, w_qkv, w_out, counts, query_index, owner):
    groups = [[2 * i + side for i in range(GROUP)] for side in range(2)]
    swap_sides = [(d, d ^ 1) for d in range(FRAMES)]
    me = lax.axis_index("frame").astype(jnp.int32).reshape(1)
    packed, place = project(features, norm_gain, query_index, w_qkv)
    mine = lax.all_to_all(packed, "frame", 0, 0, tiled=True, axis_index_groups=groups)
    picks = lax.ppermute(mine[:, TOK : TOK + CHUNK], "frame", swap_sides)
    other = lax.ppermute(mine, "frame", swap_sides)
    state1, tick = attend_own(mine, 1, 2)
    parts, tick = attend_picks(mine, picks, me, [tick])
    parts_here = lax.all_to_all(
        parts.reshape(FRAMES, QMAX, LANES), "frame", 0, 0, tiled=True
    )
    state2, _ = attend_own(mine, 2, SPLIT, [tick])
    send, att1 = track_rows(
        parts_here, w_out, features, place, query_index, counts, owner, me, [state2]
    )
    arrived = lax.all_to_all(send, "frame", 0, 0, tiled=True)
    state3, _ = attend_own(mine, SPLIT, CHUNKS, [att1])
    rest = attend_other(mine, other, [state1, state2, state3])
    rest, arrived = lax.optimization_barrier((rest, arrived))
    att2 = lax.all_to_all(rest, "frame", 0, 0, tiled=True, axis_index_groups=groups)
    return tuple(finish(att1, att2, features, w_out, place, owner, me, arrived))


def solution(mesh):
    rows = P(("scene", "frame"), None)
    in_specs = (rows, P(), P(), P(), P("scene"), rows, P("scene"))
    out_specs = (rows, P(("scene", "frame"), None, None, None))
    return jax.shard_map(
        per_device, mesh=mesh, in_specs=in_specs, out_specs=out_specs, check_vma=False
    )
```
